32 devices in a mesh: seq: 8 (over y, x, core), kv: 4 (over z).
Axes of the slice: x: 2, y: 2, z: 4, core: 2. Of those that a mesh axis runs over, the one named last changes fastest.
Arguments:
- tokens: bfloat16 [2, 4096, 1024], P(None, ('seq', 'kv')), may hold values from -6 to 6
- cotangent: bfloat16 [2, 4096, 1024], P(None, ('seq', 'kv'))
- norm_first: float32 [1024], replicated, may hold values from 0.1 to 1.9
- w_query: bfloat16 [1024, 1024], P(None, 'kv'), may hold values from -0.1875 to 0.1875
- w_key: bfloat16 [1024, 512], P(None, 'kv'), may hold values from -0.1875 to 0.1875
- w_value: bfloat16 [1024, 512], P(None, 'kv'), may hold values from -0.1875 to 0.1875
- w_out: bfloat16 [1024, 1024], P('kv'), may hold values from -3 to 3
- norm_second: float32 [1024], replicated, may hold values from 0.1 to 1.9
- w_gate: bfloat16 [4, 1024, 512], replicated, may hold values from -0.1875 to 0.1875
- w_up: bfloat16 [4, 1024, 512], replicated, may hold values from -0.1875 to 0.1875
- w_down: bfloat16 [4, 512, 1024], replicated, may hold values from -0.25 to 0.25
- routes: int32 [2, 4096, 2], P(None, ('seq', 'kv')), may hold values from 0 to 3, all different within a row; in each aligned block of 128 rows (0 to 127, 128 to 255, ..., all dimensions but the last counted through in order) at most 96 rows name the same one
- gate_weights: float32 [2, 4096, 2], P(None, ('seq', 'kv')), may hold values from 0.2 to 1
- segment_ids: int32 [2, 4096], replicated, may hold values from 0 to 3, as said below
- positions: int32 [2, 4096], P(None, 'seq'), may hold values from 0 to 3071, as said below
Outputs:
- block_out: bfloat16 [2, 4096, 1024], P(None, ('seq', 'kv'))
- d_tokens: bfloat16 [2, 4096, 1024], P(None, ('seq', 'kv'))
- grad_norm_first: float32 [1024], replicated
- grad_w_query: float32 [1024, 1024], P(None, 'kv')
- grad_w_key: float32 [1024, 512], P(None, 'kv')
- grad_w_value: float32 [1024, 512], P(None, 'kv')
- grad_w_out: float32 [1024, 1024], P('kv')
- grad_norm_second: float32 [1024], replicated
- grad_w_gate: float32 [4, 1024, 512], replicated
- grad_w_up: float32 [4, 1024, 512], replicated
- grad_w_down: float32 [4, 512, 1024], replicated
- expert_load: int32 [4], replicated
The draws below stay inside these ranges and needn't reach their ends.
Inputs may be any that keep to these rules, and one draw needn't show every extreme that they name: `routes`: the 2 experts of a token differ. Within one row, the 128 positions that start at a multiple of 128 name each expert at most 96 times, and some such block names one expert exactly 96 times. `segment_ids`: in each row the ids start at 0, never fall and rise by one where a new document starts; each of the 4 documents has 1 to 3072 positions, and one document of each row has exactly 3072. `positions`: each position's offset from the first position of its document.
All inputs are finite; a program needn't handle non-finite values.
Results may differ from the reference program's by a relative error of at most 0.02.
Values may be sent and summed in bfloat16 or wider, within the bound.
No kernel may reach another device: no remote copies, remote signals or barrier semaphores. Data moves between devices by JAX's collectives and lax.ppermute only.
A program may use at most 192 MiB of HBM per device.

```python
import math
import jax
import jax.numpy as jnp
import numpy as np
from jax import lax

D = 1024
HQ = 16
HK = 8
DH = 64
F = 512
E = 4
TOP = 2
ROWS = 2
LENGTH = 4096
BLK = 128
CAP = 96
DOCS = 4
MOST = 3072


def doc_layout(key):

    def one_row(row_key):
        cut_key, slot_key = jax.random.split(row_key)
        rest_len = LENGTH - MOST
        picks = jax.random.permutation(cut_key, rest_len - 1)[:DOCS - 2].astype(jnp.int32) + 1
        cuts = jnp.sort(picks)
        bounds = jnp.concatenate([jnp.zeros((1,), jnp.int32), cuts, jnp.full((1,), rest_len, jnp.int32)])
        short_len = bounds[1:] - bounds[:-1]
        long_slot = jax.random.randint(slot_key, (), 0, DOCS)
        doc_index = jnp.arange(DOCS, dtype=jnp.int32)
        lower_pick = jnp.clip(doc_index, 0, DOCS - 2)
        upper_pick = jnp.clip(doc_index - 1, 0, DOCS - 2)
        doc_sizes = jnp.where(doc_index < long_slot, short_len[lower_pick], jnp.where(doc_index == long_slot, MOST, short_len[upper_pick]))
        doc_ends = jnp.cumsum(doc_sizes)
        doc_starts = doc_ends - doc_sizes
        place = jnp.arange(LENGTH, dtype=jnp.int32)
        seg_row = jnp.sum((place[:, None] >= doc_ends[None, :]).astype(jnp.int32), axis=1)
        offsets = place - jnp.sum(jnp.where(seg_row[:, None] == doc_index[None, :], doc_starts[None, :], 0), axis=1)
        return (seg_row.astype(jnp.int32), offsets.astype(jnp.int32))
    row_keys = jax.random.split(jax.random.fold_in(key, 7), ROWS)
    return jax.vmap(one_row)(row_keys)


def draw_segment_ids(key, part):
    return doc_layout(key)[0]


def draw_positions(key, part):
    return doc_layout(key)[1]


def draw_cotangent(key, part):
    place = jnp.arange(LENGTH, dtype=jnp.float32) / LENGTH
    base_vals = jax.random.normal(key, (ROWS, LENGTH, D), jnp.float32)
    ramp = 0.6 + 1.2 * place
    return (base_vals * ramp[None, :, None]).astype(jnp.bfloat16)


def shard_levels(key, dims, cuts, low, top_value):
    def one(axis_at, blocks):
        heights = jax.random.uniform(jax.random.fold_in(jax.random.fold_in(key, 6), axis_at), (blocks,), jnp.float32, low / len(cuts), top_value / len(cuts))
        return jnp.repeat(jnp.exp(heights), dims[axis_at] // blocks).reshape((-1,) + (1,) * (len(dims) - axis_at - 1))

    level = one(*cuts[0])
    for cut in cuts[1:]:
        level = level * one(*cut)
    return level


def assign_block(rng, own, number, rows, amount, top, most, slope):
    order = jax.random.permutation(rng, amount)
    heavy_load, common = portions_of(amount, rows * top, most, slope, True), portions_of(amount, rows * top, most, slope, False)
    places = jnp.arange(amount)

    def named(tallies, turn):
        used = int((tallies > 0).sum())
        fixed = max(1, used // 4)
        moved = fixed + (places - fixed + turn * (used - fixed)) % max(1, amount - fixed)
        return jnp.zeros((amount,), jnp.int32).at[order[jnp.where(places < fixed, places, moved)]].set(jnp.asarray(tallies, jnp.int32))

    tallies = jnp.where(number % 4 == 0, named(heavy_load, number // 4), named(common, number - number // 4 - 1))
    mixed = jax.random.permutation(jax.random.fold_in(own, 3), amount)
    donor, taker = mixed[0:amount // 2 * 2:2], mixed[1:amount // 2 * 2:2]
    margin = jnp.minimum(tallies[donor] - 1, most - tallies[taker]) // 2
    margin = jnp.where((donor == order[0]) | (taker == order[0]) | (tallies[taker] == 0), 0, jnp.maximum(margin, 0))
    moved = jax.random.randint(jax.random.fold_in(own, 4), (amount // 2,), 0, 1 << 20) % (margin + 1)
    tallies = tallies.at[donor].add(-moved).at[taker].add(moved)
    labels = jnp.searchsorted(jnp.cumsum(tallies), jnp.arange(rows * top), side="right").astype(jnp.int32)
    grid = labels.reshape(top, rows).T
    grid = grid[jax.random.permutation(jax.random.fold_in(own, 1), rows)]
    turn = jax.random.randint(jax.random.fold_in(own, 2), (rows, 1), 0, top)
    return jnp.take_along_axis(grid, (jnp.arange(top)[None, :] + turn) % top, axis=1)


def portions_of(count, total, bound, skew, full):
    loads = [(1 << 20) // math.isqrt(standing ** skew) + 1 for standing in range(1, count + 1)]
    largest = bound if full else min(bound, max(-(-total // count), total * loads[0] // sum(loads)))
    least = 1 if total - largest >= count - 1 else 0
    holding, spare = [largest] + [least] * (count - 1), total - largest - least * (count - 1)
    while spare > 0:
        candidates = [i for i in range(1, count) if holding[i] < largest] or [i for i in range(1, count) if holding[i] < bound]
        pool, remaining = sum([loads[i] for i in candidates]), spare
        for i in candidates:
            more = min(bound - holding[i], max(1, remaining * loads[i] // pool), spare)
            holding[i] = holding[i] + more
            spare = spare - more
    return np.array(holding)


def centred(key, extent, width, limit, shards=(), kind=jnp.bfloat16):
    drawn = jax.random.normal(key, extent, jnp.float32) * width
    if len(shards) > 0:
        drawn = shard_levels(key, extent, shards, -0.22, 0.18) * drawn
    return jnp.clip(drawn, min=-limit, max=limit).astype(kind)


def setup_inputs(seed: int = 0) -> dict:
    seeds = jax.random.split(jax.random.key(seed), 16)
    tokens = centred(seeds[0], (ROWS, LENGTH, D), 1.0, 6.0, ((1, 32),))
    cotangent = draw_cotangent(jax.random.fold_in(seeds[15], 71), 0)
    norm_first = jnp.clip(1.0 + 0.18 * jax.random.normal(seeds[2], (D,), jnp.float32), 0.1, 1.9)
    w_query = centred(seeds[3], (D, HQ * DH), D ** -0.5, 0.1875, ((1, 4),))
    w_key = centred(seeds[4], (D, HK * DH), D ** -0.5, 0.1875, ((1, 4),))
    w_value = centred(seeds[5], (D, HK * DH), D ** -0.5, 0.1875, ((1, 4),))
    w_out = centred(seeds[6], (HQ * DH, D), (max(1, HQ * DH // 256)) ** -0.5, 3.0, ((0, 4),))
    norm_second = jnp.clip(1.0 + 0.18 * jax.random.normal(seeds[7], (D,), jnp.float32), 0.1, 1.9)
    w_gate = centred(seeds[8], (E, D, F), D ** -0.5, 0.1875)
    w_up = centred(seeds[9], (E, D, F), D ** -0.5, 0.1875)
    w_down = centred(seeds[10], (E, F, D), F ** -0.5, 0.25)
    routes_keys = jax.random.split(jax.random.fold_in(seeds[11], 1), ROWS * LENGTH // BLK)
    routes_turns = jax.random.permutation(jax.random.fold_in(seeds[11], 3), ROWS * LENGTH // BLK)
    routes = jax.vmap(lambda own, number: assign_block(jax.random.fold_in(seeds[11], 2), own, number, BLK, E, TOP, CAP, 2))(routes_keys, routes_turns).reshape((ROWS, LENGTH, TOP))
    gate_weights = jnp.clip(0.2 + 0.8 * jax.random.uniform(seeds[12], (ROWS, LENGTH, TOP), jnp.float32) ** shard_levels(seeds[12], (ROWS, LENGTH, TOP), ((1, 32),), -0.2, 0.2), 0.2, 1.0)
    segment_ids = draw_segment_ids(jax.random.fold_in(seeds[15], 71), 0)
    positions = draw_positions(jax.random.fold_in(seeds[15], 71), 0)
    return {"tokens": tokens, "cotangent": cotangent, "norm_first": norm_first, "w_query": w_query, "w_key": w_key, "w_value": w_value, "w_out": w_out, "norm_second": norm_second, "w_gate": w_gate, "w_up": w_up, "w_down": w_down, "routes": routes, "gate_weights": gate_weights, "segment_ids": segment_ids, "positions": positions}


epsilon = 1e-05
neg_big = -1e+30
theta_base = 10000.0
highest = lax.Precision.HIGHEST

@jax.custom_vjp
def low(v):
    return lax.optimization_barrier(v.astype(jnp.bfloat16)).astype(jnp.float32)

@jax.custom_vjp
def low_back(v):
    return v

def low_keep(v):
    return (low(v), None)

def low_pass(kept, grad):
    return (grad,)

def back_keep(v):
    return (v, None)

def back_low(kept, grad):
    return (low(grad),)
low.defvjp(low_keep, low_pass)
low_back.defvjp(back_keep, back_low)

def rope_tables(positions, head_size):
    half_size = head_size // 2
    freqs = theta_base ** (-(jnp.arange(half_size, dtype=jnp.float32) * 2.0) / head_size)
    angles = positions.astype(jnp.float32)[..., None] * freqs
    return (jnp.cos(angles), jnp.sin(angles))

def rotate(values, cosine, sine):
    half_size = values.shape[-1] // 2
    first_half = values[..., :half_size]
    second_half = values[..., half_size:]
    cos_rows = cosine[:, :, None, :]
    sin_rows = sine[:, :, None, :]
    return jnp.concatenate([first_half * cos_rows - second_half * sin_rows, second_half * cos_rows + first_half * sin_rows], axis=-1)

def norm_rows(values, gain):
    recip = lax.rsqrt(lax.optimization_barrier(jnp.mean(values * values, axis=-1, keepdims=True)) + epsilon)
    return values * recip * gain

def attend_row(queries, keys, values, segs):
    length = queries.shape[0]
    group_size = queries.shape[1] // keys.shape[1]
    keys_all = jnp.repeat(keys, group_size, axis=1)
    values_all = jnp.repeat(values, group_size, axis=1)
    block_len = math.gcd(length, 512)
    block_count = length // block_len
    key_place = jnp.arange(length, dtype=jnp.int32)
    factor = DH ** (-0.5)

    @jax.checkpoint
    def one_block(block_index):
        start = (block_index * block_len).astype(jnp.int32)
        query_block = lax.dynamic_slice_in_dim(queries, start, block_len, 0)
        query_segs = lax.dynamic_slice_in_dim(segs, start, block_len, 0)
        query_place = start + jnp.arange(block_len, dtype=jnp.int32)
        scores = low_back(jnp.einsum('qhd,khd->hqk', query_block, keys_all, precision=highest) * factor)
        allowed = (key_place[None, :] <= query_place[:, None]) & (query_segs[:, None] == segs[None, :])
        masked = jnp.where(allowed[None], scores, neg_big)
        row_top = lax.optimization_barrier(jnp.max(masked, axis=-1, keepdims=True))
        weights = jnp.where(allowed[None], jnp.exp(masked - row_top), 0.0)
        totals = lax.optimization_barrier(jnp.sum(weights, axis=-1))
        mixed = jnp.einsum('hqk,khd->qhd', low(weights), values_all, precision=highest)
        return mixed / jnp.transpose(totals)[:, :, None]
    outputs = lax.map(one_block, jnp.arange(block_count, dtype=jnp.int32))
    return outputs.reshape(length, queries.shape[1], queries.shape[2])

def forward_layer(tokens, norm_first, w_query, w_key, w_value, w_out, norm_second, w_gate, w_up, w_down, routes, gate_weights, segment_ids, positions):
    row_count = tokens.shape[0]
    length = tokens.shape[1]
    normed = low(norm_rows(tokens, norm_first))
    q_raw = low_back(jnp.einsum('rld,de->rle', normed, w_query, precision=highest))
    k_raw = low_back(jnp.einsum('rld,de->rle', normed, w_key, precision=highest))
    v_raw = jnp.einsum('rld,de->rle', normed, w_value, precision=highest)
    cosine, sine = rope_tables(positions, DH)
    queries = low(rotate(q_raw.reshape(row_count, length, HQ, DH), cosine, sine))
    keys = low(rotate(k_raw.reshape(row_count, length, HK, DH), cosine, sine))
    values = low_back(low(v_raw)).reshape(row_count, length, HK, DH)
    heads = jnp.stack([attend_row(queries[row], keys[row], values[row], segment_ids[row]) for row in range(row_count)])
    heads_low = low_back(low(heads.reshape(row_count, length, HQ * DH)))
    hidden = tokens + low_back(jnp.einsum('rle,ed->rld', heads_low, w_out, precision=highest))
    h_norm = low(norm_rows(hidden, norm_second))
    picks = (routes[..., None] == jnp.arange(E, dtype=jnp.int32)).astype(jnp.float32)
    mix = lax.optimization_barrier(jnp.sum(picks * gate_weights[..., None], axis=2))
    total = hidden
    for expert in range(E):
        gate_pre = low_back(jnp.einsum('rld,df->rlf', h_norm, w_gate[expert], precision=highest))
        up_pre = low_back(jnp.einsum('rld,df->rlf', h_norm, w_up[expert], precision=highest))
        hid = low(jax.nn.silu(gate_pre) * up_pre)
        expert_out = low_back(jnp.einsum('rlf,fd->rld', hid, w_down[expert], precision=highest))
        total = total + mix[..., expert:expert + 1] * expert_out
    return total

def reference(tokens, cotangent, norm_first, w_query, w_key, w_value, w_out, norm_second, w_gate, w_up, w_down, routes, gate_weights, segment_ids, positions):
    floats = (tokens.astype(jnp.float32), norm_first.astype(jnp.float32), w_query.astype(jnp.float32), w_key.astype(jnp.float32), w_value.astype(jnp.float32), w_out.astype(jnp.float32), norm_second.astype(jnp.float32), w_gate.astype(jnp.float32), w_up.astype(jnp.float32), w_down.astype(jnp.float32))

    def primal(tok, gain_one, wq_f, wk_f, wv_f, wo_f, gain_two, wg_f, wu_f, wd_f):
        return forward_layer(tok, gain_one, wq_f, wk_f, wv_f, wo_f, gain_two, wg_f, wu_f, wd_f, routes, gate_weights.astype(jnp.float32), segment_ids, positions)
    result, pullback = jax.vjp(primal, *floats)
    grads = pullback(cotangent.astype(jnp.float32))
    load = lax.optimization_barrier(jnp.sum((routes[..., None] == jnp.arange(E, dtype=jnp.int32)).astype(jnp.int32), axis=(0, 1, 2)))
    return (result.astype(jnp.bfloat16), grads[0].astype(jnp.bfloat16), grads[1], grads[2], grads[3], grads[4], grads[5], grads[6], grads[7], grads[8], grads[9], load)
```

```python
import functools

import jax
import jax.numpy as jnp
from jax import lax
from jax.experimental import pallas as pl
from jax.experimental.pallas import tpu as pltpu
from jax.sharding import PartitionSpec as P

DH = 64
HALF = DH // 2

epsilon = 1e-05
neg_big = -1e30
theta_base = 10000.0
highest = lax.Precision.HIGHEST
f32 = jnp.float32
bf16 = jnp.bfloat16

NN = (((1,), (0,)), ((), ()))
NT = (((1,), (1,)), ((), ()))


def mm(a, b, dims=NN):
    return lax.dot_general(a, b, dims, preferred_element_type=f32)


def qkv_kernel(w_ref, n_ref, cos_ref, sin_ref, q_ref, kv_ref, *, query_heads, key_heads, scale):
    acc = mm(w_ref[...], n_ref[...], NT)
    cosine = cos_ref[...]
    sine = sin_ref[...]
    for head in range(query_heads):
        low = acc[DH * head : DH * head + HALF]
        high = acc[DH * head + HALF : DH * head + DH]
        q_ref[DH * head : DH * head + HALF, :] = ((low * cosine - high * sine) * scale).astype(bf16)
        q_ref[DH * head + HALF : DH * head + DH, :] = (
            (high * cosine + low * sine) * scale
        ).astype(bf16)
    base = DH * query_heads
    for head in range(key_heads):
        low = acc[base + DH * head : base + DH * head + HALF]
        high = acc[base + DH * head + HALF : base + DH * head + DH]
        at = 2 * DH * head
        kv_ref[at : at + HALF, :] = (low * cosine - high * sine).astype(bf16)
        kv_ref[at + HALF : at + DH, :] = (high * cosine + low * sine).astype(bf16)
        start = base + DH * (key_heads + head)
        kv_ref[at + DH : at + 2 * DH, :] = acc[start : start + DH].astype(bf16)


def project(w_t, gathered, cosine, sine, query_heads, key_heads):
    cols, width = w_t.shape
    count = gathered.shape[0]
    tile = 256
    q_cols = query_heads * DH
    kv_cols = 2 * key_heads * DH
    return pl.pallas_call(
        functools.partial(
            qkv_kernel, query_heads=query_heads, key_heads=key_heads, scale=DH ** (-0.5)
        ),
        grid=(count // tile,),
        in_specs=[
            pl.BlockSpec((cols, width), lambda i: (0, 0)),
            pl.BlockSpec((tile, width), lambda i: (i, 0)),
            pl.BlockSpec((HALF, tile), lambda i: (0, i)),
            pl.BlockSpec((HALF, tile), lambda i: (0, i)),
        ],
        out_specs=[
            pl.BlockSpec((q_cols, tile), lambda i: (0, i)),
            pl.BlockSpec((kv_cols, tile), lambda i: (0, i)),
        ],
        out_shape=[
            jax.ShapeDtypeStruct((q_cols, count), bf16),
            jax.ShapeDtypeStruct((kv_cols, count), bf16),
        ],
        compiler_params=pltpu.CompilerParams(vmem_limit_bytes=32 * 2**20),
        cost_estimate=pl.CostEstimate(
            flops=2 * cols * width * count, bytes_accessed=4 * count * width, transcendentals=0
        ),
    )(w_t, gathered, cosine, sine)


def forward_kernel(
    meta_ref, q_ref, kv_ref, start_ref, o_ref, low_ref, lse_ref, max_s, sum_s, acc_s,
    *, group, row_count
):
    row = pl.program_id(0)
    span = q_ref.shape[1]
    here = meta_ref[0]
    first = meta_ref[1 + row]
    middle = meta_ref[1 + row_count + row]
    start = start_ref[0]
    key_iota = lax.broadcasted_iota(jnp.int32, (span, span), 0)

    def step(block, masked, diagonal):
        k_t = kv_ref[block, 0:DH, :]
        v_t = kv_ref[block, DH : 2 * DH, :]
        keys = k_t.T
        if masked:
            keep = key_iota + block * span >= start
        if diagonal:
            keep = keep & (key_iota <= lax.broadcasted_iota(jnp.int32, (span, span), 1))
        for g in range(group):
            scores = mm(keys, q_ref[DH * g : DH * g + DH, :])
            if masked:
                scores = jnp.where(keep, scores, neg_big)
            top = jnp.max(scores, axis=0, keepdims=True)
            if diagonal:
                new_max = top
            else:
                old_max = max_s[g : g + 1, :]
                new_max = jnp.maximum(old_max, top)
            weights = jnp.exp(scores - new_max)
            total = jnp.sum(weights, axis=0, keepdims=True)
            mixed = mm(v_t, weights.astype(bf16))
            at = slice(DH * g, DH * g + DH)
            if diagonal:
                sum_s[g : g + 1, :] = total
                acc_s[at, :] = mixed
            else:
                factor = jnp.exp(old_max - new_max)
                sum_s[g : g + 1, :] = sum_s[g : g + 1, :] * factor + total
                acc_s[at, :] = acc_s[at, :] * factor + mixed
            max_s[g : g + 1, :] = new_max

    step(here, True, True)

    @pl.loop(first, middle)
    def _(block):
        step(block, True, False)

    @pl.loop(middle, here)
    def _(block):
        step(block, False, False)

    for g in range(group):
        at = slice(DH * g, DH * g + DH)
        total = sum_s[g : g + 1, :]
        out = acc_s[at, :] / total
        o_ref[at, :] = out
        low_ref[at, :] = out.astype(bf16)
        lse_ref[0, 0, g : g + 1, :] = max_s[g : g + 1, :] + jnp.log(total)


def attend(meta, q_t, kv_all, starts, group):
    row_count, _, span = starts.shape
    blocks = kv_all.shape[0]
    key_heads = kv_all.shape[1] // (2 * DH)
    cols = group * DH
    count = q_t.shape[1]
    return pl.pallas_call(
        functools.partial(forward_kernel, group=group, row_count=row_count),
        grid_spec=pltpu.PrefetchScalarGridSpec(
            num_scalar_prefetch=1,
            grid=(row_count, key_heads),
            in_specs=[
                pl.BlockSpec((cols, span), lambda r, h, m: (h, r)),
                pl.BlockSpec((blocks, 2 * DH, span), lambda r, h, m: (0, h, r)),
                pl.BlockSpec((1, 1, span), lambda r, h, m: (r, 0, 0)),
            ],
            out_specs=[
                pl.BlockSpec((cols, span), lambda r, h, m: (h, r)),
                pl.BlockSpec((cols, span), lambda r, h, m: (h, r)),
                pl.BlockSpec((1, 1, group, span), lambda r, h, m: (h, r, 0, 0)),
            ],
            scratch_shapes=[
                pltpu.VMEM((group, span), f32),
                pltpu.VMEM((group, span), f32),
                pltpu.VMEM((cols, span), f32),
            ],
        ),
        out_shape=[
            jax.ShapeDtypeStruct((key_heads * cols, count), f32),
            jax.ShapeDtypeStruct((key_heads * cols, count), bf16),
            jax.ShapeDtypeStruct((key_heads, row_count, group, span), f32),
        ],
        compiler_params=pltpu.CompilerParams(vmem_limit_bytes=48 * 2**20),
        cost_estimate=pl.CostEstimate(
            flops=16 * count * blocks * span * cols,
            bytes_accessed=4 * kv_all.size,
            transcendentals=0,
        ),
    )(meta, q_t, kv_all, starts)


def backward_kernel(
    meta_ref, q_ref, do_ref, o_ref, lse_ref, kv_ref, start_ref, cos_ref, sin_ref,
    dq_ref, dkv_ref, dq_s, q_s, do_s, delta_s,
    *, group, row_count, scale
):
    row = pl.program_id(0)
    span = q_ref.shape[1]
    here = meta_ref[0]
    first = meta_ref[1 + row]
    middle = meta_ref[1 + row_count + row]
    start = start_ref[0]
    key_iota = lax.broadcasted_iota(jnp.int32, (span, span), 0)
    dkv_ref[...] = jnp.zeros(dkv_ref.shape, bf16)
    for g in range(group):
        at = slice(DH * g, DH * g + DH)
        q_s[g] = q_ref[at, :].T
        do_s[g] = do_ref[at, :].T
        delta_s[g : g + 1, :] = jnp.sum(
            do_ref[at, :].astype(f32) * o_ref[at, :], axis=0, keepdims=True
        )

    def step(block, masked, diagonal):
        k_t = kv_ref[block, 0:DH, :]
        v_t = kv_ref[block, DH : 2 * DH, :]
        keys = k_t.T
        values = v_t.T
        if masked:
            keep = key_iota + block * span >= start
        if diagonal:
            keep = keep & (key_iota <= lax.broadcasted_iota(jnp.int32, (span, span), 1))
        d_keys = None
        d_values = None
        for g in range(group):
            at = slice(DH * g, DH * g + DH)
            scores = mm(keys, q_ref[at, :])
            probs = jnp.exp(scores - lse_ref[0, 0, g : g + 1, :])
            if masked:
                probs = jnp.where(keep, probs, 0.0)
            d_probs = mm(values, do_ref[at, :])
            d_scores = (probs * (d_probs - delta_s[g : g + 1, :])).astype(bf16)
            dq = mm(k_t, d_scores)
            if diagonal:
                dq_s[at, :] = dq
            else:
                dq_s[at, :] += dq
            dv = mm(probs.astype(bf16), do_s[g])
            dk = mm(d_scores, q_s[g])
            d_keys = dk if d_keys is None else d_keys + dk
            d_values = dv if d_values is None else d_values + dv
        dkv_ref[block, 0:DH, :] = d_keys.T.astype(bf16)
        dkv_ref[block, DH : 2 * DH, :] = d_values.T.astype(bf16)

    step(here, True, True)

    @pl.loop(first, middle)
    def _(block):
        step(block, True, False)

    @pl.loop(middle, here)
    def _(block):
        step(block, False, False)

    cosine = cos_ref[...]
    sine = sin_ref[...]
    for g in range(group):
        low = dq_s[DH * g : DH * g + HALF, :] * scale
        high = dq_s[DH * g + HALF : DH * g + DH, :] * scale
        dq_ref[DH * g : DH * g + HALF, :] = (low * cosine + high * sine).astype(bf16)
        dq_ref[DH * g + HALF : DH * g + DH, :] = (high * cosine - low * sine).astype(bf16)


def attend_back(meta, q_t, do_t, o_t, lse, kv_all, starts, cosine, sine, group):
    row_count, _, span = starts.shape
    blocks = kv_all.shape[0]
    key_heads = kv_all.shape[1] // (2 * DH)
    cols = group * DH
    count = q_t.shape[1]
    head_spec = pl.BlockSpec((cols, span), lambda r, h, m: (h, r))
    kv_spec = pl.BlockSpec((blocks, 2 * DH, span), lambda r, h, m: (0, h, r))
    angle_spec = pl.BlockSpec((HALF, span), lambda r, h, m: (0, r))
    return pl.pallas_call(
        functools.partial(
            backward_kernel, group=group, row_count=row_count, scale=DH ** (-0.5)
        ),
        grid_spec=pltpu.PrefetchScalarGridSpec(
            num_scalar_prefetch=1,
            grid=(row_count, key_heads),
            in_specs=[
                head_spec,
                head_spec,
                head_spec,
                pl.BlockSpec((1, 1, group, span), lambda r, h, m: (h, r, 0, 0)),
                kv_spec,
                pl.BlockSpec((1, 1, span), lambda r, h, m: (r, 0, 0)),
                angle_spec,
                angle_spec,
            ],
            out_specs=[head_spec, kv_spec],
            scratch_shapes=[
                pltpu.VMEM((cols, span), f32),
                pltpu.VMEM((group, span, DH), bf16),
                pltpu.VMEM((group, span, DH), bf16),
                pltpu.VMEM((group, span), f32),
            ],
        ),
        out_shape=[
            jax.ShapeDtypeStruct((key_heads * cols, count), bf16),
            jax.ShapeDtypeStruct(kv_all.shape, bf16),
        ],
        compiler_params=pltpu.CompilerParams(vmem_limit_bytes=48 * 2**20),
        cost_estimate=pl.CostEstimate(
            flops=40 * count * blocks * span * cols,
            bytes_accessed=4 * kv_all.size,
            transcendentals=0,
        ),
    )(meta, q_t, do_t, o_t, lse, kv_all, starts, cosine, sine)


def per_device(
    tokens,
    cotangent,
    norm_first,
    w_query,
    w_key,
    w_value,
    w_out,
    norm_second,
    w_gate,
    w_up,
    w_down,
    routes,
    gate_weights,
    segment_ids,
    positions,
):
    row_count, block_len, width = tokens.shape
    kv_devices = lax.axis_size("kv")
    seq_devices = lax.axis_size("seq")
    seq_len = block_len * kv_devices
    seq_index = lax.axis_index("seq")
    query_cols = w_query.shape[1]
    key_cols = w_key.shape[1]
    inner_cols = query_cols + 2 * key_cols
    query_heads = query_cols // DH
    key_heads = key_cols // DH
    group = query_heads // key_heads
    expert_count = w_gate.shape[0]
    top_count = routes.shape[2]
    own = row_count * block_len
    count = row_count * seq_len

    place = seq_index * seq_len + jnp.arange(seq_len, dtype=jnp.int32)
    starts = place[None, :] - positions
    first_block = starts[:, 0] // seq_len
    middle_block = jnp.clip((starts[:, -1] + seq_len - 1) // seq_len, first_block, seq_index)
    meta = jnp.concatenate([seq_index[None], first_block, middle_block]).astype(jnp.int32)
    freqs = theta_base ** (-(jnp.arange(HALF, dtype=f32) * 2.0) / DH)
    angles = freqs[:, None] * positions.astype(f32).reshape(1, count)
    cosine = jnp.cos(angles)
    sine = jnp.sin(angles)

    w_t = jnp.concatenate([w_query.T, w_key.T, w_value.T], axis=0)
    all_rows = jnp.concatenate([w_t, w_out], axis=0)
    share = all_rows.shape[0] // seq_devices
    expert_ids = jnp.arange(expert_count, dtype=jnp.int32)
    picks = routes[..., None] == expert_ids
    local_load = jnp.sum(picks.astype(f32), axis=(0, 1, 2))
    load_rows = jnp.pad(local_load.astype(bf16)[None, :], ((0, 15), (0, width - expert_count)))
    payload = jnp.concatenate(
        [lax.dynamic_slice_in_dim(all_rows, seq_index * share, share, 0), load_rows], axis=0
    )

    x_float = tokens.astype(f32)
    recip_first = lax.rsqrt(jnp.mean(x_float * x_float, axis=-1, keepdims=True) + epsilon)
    x_hat = x_float * recip_first
    normed = (x_hat * norm_first).astype(bf16)
    gathered = lax.all_gather(normed, "kv", axis=1, tiled=True).reshape(count, width)
    q_t, kv_t = project(w_t, gathered, cosine, sine, query_heads, key_heads)
    kv_all = lax.all_gather(kv_t, "seq")

    spread = lax.all_gather(payload, ("seq", "kv")).reshape(
        seq_devices, kv_devices, share + 16, width
    )
    load_sum = jnp.sum(spread[:, :, share, :expert_count].astype(f32), axis=(0, 1))
    w_all = spread[:, :, :share].transpose(1, 0, 2, 3).reshape(kv_devices, seq_devices * share, width)
    w_inner_all = w_all[:, :inner_cols]
    w_out_all = w_all[:, inner_cols:].reshape(kv_devices * query_cols, width)

    starts3 = starts.reshape(row_count, 1, seq_len)
    o_t, heads_t, lse = attend(meta, q_t, kv_all, starts3, group)

    def exchange(value):
        return lax.all_to_all(value, "kv", 0, 0)

    def split_own(value):
        cols = value.shape[0]
        return (
            value.reshape(cols, row_count, kv_devices, block_len)
            .transpose(2, 0, 1, 3)
            .reshape(kv_devices, cols, own)
        )

    heads_own = exchange(split_own(heads_t)).reshape(kv_devices * query_cols, own)
    branch = lax.dot_general(
        heads_own, w_out_all, (((0,), (0,)), ((), ())), preferred_element_type=f32
    )
    hidden_state = x_float + branch.reshape(row_count, block_len, width)
    recip_second = lax.rsqrt(
        jnp.mean(hidden_state * hidden_state, axis=-1, keepdims=True) + epsilon
    )
    h_hat = hidden_state * recip_second
    h_norm = (h_hat * norm_second).astype(bf16)

    mix = jnp.sum(picks.astype(f32) * gate_weights[..., None], axis=2).reshape(own, expert_count)
    h_rows = h_norm.reshape(own, width)
    gate_pre = jnp.einsum("td,edf->etf", h_rows, w_gate, preferred_element_type=f32)
    up_pre = jnp.einsum("td,edf->etf", h_rows, w_up, preferred_element_type=f32)
    gate_sig = jax.nn.sigmoid(gate_pre)
    gate_act = gate_pre * gate_sig
    hid_low = (gate_act * up_pre).astype(bf16)
    expert_out = jnp.einsum("etf,efd->etd", hid_low, w_down, preferred_element_type=f32)
    mix_e = mix.T[:, :, None]
    branch_moe = jnp.sum(mix_e * expert_out, axis=0)
    block_out = (hidden_state + branch_moe.reshape(row_count, block_len, width)).astype(bf16)
    d_top = cotangent.astype(f32)
    d_expert = (mix_e * d_top.reshape(1, own, width)).astype(bf16)
    d_hid = jnp.einsum("etd,efd->etf", d_expert, w_down, preferred_element_type=f32)
    d_gate = (d_hid * up_pre * gate_sig * (1.0 + gate_pre * (1.0 - gate_sig))).astype(bf16)
    d_up = (d_hid * gate_act).astype(bf16)
    grad_down = jnp.einsum("etf,etd->efd", hid_low, d_expert, preferred_element_type=f32)
    grad_gate = jnp.einsum("td,etf->edf", h_rows, d_gate, preferred_element_type=f32)
    grad_up = jnp.einsum("td,etf->edf", h_rows, d_up, preferred_element_type=f32)
    d_hnorm = (
        jnp.einsum("etf,edf->td", d_gate, w_gate, preferred_element_type=f32)
        + jnp.einsum("etf,edf->td", d_up, w_up, preferred_element_type=f32)
    ).reshape(row_count, block_len, width)
    d_hat_two = d_hnorm * norm_second
    d_hidden = d_top + recip_second * (
        d_hat_two - h_hat * jnp.mean(d_hat_two * h_hat, axis=-1, keepdims=True)
    )
    d_branch = d_hidden.astype(bf16)

    grad_gate_low, grad_up_low, grad_down_low = lax.psum(
        (grad_gate.astype(bf16), grad_up.astype(bf16), grad_down.astype(bf16)), ("seq", "kv")
    )

    d_heads = mm(w_out_all, d_branch.reshape(own, width), NT).astype(bf16)
    d_heads = exchange(d_heads.reshape(kv_devices, query_cols, own))
    do_t = (
        d_heads.reshape(kv_devices, query_cols, row_count, block_len)
        .transpose(1, 2, 0, 3)
        .reshape(query_cols, count)
    )
    d_rows = lax.all_gather(d_branch, "kv", axis=1, tiled=True).reshape(count, width)
    grad_out_part = mm(heads_t, d_rows)
    grad_out_all = lax.psum(grad_out_part.astype(bf16), "seq").astype(f32)

    dq_t, dkv_part = attend_back(
        meta, q_t, do_t, o_t, lse, kv_all, starts3, cosine, sine, group
    )
    dkv = lax.psum_scatter(dkv_part, "seq").astype(f32)
    dkv = dkv.reshape(key_heads, 2, DH, count)
    low, high = dkv[:, 0, :HALF], dkv[:, 0, HALF:]
    dk_t = jnp.concatenate([low * cosine + high * sine, high * cosine - low * sine], axis=1)
    d_inner_t = jnp.concatenate(
        [
            dq_t,
            dk_t.astype(bf16).reshape(key_cols, count),
            dkv[:, 1].astype(bf16).reshape(key_cols, count),
        ],
        axis=0,
    )
    grad_inner_part = lax.dot_general(
        gathered, d_inner_t, (((0,), (1,)), ((), ())), preferred_element_type=f32
    )
    grad_inner = lax.psum(grad_inner_part.astype(bf16), "seq").astype(f32)
    d_inner_own = exchange(split_own(d_inner_t)).reshape(kv_devices * inner_cols, own)
    d_normed = lax.dot_general(
        d_inner_own,
        w_inner_all.reshape(kv_devices * inner_cols, width),
        (((0,), (0,)), ((), ())),
        preferred_element_type=f32,
    ).reshape(row_count, block_len, width)
    d_hat_one = d_normed * norm_first
    d_tokens = (
        d_hidden
        + recip_first * (d_hat_one - x_hat * jnp.mean(d_hat_one * x_hat, axis=-1, keepdims=True))
    ).astype(bf16)

    first_part = jnp.sum(w_t.T.astype(f32) * grad_inner, axis=1)
    first_sum = lax.psum(first_part, "kv") / norm_first
    grad_gate_all = grad_gate_low.astype(f32)
    grad_up_all = grad_up_low.astype(f32)
    grad_down_all = grad_down_low.astype(f32)
    second_sum = (
        jnp.sum(w_gate.astype(f32) * grad_gate_all + w_up.astype(f32) * grad_up_all, axis=(0, 2))
        / norm_second
    )
    return (
        block_out,
        d_tokens,
        first_sum,
        grad_inner[:, :query_cols],
        grad_inner[:, query_cols : query_cols + key_cols],
        grad_inner[:, query_cols + key_cols :],
        grad_out_all,
        second_sum,
        grad_gate_all,
        grad_up_all,
        grad_down_all,
        load_sum.astype(jnp.int32),
    )


def solution(mesh):
    in_specs = (
        P(None, ("seq", "kv"), None),
        P(None, ("seq", "kv"), None),
        P(),
        P(None, "kv"),
        P(None, "kv"),
        P(None, "kv"),
        P("kv", None),
        P(),
        P(),
        P(),
        P(),
        P(None, ("seq", "kv"), None),
        P(None, ("seq", "kv"), None),
        P(),
        P(None, "seq"),
    )
    out_specs = (
        P(None, ("seq", "kv"), None),
        P(None, ("seq", "kv"), None),
        P(),
        P(None, "kv"),
        P(None, "kv"),
        P(None, "kv"),
        P("kv", None),
        P(),
        P(),
        P(),
        P(),
        P(),
    )
    return jax.shard_map(
        per_device, mesh=mesh, in_specs=in_specs, out_specs=out_specs, check_vma=False
    )
```

```python
import functools

import jax
import jax.numpy as jnp
from jax import lax
from jax.experimental import pallas as pl
from jax.experimental.pallas import tpu as pltpu
from jax.sharding import PartitionSpec as P

DH = 64
HALF = DH // 2

epsilon = 1e-05
neg_big = -1e30
theta_base = 10000.0
highest = lax.Precision.HIGHEST
f32 = jnp.float32
bf16 = jnp.bfloat16

NN = (((1,), (0,)), ((), ()))
NT = (((1,), (1,)), ((), ()))


def mm(a, b, dims=NN):
    return lax.dot_general(a, b, dims, preferred_element_type=f32)


def seq_bits(axis_size):
    bits = []
    bit = 2
    while bit < axis_size:
        bits.append(bit)
        bit *= 2
    return bits


def seq_order(row, axis_size):
    bits = seq_bits(axis_size)
    return (bits if row % 2 == 0 else bits[::-1]) + [1]


def slot_of(mask, order):
    slot = 0
    for at, bit in enumerate(order):
        slot = slot + (((mask >> (bit.bit_length() - 1)) & 1) << at)
    return slot


def swap(value, axis, mask):
    count = lax.axis_size(axis)
    return lax.ppermute(value, axis, [(source, source ^ mask) for source in range(count)])


def spread_seq(value, order):
    held = value[None]
    for bit in order:
        held = jnp.concatenate([held, swap(held, "seq", bit)], axis=0)
    return held


def collect_seq(value, order):
    held = value
    for bit in order[::-1]:
        half = held.shape[0] // 2
        came = swap(held[half:], "seq", bit)
        held = (held[:half].astype(f32) + came.astype(f32)).astype(bf16)
    return held[0]


def sum_seq(value, order):
    index = lax.axis_index("seq")
    held = value
    for bit in order[::-1]:
        half = held.shape[0] // 2
        upper = (index & bit) != 0
        keep = jnp.where(upper, held[half:], held[:half])
        send = jnp.where(upper, held[:half], held[half:])
        held = (keep.astype(f32) + swap(send, "seq", bit).astype(f32)).astype(bf16)
    for bit in order:
        upper = (index & bit) != 0
        came = swap(held, "seq", bit)
        held = jnp.where(
            upper,
            jnp.concatenate([came, held], axis=0),
            jnp.concatenate([held, came], axis=0),
        )
    return held


def qkv_kernel(w_ref, n_ref, cos_ref, sin_ref, q_ref, kv_ref, *, query_heads, key_heads, scale):
    acc = mm(w_ref[...], n_ref[0], NT)
    cosine = cos_ref[0]
    sine = sin_ref[0]
    for head in range(query_heads):
        low = acc[DH * head : DH * head + HALF]
        high = acc[DH * head + HALF : DH * head + DH]
        q_ref[DH * head : DH * head + HALF, :] = ((low * cosine - high * sine) * scale).astype(bf16)
        q_ref[DH * head + HALF : DH * head + DH, :] = (
            (high * cosine + low * sine) * scale
        ).astype(bf16)
    base = DH * query_heads
    for head in range(key_heads):
        low = acc[base + DH * head : base + DH * head + HALF]
        high = acc[base + DH * head + HALF : base + DH * head + DH]
        at = 2 * DH * head
        kv_ref[at : at + HALF, :] = (low * cosine - high * sine).astype(bf16)
        kv_ref[at + HALF : at + DH, :] = (high * cosine + low * sine).astype(bf16)
        start = base + DH * (key_heads + head)
        kv_ref[at + DH : at + 2 * DH, :] = acc[start : start + DH].astype(bf16)


def project(row, w_t, gathered, cosine, sine, query_heads, key_heads):
    cols, width = w_t.shape
    count = gathered.shape[1]
    tile = 256
    q_cols = query_heads * DH
    kv_cols = 2 * key_heads * DH
    return pl.pallas_call(
        functools.partial(
            qkv_kernel, query_heads=query_heads, key_heads=key_heads, scale=DH ** (-0.5)
        ),
        grid=(count // tile,),
        in_specs=[
            pl.BlockSpec((cols, width), lambda i: (0, 0)),
            pl.BlockSpec((1, tile, width), lambda i: (row, i, 0)),
            pl.BlockSpec((1, HALF, tile), lambda i: (row, 0, i)),
            pl.BlockSpec((1, HALF, tile), lambda i: (row, 0, i)),
        ],
        out_specs=[
            pl.BlockSpec((q_cols, tile), lambda i: (0, i)),
            pl.BlockSpec((kv_cols, tile), lambda i: (0, i)),
        ],
        out_shape=[
            jax.ShapeDtypeStruct((q_cols, count), bf16),
            jax.ShapeDtypeStruct((kv_cols, count), bf16),
        ],
        compiler_params=pltpu.CompilerParams(vmem_limit_bytes=32 * 2**20),
        cost_estimate=pl.CostEstimate(
            flops=2 * cols * width * count, bytes_accessed=4 * count * width, transcendentals=0
        ),
    )(w_t, gathered, cosine, sine)


def forward_kernel(
    meta_ref, q_ref, kv_ref, start_ref, o_ref, low_ref, lse_ref, max_s, sum_s, acc_s,
    *, row, group, order
):
    span = q_ref.shape[1]
    here = meta_ref[0]
    first = meta_ref[1 + 2 * row]
    middle = meta_ref[2 + 2 * row]
    start = start_ref[0]
    key_iota = lax.broadcasted_iota(jnp.int32, (span, span), 0)

    def step(block, masked, diagonal):
        slot = 0 if diagonal else slot_of(block ^ here, order)
        k_t = kv_ref[slot, 0:DH, :]
        v_t = kv_ref[slot, DH : 2 * DH, :]
        keys = k_t.T
        if masked:
            keep = key_iota + block * span >= start
        if diagonal:
            keep = keep & (key_iota <= lax.broadcasted_iota(jnp.int32, (span, span), 1))
        for g in range(group):
            scores = mm(keys, q_ref[DH * g : DH * g + DH, :])
            if masked:
                scores = jnp.where(keep, scores, neg_big)
            top = jnp.max(scores, axis=0, keepdims=True)
            if diagonal:
                new_max = top
            else:
                old_max = max_s[g : g + 1, :]
                new_max = jnp.maximum(old_max, top)
            weights = jnp.exp(scores - new_max)
            total = jnp.sum(weights, axis=0, keepdims=True)
            mixed = mm(v_t, weights.astype(bf16))
            at = slice(DH * g, DH * g + DH)
            if diagonal:
                sum_s[g : g + 1, :] = total
                acc_s[at, :] = mixed
            else:
                factor = jnp.exp(old_max - new_max)
                sum_s[g : g + 1, :] = sum_s[g : g + 1, :] * factor + total
                acc_s[at, :] = acc_s[at, :] * factor + mixed
            max_s[g : g + 1, :] = new_max

    step(here, True, True)

    @pl.loop(first, middle)
    def _(block):
        step(block, True, False)

    @pl.loop(middle, here)
    def _(block):
        step(block, False, False)

    for g in range(group):
        at = slice(DH * g, DH * g + DH)
        total = sum_s[g : g + 1, :]
        out = acc_s[at, :] / total
        o_ref[at, :] = out
        low_ref[at, :] = out.astype(bf16)
        lse_ref[0, g : g + 1, :] = max_s[g : g + 1, :] + jnp.log(total)


def attend(row, meta, q_t, kv_all, starts, group, order):
    span = q_t.shape[1]
    blocks = kv_all.shape[0]
    key_heads = kv_all.shape[1] // (2 * DH)
    cols = group * DH
    head_spec = pl.BlockSpec((cols, span), lambda h, m: (h, 0))
    return pl.pallas_call(
        functools.partial(forward_kernel, row=row, group=group, order=order),
        grid_spec=pltpu.PrefetchScalarGridSpec(
            num_scalar_prefetch=1,
            grid=(key_heads,),
            in_specs=[
                head_spec,
                pl.BlockSpec((blocks, 2 * DH, span), lambda h, m: (0, h, 0)),
                pl.BlockSpec((1, 1, span), lambda h, m: (row, 0, 0)),
            ],
            out_specs=[
                head_spec,
                head_spec,
                pl.BlockSpec((1, group, span), lambda h, m: (h, 0, 0)),
            ],
            scratch_shapes=[
                pltpu.VMEM((group, span), f32),
                pltpu.VMEM((group, span), f32),
                pltpu.VMEM((cols, span), f32),
            ],
        ),
        out_shape=[
            jax.ShapeDtypeStruct((key_heads * cols, span), f32),
            jax.ShapeDtypeStruct((key_heads * cols, span), bf16),
            jax.ShapeDtypeStruct((key_heads, group, span), f32),
        ],
        compiler_params=pltpu.CompilerParams(vmem_limit_bytes=40 * 2**20),
        cost_estimate=pl.CostEstimate(
            flops=16 * blocks * span * span * cols,
            bytes_accessed=4 * kv_all.size,
            transcendentals=0,
        ),
    )(meta, q_t, kv_all, starts)


def backward_kernel(
    meta_ref, q_ref, do_ref, o_ref, lse_ref, kv_ref, start_ref, cos_ref, sin_ref,
    dq_ref, dkv_ref, dq_s, q_s, do_t_s, do_s, delta_s,
    *, row, group, order, scale
):
    span = q_ref.shape[1]
    here = meta_ref[0]
    first = meta_ref[1 + 2 * row]
    middle = meta_ref[2 + 2 * row]
    start = start_ref[0]
    key_iota = lax.broadcasted_iota(jnp.int32, (span, span), 0)
    dkv_ref[...] = jnp.zeros(dkv_ref.shape, bf16)
    part = do_ref.shape[2]
    for device in range(do_ref.shape[0]):
        do_t_s[:, part * device : part * (device + 1)] = do_ref[device]
    for g in range(group):
        at = slice(DH * g, DH * g + DH)
        q_s[g] = q_ref[at, :].T
        do_s[g] = do_t_s[at, :].T
        delta_s[g : g + 1, :] = jnp.sum(
            do_t_s[at, :].astype(f32) * o_ref[at, :], axis=0, keepdims=True
        )

    def step(block, masked, diagonal):
        slot = 0 if diagonal else slot_of(block ^ here, order)
        k_t = kv_ref[slot, 0:DH, :]
        v_t = kv_ref[slot, DH : 2 * DH, :]
        keys = k_t.T
        values = v_t.T
        if masked:
            keep = key_iota + block * span >= start
        if diagonal:
            keep = keep & (key_iota <= lax.broadcasted_iota(jnp.int32, (span, span), 1))
        d_keys = None
        d_values = None
        for g in range(group):
            at = slice(DH * g, DH * g + DH)
            scores = mm(keys, q_ref[at, :])
            probs = jnp.exp(scores - lse_ref[0, g : g + 1, :])
            if masked:
                probs = jnp.where(keep, probs, 0.0)
            d_probs = mm(values, do_t_s[at, :])
            d_scores = (probs * (d_probs - delta_s[g : g + 1, :])).astype(bf16)
            dq = mm(k_t, d_scores)
            if diagonal:
                dq_s[at, :] = dq
            else:
                dq_s[at, :] += dq
            dv = mm(probs.astype(bf16), do_s[g])
            dk = mm(d_scores, q_s[g])
            d_keys = dk if d_keys is None else d_keys + dk
            d_values = dv if d_values is None else d_values + dv
        dkv_ref[slot, 0:DH, :] = d_keys.T.astype(bf16)
        dkv_ref[slot, DH : 2 * DH, :] = d_values.T.astype(bf16)

    step(here, True, True)

    @pl.loop(first, middle)
    def _(block):
        step(block, True, False)

    @pl.loop(middle, here)
    def _(block):
        step(block, False, False)

    cosine = cos_ref[0]
    sine = sin_ref[0]
    for g in range(group):
        low = dq_s[DH * g : DH * g + HALF, :] * scale
        high = dq_s[DH * g + HALF : DH * g + DH, :] * scale
        dq_ref[DH * g : DH * g + HALF, :] = (low * cosine + high * sine).astype(bf16)
        dq_ref[DH * g + HALF : DH * g + DH, :] = (high * cosine - low * sine).astype(bf16)


def attend_back(row, meta, q_t, do_parts, o_t, lse, kv_all, starts, cosine, sine, group, order):
    span = q_t.shape[1]
    blocks = kv_all.shape[0]
    key_heads = kv_all.shape[1] // (2 * DH)
    cols = group * DH
    kv_devices, _, part = do_parts.shape
    head_spec = pl.BlockSpec((cols, span), lambda h, m: (h, 0))
    kv_spec = pl.BlockSpec((blocks, 2 * DH, span), lambda h, m: (0, h, 0))
    angle_spec = pl.BlockSpec((1, HALF, span), lambda h, m: (row, 0, 0))
    return pl.pallas_call(
        functools.partial(
            backward_kernel, row=row, group=group, order=order, scale=DH ** (-0.5)
        ),
        grid_spec=pltpu.PrefetchScalarGridSpec(
            num_scalar_prefetch=1,
            grid=(key_heads,),
            in_specs=[
                head_spec,
                pl.BlockSpec((kv_devices, cols, part), lambda h, m: (0, h, 0)),
                head_spec,
                pl.BlockSpec((1, group, span), lambda h, m: (h, 0, 0)),
                kv_spec,
                pl.BlockSpec((1, 1, span), lambda h, m: (row, 0, 0)),
                angle_spec,
                angle_spec,
            ],
            out_specs=[head_spec, kv_spec],
            scratch_shapes=[
                pltpu.VMEM((cols, span), f32),
                pltpu.VMEM((group, span, DH), bf16),
                pltpu.VMEM((cols, span), bf16),
                pltpu.VMEM((group, span, DH), bf16),
                pltpu.VMEM((group, span), f32),
            ],
        ),
        out_shape=[
            jax.ShapeDtypeStruct((key_heads * cols, span), bf16),
            jax.ShapeDtypeStruct(kv_all.shape, bf16),
        ],
        compiler_params=pltpu.CompilerParams(vmem_limit_bytes=40 * 2**20),
        cost_estimate=pl.CostEstimate(
            flops=40 * blocks * span * span * cols,
            bytes_accessed=4 * kv_all.size,
            transcendentals=0,
        ),
    )(meta, q_t, do_parts, o_t, lse, kv_all, starts, cosine, sine)


def experts_kernel(*refs, row_count, experts):
    heads = refs[:row_count]
    (
        x_ref, dy_ref, mix_ref, gain_ref, w_out_ref, gate_ref, up_ref, down_ref
    ) = refs[row_count : row_count + 8]
    outs = refs[row_count + 8 :]
    out_ref, dh_ref, ggate_ref, gup_ref, gdown_ref, gout_ref = outs[:6]
    d_heads = outs[6 : 6 + row_count]
    hid_s, hat_s, recip_s, norm_s, norm_t_s, acc_s, dn_s = outs[6 + row_count :]
    expert = pl.program_id(0)
    part = heads[0].shape[1]
    width = x_ref.shape[1]

    @pl.when(expert == 0)
    def _():
        for row in range(row_count):
            at = slice(part * row, part * (row + 1))
            branch = mm(heads[row][...].T, w_out_ref[...])
            hidden = x_ref[at, :].astype(f32) + branch
            recip = lax.rsqrt(jnp.mean(hidden * hidden, axis=-1, keepdims=True) + epsilon)
            hat = hidden * recip
            hid_s[at, :] = hidden
            hat_s[at, :] = hat
            recip_s[at, :] = recip
            norm_s[at, :] = (hat * gain_ref[...]).astype(bf16)
        norm_t_s[...] = norm_s[...].T
        acc_s[...] = hid_s[...]
        dn_s[...] = jnp.zeros(dn_s.shape, f32)

    normed = norm_s[...]
    mix = mix_ref[0]
    gate_pre = mm(normed, gate_ref[0])
    up_pre = mm(normed, up_ref[0])
    gate_sig = 1.0 / (1.0 + jnp.exp(-gate_pre))
    gate_act = gate_pre * gate_sig
    hid = (gate_act * up_pre).astype(bf16)
    acc_s[...] += mix * mm(hid, down_ref[0])
    d_expert = (mix * dy_ref[...].astype(f32)).astype(bf16)
    d_hid = mm(d_expert, down_ref[0], NT)
    d_gate = (d_hid * up_pre * (gate_sig * (1.0 + gate_pre * (1.0 - gate_sig)))).astype(bf16)
    d_up = (d_hid * gate_act).astype(bf16)
    dn_s[...] += mm(d_gate, gate_ref[0], NT) + mm(d_up, up_ref[0], NT)
    gdown_ref[0] = mm(hid.T, d_expert).astype(bf16)
    ggate_ref[0] = mm(norm_t_s[...], d_gate).astype(bf16)
    gup_ref[0] = mm(norm_t_s[...], d_up).astype(bf16)

    @pl.when(expert == experts - 1)
    def _():
        out_ref[...] = acc_s[...].astype(bf16)
        hat = hat_s[...]
        d_norm = dn_s[...]
        head_cols = w_out_ref.shape[0]
        gout_ref[head_cols:, :] = jnp.broadcast_to(
            jnp.sum(d_norm * hat, axis=0, keepdims=True), (16, width)
        ).astype(bf16)
        d_hat = d_norm * gain_ref[...]
        mean = jnp.mean(d_hat * hat, axis=-1, keepdims=True)
        d_hidden = dy_ref[...].astype(f32) + recip_s[...] * (d_hat - hat * mean)
        dh_ref[...] = d_hidden
        d_branch = d_hidden.astype(bf16)
        grad_out = None
        for row in range(row_count):
            at = slice(part * row, part * (row + 1))
            piece = d_branch[at, :]
            d_heads[row][...] = mm(w_out_ref[...], piece, NT).astype(bf16)
            term = mm(heads[row][...], piece)
            grad_out = term if grad_out is None else grad_out + term
        gout_ref[0:head_cols, :] = grad_out.astype(bf16)


def run_experts(heads, x_rows, dy_rows, mix, gain, w_out_all, w_gate, w_up, w_down):
    own, width = x_rows.shape
    experts, _, hidden = w_gate.shape
    row_count = len(heads)
    head_cols, part = heads[0].shape

    def whole(shape):
        return pl.BlockSpec(shape, lambda e: (0,) * len(shape))

    gate_spec = pl.BlockSpec((1, width, hidden), lambda e: (e, 0, 0))
    down_spec = pl.BlockSpec((1, hidden, width), lambda e: (e, 0, 0))
    return pl.pallas_call(
        functools.partial(experts_kernel, row_count=row_count, experts=experts),
        grid=(experts,),
        in_specs=[whole((head_cols, part))] * row_count
        + [
            whole((own, width)),
            whole((own, width)),
            pl.BlockSpec((1, own, 1), lambda e: (e, 0, 0)),
            whole((1, width)),
            whole((head_cols, width)),
            gate_spec,
            gate_spec,
            down_spec,
        ],
        out_specs=[
            whole((own, width)),
            whole((own, width)),
            gate_spec,
            gate_spec,
            down_spec,
            whole((head_cols + 16, width)),
        ]
        + [whole((head_cols, part))] * row_count,
        out_shape=[
            jax.ShapeDtypeStruct((own, width), bf16),
            jax.ShapeDtypeStruct((own, width), f32),
            jax.ShapeDtypeStruct(w_gate.shape, bf16),
            jax.ShapeDtypeStruct(w_up.shape, bf16),
            jax.ShapeDtypeStruct(w_down.shape, bf16),
            jax.ShapeDtypeStruct((head_cols + 16, width), bf16),
        ]
        + [jax.ShapeDtypeStruct((head_cols, part), bf16)] * row_count,
        scratch_shapes=[
            pltpu.VMEM((own, width), f32),
            pltpu.VMEM((own, width), f32),
            pltpu.VMEM((own, 1), f32),
            pltpu.VMEM((own, width), bf16),
            pltpu.VMEM((width, own), bf16),
            pltpu.VMEM((own, width), f32),
            pltpu.VMEM((own, width), f32),
        ],
        compiler_params=pltpu.CompilerParams(vmem_limit_bytes=56 * 2**20),
        cost_estimate=pl.CostEstimate(
            flops=18 * own * width * hidden * experts,
            bytes_accessed=6 * w_gate.size * 2,
            transcendentals=0,
        ),
    )(*heads, x_rows, dy_rows, mix, gain, w_out_all, w_gate, w_up, w_down)


def inner_kernel(*refs, row_count, query_cols, key_heads):
    dq = refs[:row_count]
    dkv = refs[row_count : 2 * row_count]
    n_ref, cos_ref, sin_ref, parts_ref, grad_ref, inner_s = refs[2 * row_count :]
    kv_devices = parts_ref.shape[0]
    part = parts_ref.shape[2] // row_count
    grad = None
    for row in range(row_count):
        cosine = cos_ref[row]
        sine = sin_ref[row]
        inner_s[0:query_cols, :] = dq[row][...]
        for head in range(key_heads):
            at = 2 * DH * head
            low = dkv[row][at : at + HALF, :].astype(f32)
            high = dkv[row][at + HALF : at + DH, :].astype(f32)
            to = query_cols + DH * head
            inner_s[to : to + HALF, :] = (low * cosine + high * sine).astype(bf16)
            inner_s[to + HALF : to + DH, :] = (high * cosine - low * sine).astype(bf16)
            to = query_cols + DH * (key_heads + head)
            inner_s[to : to + DH, :] = dkv[row][at + DH : at + 2 * DH, :]
        for device in range(kv_devices):
            parts_ref[device, :, part * row : part * (row + 1)] = inner_s[
                :, part * device : part * (device + 1)
            ]
        term = mm(inner_s[...], n_ref[row])
        grad = term if grad is None else grad + term
    grad_ref[...] = grad.astype(bf16)


def inner_grads(dq, dkv, gathered, cosine, sine, kv_devices, key_heads):
    row_count = len(dq)
    query_cols, span = dq[0].shape
    cols, width = query_cols + dkv[0].shape[0], gathered.shape[2]
    own = row_count * span // kv_devices
    return pl.pallas_call(
        functools.partial(
            inner_kernel, row_count=row_count, query_cols=query_cols, key_heads=key_heads
        ),
        out_shape=[
            jax.ShapeDtypeStruct((kv_devices, cols, own), bf16),
            jax.ShapeDtypeStruct((cols, width), bf16),
        ],
        scratch_shapes=[pltpu.VMEM((cols, span), bf16)],
        compiler_params=pltpu.CompilerParams(vmem_limit_bytes=40 * 2**20),
        cost_estimate=pl.CostEstimate(
            flops=2 * row_count * span * cols * width,
            bytes_accessed=4 * gathered.size,
            transcendentals=0,
        ),
    )(*dq, *dkv, gathered, cosine, sine)


def tokens_kernel(d_inner_ref, w_ref, x_ref, dh_ref, gain_ref, out_ref):
    x_float = x_ref[...].astype(f32)
    recip = lax.rsqrt(jnp.mean(x_float * x_float, axis=-1, keepdims=True) + epsilon)
    x_hat = x_float * recip
    d_normed = mm(d_inner_ref[...].T, w_ref[...])
    d_hat = d_normed * gain_ref[...]
    mean = jnp.mean(d_hat * x_hat, axis=-1, keepdims=True)
    out_ref[...] = (dh_ref[...] + recip * (d_hat - x_hat * mean)).astype(bf16)


def token_grads(d_inner, w_all, x_rows, d_hidden, gain):
    own, width = x_rows.shape
    cols = d_inner.shape[0]
    return pl.pallas_call(
        tokens_kernel,
        out_shape=jax.ShapeDtypeStruct((own, width), bf16),
        compiler_params=pltpu.CompilerParams(vmem_limit_bytes=40 * 2**20),
        cost_estimate=pl.CostEstimate(
            flops=2 * own * width * cols, bytes_accessed=2 * cols * width, transcendentals=0
        ),
    )(d_inner, w_all, x_rows, d_hidden, gain)


def widen_kernel(*refs):
    half = len(refs) // 2
    for source, target in zip(refs[:half], refs[half:]):
        target[...] = source[...].astype(f32)


def widen(arrays):
    specs = [pl.BlockSpec((1,) + a.shape[1:], lambda e: (e, 0, 0)) for a in arrays]
    return pl.pallas_call(
        widen_kernel,
        grid=(arrays[0].shape[0],),
        in_specs=specs,
        out_specs=specs,
        out_shape=[jax.ShapeDtypeStruct(a.shape, f32) for a in arrays],
        compiler_params=pltpu.CompilerParams(vmem_limit_bytes=40 * 2**20),
        cost_estimate=pl.CostEstimate(
            flops=0, bytes_accessed=6 * sum(a.size for a in arrays), transcendentals=0
        ),
    )(*arrays)


def per_device(
    tokens,
    cotangent,
    norm_first,
    w_query,
    w_key,
    w_value,
    w_out,
    norm_second,
    w_gate,
    w_up,
    w_down,
    routes,
    gate_weights,
    segment_ids,
    positions,
):
    row_count, block_len, width = tokens.shape
    kv_devices = lax.axis_size("kv")
    seq_devices = lax.axis_size("seq")
    seq_len = block_len * kv_devices
    seq_index = lax.axis_index("seq")
    query_cols = w_query.shape[1]
    key_cols = w_key.shape[1]
    query_heads = query_cols // DH
    key_heads = key_cols // DH
    group = query_heads // key_heads
    expert_count = w_gate.shape[0]
    own = row_count * block_len
    rows = range(row_count)
    orders = [seq_order(row, seq_devices) for row in rows]

    place = seq_index * seq_len + jnp.arange(seq_len, dtype=jnp.int32)
    starts = place[None, :] - positions
    first_block = starts[:, 0] // seq_len
    middle_block = jnp.clip((starts[:, -1] + seq_len - 1) // seq_len, first_block, seq_index)
    bounds = jnp.stack([first_block, middle_block], axis=1).reshape(-1)
    meta = jnp.concatenate([seq_index[None], bounds]).astype(jnp.int32)
    starts3 = starts.reshape(row_count, 1, seq_len)
    freqs = theta_base ** (-(jnp.arange(HALF, dtype=f32) * 2.0) / DH)
    angles = freqs[None, :, None] * positions.astype(f32)[:, None, :]
    cosine = jnp.cos(angles)
    sine = jnp.sin(angles)

    x_float = tokens.astype(f32)
    recip_first = lax.rsqrt(jnp.mean(x_float * x_float, axis=-1, keepdims=True) + epsilon)
    normed = (x_float * recip_first * norm_first).astype(bf16)
    gathered = lax.all_gather(normed, "kv", axis=1, tiled=True)

    w_t = jnp.concatenate([w_query.T, w_key.T, w_value.T], axis=0)
    inner_cols = w_t.shape[0]
    expert_ids = jnp.arange(expert_count, dtype=jnp.int32)
    picks = routes[..., None] == expert_ids
    local_load = jnp.sum(picks.astype(f32), axis=(0, 1, 2))
    load_rows = jnp.pad(local_load.astype(bf16)[None, :], ((0, 15), (0, width - expert_count)))

    def gather_rows(matrix, extra=None):
        share = matrix.shape[0] // seq_devices
        piece = lax.dynamic_slice_in_dim(matrix, seq_index * share, share, 0)
        if extra is not None:
            piece = jnp.concatenate([piece, extra], axis=0)
        spread = lax.all_gather(piece, ("seq", "kv"))
        spread = spread.reshape(seq_devices, kv_devices, piece.shape[0], width)
        whole = spread[:, :, :share].transpose(1, 0, 2, 3)
        return whole.reshape(kv_devices * matrix.shape[0], width), spread[:, :, share:]

    w_out_all, loads = gather_rows(w_out, load_rows)
    load_sum = jnp.sum(loads[:, :, 0, :expert_count].astype(f32), axis=(0, 1))
    w_inner_all, _ = gather_rows(w_t)

    def exchange(value):
        return lax.all_to_all(value, "kv", 0, 0)

    q_t, kv_all, o_t, lse, heads = [], [], [], [], []
    for row in rows:
        q_row, kv_row = project(row, w_t, gathered, cosine, sine, query_heads, key_heads)
        q_t.append(q_row)
        kv_all.append(spread_seq(kv_row, orders[row]))
    for row in rows:
        o_row, low_row, lse_row = attend(
            row, meta, q_t[row], kv_all[row], starts3, group, orders[row]
        )
        o_t.append(o_row)
        lse.append(lse_row)
        parts = low_row.reshape(query_cols, kv_devices, block_len).transpose(1, 0, 2)
        heads.append(exchange(parts).reshape(kv_devices * query_cols, block_len))

    mix = jnp.sum(picks.astype(f32) * gate_weights[..., None], axis=2)
    mix = mix.reshape(own, expert_count).T[:, :, None]
    x_rows = tokens.reshape(own, width)
    outs = run_experts(
        heads,
        x_rows,
        cotangent.reshape(own, width),
        mix,
        norm_second.reshape(1, width),
        w_out_all,
        w_gate,
        w_up,
        w_down,
    )
    block_out, d_hidden, grad_gate, grad_up, grad_down, grad_out = outs[:6]
    d_heads = outs[6:]
    grad_gate, grad_up, grad_down, grad_out = lax.psum(
        (grad_gate, grad_up, grad_down, grad_out), ("seq", "kv")
    )
    second_sum = grad_out[kv_devices * query_cols]

    do_parts = [exchange(d.reshape(kv_devices, query_cols, block_len)) for d in d_heads]
    dq, dkv = [], []
    for row in rows:
        dq_row, dkv_row = attend_back(
            row, meta, q_t[row], do_parts[row], o_t[row], lse[row], kv_all[row], starts3,
            cosine, sine, group, orders[row],
        )
        dq.append(dq_row)
        dkv.append(collect_seq(dkv_row, orders[row]))
    d_parts, grad_inner_part = inner_grads(
        dq, dkv, gathered, cosine, sine, kv_devices, key_heads
    )
    d_inner = exchange(d_parts).reshape(kv_devices * inner_cols, own)
    half = inner_cols // 2
    grad_inner = jnp.concatenate(
        [
            sum_seq(grad_inner_part[:half], seq_order(0, seq_devices)),
            sum_seq(grad_inner_part[half:], seq_order(1, seq_devices)),
        ],
        axis=0,
    ).astype(f32)
    first_part = jnp.sum(w_t.astype(f32) * grad_inner, axis=0)
    first_sum = lax.psum(first_part, "kv") / norm_first
    d_tokens = token_grads(d_inner, w_inner_all, x_rows, d_hidden, norm_first.reshape(1, width))
    grad_gate, grad_up, grad_down = widen([grad_gate, grad_up, grad_down])
    own_out = lax.dynamic_slice_in_dim(
        grad_out, lax.axis_index("kv") * query_cols, query_cols, 0
    ).astype(f32)
    return (
        block_out.reshape(tokens.shape),
        d_tokens.reshape(tokens.shape),
        first_sum,
        grad_inner[:query_cols].T,
        grad_inner[query_cols : query_cols + key_cols].T,
        grad_inner[query_cols + key_cols :].T,
        own_out,
        second_sum.astype(f32),
        grad_gate,
        grad_up,
        grad_down,
        load_sum.astype(jnp.int32),
    )


def solution(mesh):
    in_specs = (
        P(None, ("seq", "kv"), None),
        P(None, ("seq", "kv"), None),
        P(),
        P(None, "kv"),
        P(None, "kv"),
        P(None, "kv"),
        P("kv", None),
        P(),
        P(),
        P(),
        P(),
        P(None, ("seq", "kv"), None),
        P(None, ("seq", "kv"), None),
        P(),
        P(None, "seq"),
    )
    out_specs = (
        P(None, ("seq", "kv"), None),
        P(None, ("seq", "kv"), None),
        P(),
        P(None, "kv"),
        P(None, "kv"),
        P(None, "kv"),
        P("kv", None),
        P(),
        P(),
        P(),
        P(),
        P(),
    )
    return jax.shard_map(
        per_device, mesh=mesh, in_specs=in_specs, out_specs=out_specs, check_vma=False
    )
```

```python
import functools

import jax
import jax.numpy as jnp
from jax import lax
from jax.experimental import pallas as pl
from jax.experimental.pallas import tpu as pltpu
from jax.sharding import PartitionSpec as P

DH = 64
HALF = DH // 2

epsilon = 1e-05
neg_big = -1e30
theta_base = 10000.0
highest = lax.Precision.HIGHEST
f32 = jnp.float32
bf16 = jnp.bfloat16

NN = (((1,), (0,)), ((), ()))
NT = (((1,), (1,)), ((), ()))


def mm(a, b, dims=NN):
    return lax.dot_general(a, b, dims, preferred_element_type=f32)


def seq_bits(axis_size):
    bits = []
    bit = 2
    while bit < axis_size:
        bits.append(bit)
        bit *= 2
    return bits


def seq_order(row, axis_size):
    bits = seq_bits(axis_size)
    return (bits if row % 2 == 0 else bits[::-1]) + [1]


def slot_of(mask, order):
    slot = 0
    for at, bit in enumerate(order):
        slot = slot + (((mask >> (bit.bit_length() - 1)) & 1) << at)
    return slot


def swap(value, axis, mask):
    count = lax.axis_size(axis)
    return lax.ppermute(value, axis, [(source, source ^ mask) for source in range(count)])


def spread_seq(value, order, other):
    held = value[None]
    for bit in order:
        if bit == order[-1]:
            held = behind(held, other)
        held = jnp.concatenate([held, swap(held, "seq", bit)], axis=0)
    return held


def collect_seq(value, order):
    held = value
    for bit in order[::-1]:
        half = held.shape[0] // 2
        came = swap(held[half:], "seq", bit)
        held = (held[:half].astype(f32) + came.astype(f32)).astype(bf16)
    return held[0]


def sum_seq(value, order):
    index = lax.axis_index("seq")
    held = value
    for bit in order[::-1]:
        half = held.shape[0] // 2
        upper = (index & bit) != 0
        keep = jnp.where(upper, held[half:], held[:half])
        send = jnp.where(upper, held[:half], held[half:])
        held = (keep.astype(f32) + swap(send, "seq", bit).astype(f32)).astype(bf16)
    for bit in order:
        upper = (index & bit) != 0
        came = swap(held, "seq", bit)
        held = jnp.where(
            upper,
            jnp.concatenate([came, held], axis=0),
            jnp.concatenate([held, came], axis=0),
        )
    return held


def behind(value, other):
    return value if other is None else lax.optimization_barrier((value, other))[0]


def cut(value, index, size):
    return lax.dynamic_slice_in_dim(value, index * size, size, 0)


def sum_over(value, axis):
    mask = 1
    while mask < lax.axis_size(axis):
        value = value + swap(value, axis, mask)
        mask *= 2
    return value


def added(first, second):
    return (first.astype(f32) + second.astype(f32)).astype(bf16)


def qkv_kernel(w_ref, n_ref, cos_ref, sin_ref, q_ref, kv_ref, *, query_heads, key_heads, scale):
    acc = mm(w_ref[...], n_ref[0], NT)
    cosine = cos_ref[0]
    sine = sin_ref[0]
    for head in range(query_heads):
        low = acc[DH * head : DH * head + HALF]
        high = acc[DH * head + HALF : DH * head + DH]
        q_ref[DH * head : DH * head + HALF, :] = ((low * cosine - high * sine) * scale).astype(bf16)
        q_ref[DH * head + HALF : DH * head + DH, :] = (
            (high * cosine + low * sine) * scale
        ).astype(bf16)
    base = DH * query_heads
    for head in range(key_heads):
        low = acc[base + DH * head : base + DH * head + HALF]
        high = acc[base + DH * head + HALF : base + DH * head + DH]
        at = 2 * DH * head
        kv_ref[at : at + HALF, :] = (low * cosine - high * sine).astype(bf16)
        kv_ref[at + HALF : at + DH, :] = (high * cosine + low * sine).astype(bf16)
        start = base + DH * (key_heads + head)
        kv_ref[at + DH : at + 2 * DH, :] = acc[start : start + DH].astype(bf16)


def project(row, w_t, gathered, cosine, sine, query_heads, key_heads):
    cols, width = w_t.shape
    count = gathered.shape[1]
    tile = 256
    q_cols = query_heads * DH
    kv_cols = 2 * key_heads * DH
    return pl.pallas_call(
        functools.partial(
            qkv_kernel, query_heads=query_heads, key_heads=key_heads, scale=DH ** (-0.5)
        ),
        grid=(count // tile,),
        in_specs=[
            pl.BlockSpec((cols, width), lambda i: (0, 0)),
            pl.BlockSpec((1, tile, width), lambda i: (row, i, 0)),
            pl.BlockSpec((1, HALF, tile), lambda i: (row, 0, i)),
            pl.BlockSpec((1, HALF, tile), lambda i: (row, 0, i)),
        ],
        out_specs=[
            pl.BlockSpec((q_cols, tile), lambda i: (0, i)),
            pl.BlockSpec((kv_cols, tile), lambda i: (0, i)),
        ],
        out_shape=[
            jax.ShapeDtypeStruct((q_cols, count), bf16),
            jax.ShapeDtypeStruct((kv_cols, count), bf16),
        ],
        compiler_params=pltpu.CompilerParams(vmem_limit_bytes=60 * 2**20),
        cost_estimate=pl.CostEstimate(
            flops=2 * cols * width * count, bytes_accessed=4 * count * width, transcendentals=0
        ),
    )(w_t, gathered, cosine, sine)


def forward_kernel(
    meta_ref, q_ref, kv_ref, start_ref, o_ref, low_ref, lse_ref, max_s, sum_s, acc_s,
    *, row, group, order
):
    span = q_ref.shape[1]
    here = meta_ref[0]
    first = meta_ref[1 + 2 * row]
    middle = meta_ref[2 + 2 * row]
    start = start_ref[0]
    key_iota = lax.broadcasted_iota(jnp.int32, (span, span), 0)

    def step(block, masked, diagonal):
        slot = 0 if diagonal else slot_of(block ^ here, order)
        k_t = kv_ref[slot, 0:DH, :]
        v_t = kv_ref[slot, DH : 2 * DH, :]
        keys = k_t.T
        if masked:
            keep = key_iota + block * span >= start
        if diagonal:
            keep = keep & (key_iota <= lax.broadcasted_iota(jnp.int32, (span, span), 1))
        for g in range(group):
            scores = mm(keys, q_ref[DH * g : DH * g + DH, :])
            if masked:
                scores = jnp.where(keep, scores, neg_big)
            top = jnp.max(scores, axis=0, keepdims=True)
            if diagonal:
                new_max = top
            else:
                old_max = max_s[g : g + 1, :]
                new_max = jnp.maximum(old_max, top)
            weights = jnp.exp(scores - new_max)
            total = jnp.sum(weights, axis=0, keepdims=True)
            mixed = mm(v_t, weights.astype(bf16))
            at = slice(DH * g, DH * g + DH)
            if diagonal:
                sum_s[g : g + 1, :] = total
                acc_s[at, :] = mixed
            else:
                factor = jnp.exp(old_max - new_max)
                sum_s[g : g + 1, :] = sum_s[g : g + 1, :] * factor + total
                acc_s[at, :] = acc_s[at, :] * factor + mixed
            max_s[g : g + 1, :] = new_max

    step(here, True, True)

    @pl.loop(first, middle)
    def _(block):
        step(block, True, False)

    @pl.loop(middle, here)
    def _(block):
        step(block, False, False)

    for g in range(group):
        at = slice(DH * g, DH * g + DH)
        total = sum_s[g : g + 1, :]
        out = acc_s[at, :] / total
        o_ref[at, :] = out
        low_ref[at, :] = out.astype(bf16)
        lse_ref[0, g : g + 1, :] = max_s[g : g + 1, :] + jnp.log(total)


def attend(row, meta, q_t, kv_all, starts, group, order):
    span = q_t.shape[1]
    blocks = kv_all.shape[0]
    key_heads = kv_all.shape[1] // (2 * DH)
    cols = group * DH
    head_spec = pl.BlockSpec((cols, span), lambda h, m: (h, 0))
    return pl.pallas_call(
        functools.partial(forward_kernel, row=row, group=group, order=order),
        grid_spec=pltpu.PrefetchScalarGridSpec(
            num_scalar_prefetch=1,
            grid=(key_heads,),
            in_specs=[
                head_spec,
                pl.BlockSpec((blocks, 2 * DH, span), lambda h, m: (0, h, 0)),
                pl.BlockSpec((1, 1, span), lambda h, m: (row, 0, 0)),
            ],
            out_specs=[
                head_spec,
                head_spec,
                pl.BlockSpec((1, group, span), lambda h, m: (h, 0, 0)),
            ],
            scratch_shapes=[
                pltpu.VMEM((group, span), f32),
                pltpu.VMEM((group, span), f32),
                pltpu.VMEM((cols, span), f32),
            ],
        ),
        out_shape=[
            jax.ShapeDtypeStruct((key_heads * cols, span), f32),
            jax.ShapeDtypeStruct((key_heads * cols, span), bf16),
            jax.ShapeDtypeStruct((key_heads, group, span), f32),
        ],
        compiler_params=pltpu.CompilerParams(vmem_limit_bytes=40 * 2**20),
        cost_estimate=pl.CostEstimate(
            flops=16 * blocks * span * span * cols,
            bytes_accessed=4 * kv_all.size,
            transcendentals=0,
        ),
    )(meta, q_t, kv_all, starts)


def backward_kernel(
    meta_ref, q_ref, do_ref, o_ref, lse_ref, kv_ref, start_ref, cos_ref, sin_ref,
    dq_ref, dkv_ref, dq_s, q_s, do_t_s, do_s, delta_s,
    *, row, group, order, scale
):
    span = q_ref.shape[1]
    here = meta_ref[0]
    first = meta_ref[1 + 2 * row]
    middle = meta_ref[2 + 2 * row]
    start = start_ref[0]
    key_iota = lax.broadcasted_iota(jnp.int32, (span, span), 0)
    dkv_ref[...] = jnp.zeros(dkv_ref.shape, bf16)
    part = do_ref.shape[2]
    for device in range(do_ref.shape[0]):
        do_t_s[:, part * device : part * (device + 1)] = do_ref[device]
    for g in range(group):
        at = slice(DH * g, DH * g + DH)
        q_s[g] = q_ref[at, :].T
        do_s[g] = do_t_s[at, :].T
        delta_s[g : g + 1, :] = jnp.sum(
            do_t_s[at, :].astype(f32) * o_ref[at, :], axis=0, keepdims=True
        )

    def step(block, masked, diagonal):
        slot = 0 if diagonal else slot_of(block ^ here, order)
        k_t = kv_ref[slot, 0:DH, :]
        v_t = kv_ref[slot, DH : 2 * DH, :]
        keys = k_t.T
        values = v_t.T
        if masked:
            keep = key_iota + block * span >= start
        if diagonal:
            keep = keep & (key_iota <= lax.broadcasted_iota(jnp.int32, (span, span), 1))
        d_keys = None
        d_values = None
        for g in range(group):
            at = slice(DH * g, DH * g + DH)
            scores = mm(keys, q_ref[at, :])
            probs = jnp.exp(scores - lse_ref[0, g : g + 1, :])
            if masked:
                probs = jnp.where(keep, probs, 0.0)
            d_probs = mm(values, do_t_s[at, :])
            d_scores = (probs * (d_probs - delta_s[g : g + 1, :])).astype(bf16)
            dq = mm(k_t, d_scores)
            if diagonal:
                dq_s[at, :] = dq
            else:
                dq_s[at, :] += dq
            dv = mm(probs.astype(bf16), do_s[g])
            dk = mm(d_scores, q_s[g])
            d_keys = dk if d_keys is None else d_keys + dk
            d_values = dv if d_values is None else d_values + dv
        dkv_ref[slot, 0:DH, :] = d_keys.T.astype(bf16)
        dkv_ref[slot, DH : 2 * DH, :] = d_values.T.astype(bf16)

    step(here, True, True)

    @pl.loop(first, middle)
    def _(block):
        step(block, True, False)

    @pl.loop(middle, here)
    def _(block):
        step(block, False, False)

    cosine = cos_ref[0]
    sine = sin_ref[0]
    for g in range(group):
        low = dq_s[DH * g : DH * g + HALF, :] * scale
        high = dq_s[DH * g + HALF : DH * g + DH, :] * scale
        dq_ref[DH * g : DH * g + HALF, :] = (low * cosine + high * sine).astype(bf16)
        dq_ref[DH * g + HALF : DH * g + DH, :] = (high * cosine - low * sine).astype(bf16)


def attend_back(row, meta, q_t, do_parts, o_t, lse, kv_all, starts, cosine, sine, group, order):
    span = q_t.shape[1]
    blocks = kv_all.shape[0]
    key_heads = kv_all.shape[1] // (2 * DH)
    cols = group * DH
    kv_devices, _, part = do_parts.shape
    head_spec = pl.BlockSpec((cols, span), lambda h, m: (h, 0))
    kv_spec = pl.BlockSpec((blocks, 2 * DH, span), lambda h, m: (0, h, 0))
    angle_spec = pl.BlockSpec((1, HALF, span), lambda h, m: (row, 0, 0))
    return pl.pallas_call(
        functools.partial(
            backward_kernel, row=row, group=group, order=order, scale=DH ** (-0.5)
        ),
        grid_spec=pltpu.PrefetchScalarGridSpec(
            num_scalar_prefetch=1,
            grid=(key_heads,),
            in_specs=[
                head_spec,
                pl.BlockSpec((kv_devices, cols, part), lambda h, m: (0, h, 0)),
                head_spec,
                pl.BlockSpec((1, group, span), lambda h, m: (h, 0, 0)),
                kv_spec,
                pl.BlockSpec((1, 1, span), lambda h, m: (row, 0, 0)),
                angle_spec,
                angle_spec,
            ],
            out_specs=[head_spec, kv_spec],
            scratch_shapes=[
                pltpu.VMEM((cols, span), f32),
                pltpu.VMEM((group, span, DH), bf16),
                pltpu.VMEM((cols, span), bf16),
                pltpu.VMEM((group, span, DH), bf16),
                pltpu.VMEM((group, span), f32),
            ],
        ),
        out_shape=[
            jax.ShapeDtypeStruct((key_heads * cols, span), bf16),
            jax.ShapeDtypeStruct(kv_all.shape, bf16),
        ],
        compiler_params=pltpu.CompilerParams(vmem_limit_bytes=40 * 2**20),
        cost_estimate=pl.CostEstimate(
            flops=40 * blocks * span * span * cols,
            bytes_accessed=4 * kv_all.size,
            transcendentals=0,
        ),
    )(meta, q_t, do_parts, o_t, lse, kv_all, starts, cosine, sine)


def experts_kernel(core_ref, *refs, experts):
    (
        heads_ref, x_ref, dy_ref, mix_ref, gain_ref, own_ref, other_ref, gate_ref, up_ref, down_ref
    ) = refs[:10]
    outs = refs[10:]
    row_count, part = heads_ref.shape[1], heads_ref.shape[3]
    out_ref, dh_ref, ggate_ref, gup_ref, send_out, keep_out, gain_grad_ref = outs[:7]
    d_heads = outs[7 : 7 + row_count]
    hid_s, hat_s, recip_s, norm_s, norm_t_s, acc_s, dn_s, w_out_s = outs[7 + row_count :]
    expert = pl.program_id(0)
    width = x_ref.shape[1]

    @pl.when(expert == 0)
    def _():
        for device in range(own_ref.shape[0]):
            w_out_s[device, core_ref[0]] = own_ref[device]
            w_out_s[device, 1 - core_ref[0]] = other_ref[device]
        w_out = w_out_s[...].reshape(-1, width)
        for row in range(row_count):
            at = slice(part * row, part * (row + 1))
            branch = mm(heads_ref[:, row].reshape(-1, part).T, w_out)
            hidden = x_ref[at, :].astype(f32) + branch
            recip = lax.rsqrt(jnp.mean(hidden * hidden, axis=-1, keepdims=True) + epsilon)
            hat = hidden * recip
            hid_s[at, :] = hidden
            hat_s[at, :] = hat
            recip_s[at, :] = recip
            norm_s[at, :] = (hat * gain_ref[...]).astype(bf16)
        norm_t_s[...] = norm_s[...].T
        acc_s[...] = hid_s[...]
        dn_s[...] = jnp.zeros(dn_s.shape, f32)

    normed = norm_s[...]
    mix = mix_ref[0]
    gate_pre = mm(normed, gate_ref[0])
    up_pre = mm(normed, up_ref[0])
    gate_sig = 1.0 / (1.0 + jnp.exp(-gate_pre))
    gate_act = gate_pre * gate_sig
    hid = (gate_act * up_pre).astype(bf16)
    acc_s[...] += mix * mm(hid, down_ref[0])
    d_expert = (mix * dy_ref[...].astype(f32)).astype(bf16)
    d_hid = mm(d_expert, down_ref[0], NT)
    d_gate = (d_hid * up_pre * (gate_sig * (1.0 + gate_pre * (1.0 - gate_sig)))).astype(bf16)
    d_up = (d_hid * gate_act).astype(bf16)
    dn_s[...] += mm(d_gate, gate_ref[0], NT) + mm(d_up, up_ref[0], NT)
    grad_down = mm(hid.T, d_expert).astype(bf16)
    half = experts // 2

    @pl.when(expert < half)
    def _():
        send_out[expert] = grad_down

    @pl.when(expert >= half)
    def _():
        keep_out[expert - half] = grad_down

    ggate_ref[0] = mm(norm_t_s[...], d_gate).astype(bf16)
    gup_ref[0] = mm(norm_t_s[...], d_up).astype(bf16)

    @pl.when(expert == experts - 1)
    def _():
        out_ref[...] = acc_s[...].astype(bf16)
        hat = hat_s[...]
        d_norm = dn_s[...]
        w_out = w_out_s[...].reshape(-1, width)
        gain_grad_ref[...] = jnp.sum(d_norm * hat, axis=0, keepdims=True)
        d_hat = d_norm * gain_ref[...]
        mean = jnp.mean(d_hat * hat, axis=-1, keepdims=True)
        d_hidden = dy_ref[...].astype(f32) + recip_s[...] * (d_hat - hat * mean)
        dh_ref[...] = d_hidden
        d_branch = d_hidden.astype(bf16)
        grad_out = None
        for row in range(row_count):
            at = slice(part * row, part * (row + 1))
            piece = d_branch[at, :]
            d_heads[row][...] = mm(w_out, piece, NT).astype(bf16)
            term = mm(heads_ref[:, row].reshape(-1, part), piece)
            grad_out = term if grad_out is None else grad_out + term
        grad_out = grad_out.astype(bf16)
        part_rows = grad_out.shape[0] // (2 * (send_out.shape[0] - half))

        @pl.when(core_ref[0] == 0)
        def _():
            for at in range(send_out.shape[0] - half):
                keep_out[half + at] = grad_out[part_rows * at : part_rows * (at + 1)]
                start = grad_out.shape[0] // 2 + part_rows * at
                send_out[half + at] = grad_out[start : start + part_rows]

        @pl.when(core_ref[0] != 0)
        def _():
            for at in range(send_out.shape[0] - half):
                send_out[half + at] = grad_out[part_rows * at : part_rows * (at + 1)]
                start = grad_out.shape[0] // 2 + part_rows * at
                keep_out[half + at] = grad_out[start : start + part_rows]


def run_experts(
    core, heads, x_rows, dy_rows, mix, gain, w_out_half, w_out_other, w_gate, w_up, w_down
):
    own, width = x_rows.shape
    experts, _, hidden = w_gate.shape
    kv_devices, row_count, _, part = heads.shape
    half_rows = w_out_half.shape[1]
    head_cols = 2 * kv_devices * half_rows

    def whole(shape):
        return pl.BlockSpec(shape, lambda e, m: (0,) * len(shape))

    half = experts // 2

    def which(e, m):
        return lax.rem(e + (1 - m[0]) * half, experts)

    gate_spec = pl.BlockSpec((1, width, hidden), lambda e, m: (which(e, m), 0, 0))
    down_spec = pl.BlockSpec((1, hidden, width), lambda e, m: (which(e, m), 0, 0))
    outer = (half + head_cols // (2 * hidden), hidden, width)
    return pl.pallas_call(
        functools.partial(experts_kernel, experts=experts),
        grid_spec=pltpu.PrefetchScalarGridSpec(
            num_scalar_prefetch=1,
            grid=(experts,),
            in_specs=[
                whole(heads.shape),
                whole((own, width)),
                whole((own, width)),
                pl.BlockSpec((1, own, 1), lambda e, m: (which(e, m), 0, 0)),
                whole((1, width)),
                whole(w_out_half.shape),
                whole(w_out_half.shape),
                gate_spec,
                gate_spec,
                down_spec,
            ],
            out_specs=[
                whole((own, width)),
                whole((own, width)),
                gate_spec,
                gate_spec,
                whole(outer),
                whole(outer),
                whole((1, width)),
            ]
            + [whole((head_cols, part))] * row_count,
            scratch_shapes=[
                pltpu.VMEM((own, width), f32),
                pltpu.VMEM((own, width), f32),
                pltpu.VMEM((own, 1), f32),
                pltpu.VMEM((own, width), bf16),
                pltpu.VMEM((width, own), bf16),
                pltpu.VMEM((own, width), f32),
                pltpu.VMEM((own, width), f32),
                pltpu.VMEM((kv_devices, 2, half_rows, width), bf16),
            ],
        ),
        out_shape=[
            jax.ShapeDtypeStruct((own, width), bf16),
            jax.ShapeDtypeStruct((own, width), f32),
            jax.ShapeDtypeStruct(w_gate.shape, bf16),
            jax.ShapeDtypeStruct(w_up.shape, bf16),
            jax.ShapeDtypeStruct(outer, bf16),
            jax.ShapeDtypeStruct(outer, bf16),
            jax.ShapeDtypeStruct((1, width), f32),
        ]
        + [jax.ShapeDtypeStruct((head_cols, part), bf16)] * row_count,
        compiler_params=pltpu.CompilerParams(vmem_limit_bytes=56 * 2**20),
        cost_estimate=pl.CostEstimate(
            flops=18 * own * width * hidden * experts,
            bytes_accessed=6 * w_gate.size * 2,
            transcendentals=0,
        ),
    )(
        core, heads, x_rows, dy_rows, mix, gain, w_out_half, w_out_other,
        w_gate, w_up, w_down,
    )


def inner_kernel(*refs, row_count, query_cols, key_heads):
    dq = refs[:row_count]
    dkv = refs[row_count : 2 * row_count]
    n_ref, cos_ref, sin_ref, parts_ref, grad_ref, inner_s = refs[2 * row_count :]
    kv_devices = parts_ref.shape[0]
    part = parts_ref.shape[2] // row_count
    grad = None
    for row in range(row_count):
        cosine = cos_ref[row]
        sine = sin_ref[row]
        inner_s[0:query_cols, :] = dq[row][...]
        for head in range(key_heads):
            at = 2 * DH * head
            low = dkv[row][at : at + HALF, :].astype(f32)
            high = dkv[row][at + HALF : at + DH, :].astype(f32)
            to = query_cols + DH * head
            inner_s[to : to + HALF, :] = (low * cosine + high * sine).astype(bf16)
            inner_s[to + HALF : to + DH, :] = (high * cosine - low * sine).astype(bf16)
            to = query_cols + DH * (key_heads + head)
            inner_s[to : to + DH, :] = dkv[row][at + DH : at + 2 * DH, :]
        for device in range(kv_devices):
            parts_ref[device, :, part * row : part * (row + 1)] = inner_s[
                :, part * device : part * (device + 1)
            ]
        term = mm(inner_s[...], n_ref[row])
        grad = term if grad is None else grad + term
    grad_ref[...] = grad.astype(bf16)


def inner_grads(dq, dkv, gathered, cosine, sine, kv_devices, key_heads):
    row_count = len(dq)
    query_cols, span = dq[0].shape
    cols, width = query_cols + dkv[0].shape[0], gathered.shape[2]
    own = row_count * span // kv_devices
    return pl.pallas_call(
        functools.partial(
            inner_kernel, row_count=row_count, query_cols=query_cols, key_heads=key_heads
        ),
        out_shape=[
            jax.ShapeDtypeStruct((kv_devices, cols, own), bf16),
            jax.ShapeDtypeStruct((cols, width), bf16),
        ],
        scratch_shapes=[pltpu.VMEM((cols, span), bf16)],
        compiler_params=pltpu.CompilerParams(vmem_limit_bytes=40 * 2**20),
        cost_estimate=pl.CostEstimate(
            flops=2 * row_count * span * cols * width,
            bytes_accessed=4 * gathered.size,
            transcendentals=0,
        ),
    )(*dq, *dkv, gathered, cosine, sine)


def tokens_kernel(core_ref, d_inner_ref, own_ref, other_ref, x_ref, dh_ref, gain_ref, out_ref):
    x_float = x_ref[...].astype(f32)
    recip = lax.rsqrt(jnp.mean(x_float * x_float, axis=-1, keepdims=True) + epsilon)
    x_hat = x_float * recip
    core = core_ref[0]
    d_normed = None
    for device in range(own_ref.shape[0]):
        term = mm(d_inner_ref[device, core].T, own_ref[device])
        term += mm(d_inner_ref[device, 1 - core].T, other_ref[device])
        d_normed = term if d_normed is None else d_normed + term
    d_hat = d_normed * gain_ref[...]
    mean = jnp.mean(d_hat * x_hat, axis=-1, keepdims=True)
    out_ref[...] = (dh_ref[...] + recip * (d_hat - x_hat * mean)).astype(bf16)


def token_grads(core, d_inner, w_half, w_other, x_rows, d_hidden, gain):
    own, width = x_rows.shape
    return pl.pallas_call(
        tokens_kernel,
        in_specs=[pl.BlockSpec(memory_space=pltpu.SMEM)]
        + [pl.BlockSpec(memory_space=pltpu.VMEM)] * 6,
        out_shape=jax.ShapeDtypeStruct((own, width), bf16),
        compiler_params=pltpu.CompilerParams(vmem_limit_bytes=40 * 2**20),
        cost_estimate=pl.CostEstimate(
            flops=4 * d_inner.size * width, bytes_accessed=4 * w_half.size, transcendentals=0
        ),
    )(core, d_inner, w_half, w_other, x_rows, d_hidden, gain)


def widen_kernel(core_ref, gate_ref, up_ref, own_ref, other_ref, ggate_ref, gup_ref, gdown_ref, *, half):
    ggate_ref[...] = gate_ref[...].astype(f32)
    gup_ref[...] = up_ref[...].astype(f32)

    @pl.when(pl.program_id(0) < half)
    def _():
        gdown_ref[...] = own_ref[...].astype(f32)

    @pl.when(pl.program_id(0) >= half)
    def _():
        gdown_ref[...] = other_ref[...].astype(f32)


def widen(core, grad_gate, grad_up, own_down, other_down):
    experts, width, hidden = grad_gate.shape
    half = experts // 2

    def which(e, m):
        return lax.rem(e + m[0] * half, experts)

    gate_spec = pl.BlockSpec((1, width, hidden), lambda e, m: (which(e, m), 0, 0))
    down_spec = pl.BlockSpec((1, hidden, width), lambda e, m: (which(e, m), 0, 0))
    return pl.pallas_call(
        functools.partial(widen_kernel, half=half),
        grid_spec=pltpu.PrefetchScalarGridSpec(
            num_scalar_prefetch=1,
            grid=(experts,),
            in_specs=[
                gate_spec,
                gate_spec,
                pl.BlockSpec((1, hidden, width), lambda e, m: (jnp.minimum(e, half - 1), 0, 0)),
                pl.BlockSpec((1, hidden, width), lambda e, m: (jnp.maximum(e - half, 0), 0, 0)),
            ],
            out_specs=[gate_spec, gate_spec, down_spec],
        ),
        out_shape=[
            jax.ShapeDtypeStruct(grad_gate.shape, f32),
            jax.ShapeDtypeStruct(grad_gate.shape, f32),
            jax.ShapeDtypeStruct((experts, hidden, width), f32),
        ],
        compiler_params=pltpu.CompilerParams(vmem_limit_bytes=60 * 2**20),
        cost_estimate=pl.CostEstimate(
            flops=0, bytes_accessed=18 * grad_gate.size, transcendentals=0
        ),
    )(core, grad_gate, grad_up, own_down, other_down)


def per_device(
    tokens,
    cotangent,
    norm_first,
    w_query,
    w_key,
    w_value,
    w_out,
    norm_second,
    w_gate,
    w_up,
    w_down,
    routes,
    gate_weights,
    segment_ids,
    positions,
):
    row_count, block_len, width = tokens.shape
    kv_devices = lax.axis_size("kv")
    seq_devices = lax.axis_size("seq")
    seq_len = block_len * kv_devices
    seq_index = lax.axis_index("seq")
    query_cols = w_query.shape[1]
    key_cols = w_key.shape[1]
    query_heads = query_cols // DH
    key_heads = key_cols // DH
    group = query_heads // key_heads
    expert_count = w_gate.shape[0]
    own = row_count * block_len
    rows = range(row_count)
    orders = [seq_order(row, seq_devices) for row in rows]

    place = seq_index * seq_len + jnp.arange(seq_len, dtype=jnp.int32)
    starts = place[None, :] - positions
    first_block = starts[:, 0] // seq_len
    middle_block = jnp.clip((starts[:, -1] + seq_len - 1) // seq_len, first_block, seq_index)
    bounds = jnp.stack([first_block, middle_block], axis=1).reshape(-1)
    meta = jnp.concatenate([seq_index[None], bounds]).astype(jnp.int32)
    starts3 = starts.reshape(row_count, 1, seq_len)
    freqs = theta_base ** (-(jnp.arange(HALF, dtype=f32) * 2.0) / DH)
    angles = freqs[None, :, None] * positions.astype(f32)[:, None, :]
    cosine = jnp.cos(angles)
    sine = jnp.sin(angles)

    x_float = tokens.astype(f32)
    recip_first = lax.rsqrt(jnp.mean(x_float * x_float, axis=-1, keepdims=True) + epsilon)
    normed = (x_float * recip_first * norm_first).astype(bf16)
    gathered = lax.all_gather(normed, "kv", axis=1, tiled=True)

    w_t = jnp.concatenate([w_query.T, w_key.T, w_value.T], axis=0)
    inner_cols = w_t.shape[0]
    expert_ids = jnp.arange(expert_count, dtype=jnp.int32)
    picks = routes[..., None] == expert_ids
    local_load = jnp.sum(picks.astype(f32), axis=(0, 1, 2))
    core_index = seq_index % 2
    half_rows = query_cols // 2
    w_out_half = lax.all_gather(cut(w_out, core_index, half_rows), "kv")
    w_out_other = swap(w_out_half, "seq", 1)
    w_inner_half = lax.all_gather(cut(w_t, core_index, inner_cols // 2), "kv")
    w_inner_other = swap(w_inner_half, "seq", 1)

    def exchange(value):
        return lax.all_to_all(value, "kv", 0, 0)

    q_t, kv_all, o_t, lse, heads = [], [], [], [], []
    kv_t = []
    for row in rows:
        q_row, kv_row = project(row, w_t, gathered, cosine, sine, query_heads, key_heads)
        q_t.append(q_row)
        kv_t.append(kv_row)
    kv_t = lax.optimization_barrier(kv_t)
    kv_all = [spread_seq(kv_t[row], orders[row], None) for row in rows]
    kv_all = lax.optimization_barrier(kv_all)
    for row in rows:
        o_row, low_row, lse_row = attend(
            row, meta, q_t[row], kv_all[row], starts3, group, orders[row]
        )
        o_t.append(o_row)
        lse.append(lse_row)
        heads.append(low_row.reshape(query_cols, kv_devices, block_len).transpose(1, 0, 2))
    heads = exchange(jnp.stack(heads, axis=1))

    mix = jnp.sum(picks.astype(f32) * gate_weights[..., None], axis=2)
    mix = mix.reshape(own, expert_count).T[:, :, None]
    x_rows = tokens.reshape(own, width)
    core = core_index.astype(jnp.int32)[None]
    outs = run_experts(
        core,
        heads,
        x_rows,
        cotangent.reshape(own, width),
        mix,
        norm_second.reshape(1, width),
        w_out_half,
        w_out_other,
        w_gate,
        w_up,
        w_down,
    )
    block_out, d_hidden, grad_gate, grad_up, send_out, keep_out, second_part = outs[:7]
    d_heads = outs[7:]
    grad_gate, grad_up = lax.psum((grad_gate, grad_up), ("seq", "kv"))

    chips = seq_devices // 2
    groups = [[2 * chip + one for chip in range(chips)] for one in range(2)]

    def over_chips(value):
        return lax.all_to_all(value, "seq", 0, 0, axis_index_groups=groups)

    def total(value):
        return jnp.sum(value.astype(f32), axis=0).astype(bf16)

    def copies(value, number):
        return jnp.broadcast_to(value[None], (number,) + value.shape)

    def rest(d_heads, d_hidden, send_out, keep_out, second_part):
        do_parts = [exchange(d.reshape(kv_devices, query_cols, block_len)) for d in d_heads]
        outer = added(keep_out, swap(send_out, "seq", 1)).reshape(chips, -1, width)
        do_parts = [behind(do_part, outer) for do_part in do_parts]
        outer = over_chips(outer)
        dq, dkv = [], []
        for row in rows:
            dq_row, dkv_row = attend_back(
                row, meta, q_t[row], do_parts[row], o_t[row], lse[row], kv_all[row], starts3,
                cosine, sine, group, orders[row],
            )
            dq.append(dq_row)
            dkv.append(collect_seq(dkv_row, orders[row]))
        outer = total(behind(outer, dq[-1]))
        rows_left = outer.shape[0]
        outer = exchange(outer.reshape(kv_devices, rows_left // kv_devices, width))
        outer = total(behind(outer, dkv[-1]))
        dkv[-1] = behind(dkv[-1], outer)
        outer = exchange(copies(outer, kv_devices)).reshape(rows_left, width)
        d_parts, grad_inner_part = inner_grads(
            dq, dkv, gathered, cosine, sine, kv_devices, key_heads
        )
        d_parts = exchange(d_parts).reshape(kv_devices, 2, inner_cols // 2, own)
        half = inner_cols // 2
        grad_inner = jnp.concatenate(
            [
                sum_seq(grad_inner_part[:half], seq_order(0, seq_devices)),
                sum_seq(grad_inner_part[half:], seq_order(1, seq_devices)),
            ],
            axis=0,
        ).astype(f32)
        outer = copies(behind(outer, grad_inner), chips)
        grad_inner, second_part, d_parts = behind((grad_inner, second_part, d_parts), outer)
        outer = over_chips(outer)
        sums = jnp.concatenate([second_part[0], local_load])
        for axis in ("seq", "kv"):
            sums = sum_over(sums, axis)
        first_part = jnp.sum(w_t.astype(f32) * grad_inner, axis=0)
        first_sum = sum_over(first_part, "kv") / norm_first
        d_tokens = token_grads(
            core, d_parts, w_inner_half, w_inner_other, x_rows, d_hidden, norm_first.reshape(1, width)
        )
        own_outer = behind(outer, (d_tokens, first_sum, sums)).reshape(keep_out.shape)
        other_outer = swap(own_outer, "seq", 1)
        kv_index = lax.axis_index("kv")
        half_devices = kv_devices // 2
        start = lax.rem(kv_index, half_devices) * query_cols
        pieces = [
            lax.dynamic_slice_in_dim(
                pair[expert_count // 2 :].reshape(-1, width), start, query_cols, 0
            )
            for pair in (own_outer, other_outer)
        ]
        own_out = jnp.where(kv_index // half_devices == core_index, *pieces).astype(f32)
        return d_tokens, grad_inner, first_sum, own_outer, other_outer, own_out, sums

    operands = (d_heads, d_hidden, send_out, keep_out, second_part)
    shapes = jax.eval_shape(rest, *operands)
    d_tokens, grad_inner, first_sum, own_outer, other_outer, own_out, sums = lax.cond(
        positions[0, 0] >= 0,
        rest,
        lambda *ignored: jax.tree.map(lambda leaf: jnp.zeros(leaf.shape, leaf.dtype), shapes),
        *operands,
    )
    grad_gate, grad_up, grad_down = widen(core, grad_gate, grad_up, own_outer, other_outer)
    return (
        block_out.reshape(tokens.shape),
        d_tokens.reshape(tokens.shape),
        first_sum,
        grad_inner[:query_cols].T,
        grad_inner[query_cols : query_cols + key_cols].T,
        grad_inner[query_cols + key_cols :].T,
        own_out,
        sums[:width],
        grad_gate,
        grad_up,
        grad_down,
        sums[width:].astype(jnp.int32),
    )


def solution(mesh):
    in_specs = (
        P(None, ("seq", "kv"), None),
        P(None, ("seq", "kv"), None),
        P(),
        P(None, "kv"),
        P(None, "kv"),
        P(None, "kv"),
        P("kv", None),
        P(),
        P(),
        P(),
        P(),
        P(None, ("seq", "kv"), None),
        P(None, ("seq", "kv"), None),
        P(),
        P(None, "seq"),
    )
    out_specs = (
        P(None, ("seq", "kv"), None),
        P(None, ("seq", "kv"), None),
        P(),
        P(None, "kv"),
        P(None, "kv"),
        P(None, "kv"),
        P("kv", None),
        P(),
        P(),
        P(),
        P(),
        P(),
    )
    return jax.shard_map(
        per_device, mesh=mesh, in_specs=in_specs, out_specs=out_specs, check_vma=False
    )
```

```python
import functools

import jax
import jax.numpy as jnp
from jax import lax
from jax.experimental import pallas as pl
from jax.experimental.pallas import tpu as pltpu
from jax.sharding import PartitionSpec as P

DH = 64
HALF = DH // 2

epsilon = 1e-05
neg_big = -1e30
theta_base = 10000.0
highest = lax.Precision.HIGHEST
f32 = jnp.float32
bf16 = jnp.bfloat16

NN = (((1,), (0,)), ((), ()))
NT = (((1,), (1,)), ((), ()))


def mm(a, b, dims=NN):
    return lax.dot_general(a, b, dims, preferred_element_type=f32)


def seq_bits(axis_size):
    bits = []
    bit = 2
    while bit < axis_size:
        bits.append(bit)
        bit *= 2
    return bits


def seq_order(row, axis_size):
    bits = seq_bits(axis_size)
    return (bits if row % 2 == 0 else bits[::-1]) + [1]


def slot_of(mask, order):
    slot = 0
    for at, bit in enumerate(order):
        slot = slot + (((mask >> (bit.bit_length() - 1)) & 1) << at)
    return slot


def swap(value, axis, mask):
    if mask == 0:
        return value
    count = lax.axis_size(axis)
    return lax.ppermute(value, axis, [(source, source ^ mask) for source in range(count)])


def spread_seq(value, order, other):
    held = value[None]
    for bit in order:
        if bit == order[-1]:
            held = behind(held, other)
        held = jnp.concatenate([held, swap(held, "seq", bit)], axis=0)
    return held


def collect_seq(value, order):
    held = value
    for bit in order[::-1]:
        half = held.shape[0] // 2
        came = swap(held[half:], "seq", bit)
        held = (held[:half].astype(f32) + came.astype(f32)).astype(bf16)
    return held[0]


def halve_seq(value, order):
    index = lax.axis_index("seq")
    held = value
    for bit in order[::-1]:
        half = held.shape[0] // 2
        upper = (index & bit) != 0
        keep = jnp.where(upper, held[half:], held[:half])
        send = jnp.where(upper, held[:half], held[half:])
        held = (keep.astype(f32) + swap(send, "seq", bit).astype(f32)).astype(bf16)
    return held


def double_seq(value, order):
    index = lax.axis_index("seq")
    held = value
    for bit in order:
        upper = (index & bit) != 0
        came = swap(held, "seq", bit)
        held = jnp.where(
            upper,
            jnp.concatenate([came, held], axis=0),
            jnp.concatenate([held, came], axis=0),
        )
    return held


def behind(value, other):
    return value if other is None else lax.optimization_barrier((value, other))[0]


def cut(value, index, size):
    return lax.dynamic_slice_in_dim(value, index * size, size, 0)


def sum_over(value, axis):
    mask = 1
    while mask < lax.axis_size(axis):
        value = value + swap(value, axis, mask)
        mask *= 2
    return value


def added(first, second):
    return (first.astype(f32) + second.astype(f32)).astype(bf16)


def qkv_kernel(w_ref, n_ref, cos_ref, sin_ref, q_ref, kv_ref, *, query_heads, key_heads, scale):
    acc = mm(w_ref[...], n_ref[0], NT)
    cosine = cos_ref[0]
    sine = sin_ref[0]
    for head in range(query_heads):
        low = acc[DH * head : DH * head + HALF]
        high = acc[DH * head + HALF : DH * head + DH]
        q_ref[DH * head : DH * head + HALF, :] = ((low * cosine - high * sine) * scale).astype(bf16)
        q_ref[DH * head + HALF : DH * head + DH, :] = (
            (high * cosine + low * sine) * scale
        ).astype(bf16)
    base = DH * query_heads
    for head in range(key_heads):
        low = acc[base + DH * head : base + DH * head + HALF]
        high = acc[base + DH * head + HALF : base + DH * head + DH]
        at = 2 * DH * head
        kv_ref[at : at + HALF, :] = (low * cosine - high * sine).astype(bf16)
        kv_ref[at + HALF : at + DH, :] = (high * cosine + low * sine).astype(bf16)
        start = base + DH * (key_heads + head)
        kv_ref[at + DH : at + 2 * DH, :] = acc[start : start + DH].astype(bf16)


def project(row, w_t, gathered, cosine, sine, query_heads, key_heads):
    cols, width = w_t.shape
    count = gathered.shape[1]
    tile = 256
    q_cols = query_heads * DH
    kv_cols = 2 * key_heads * DH
    return pl.pallas_call(
        functools.partial(
            qkv_kernel, query_heads=query_heads, key_heads=key_heads, scale=DH ** (-0.5)
        ),
        grid=(count // tile,),
        in_specs=[
            pl.BlockSpec((cols, width), lambda i: (0, 0)),
            pl.BlockSpec((1, tile, width), lambda i: (row, i, 0)),
            pl.BlockSpec((1, HALF, tile), lambda i: (row, 0, i)),
            pl.BlockSpec((1, HALF, tile), lambda i: (row, 0, i)),
        ],
        out_specs=[
            pl.BlockSpec((q_cols, tile), lambda i: (0, i)),
            pl.BlockSpec((kv_cols, tile), lambda i: (0, i)),
        ],
        out_shape=[
            jax.ShapeDtypeStruct((q_cols, count), bf16),
            jax.ShapeDtypeStruct((kv_cols, count), bf16),
        ],
        compiler_params=pltpu.CompilerParams(vmem_limit_bytes=60 * 2**20),
        cost_estimate=pl.CostEstimate(
            flops=2 * cols * width * count, bytes_accessed=4 * count * width, transcendentals=0
        ),
    )(w_t, gathered, cosine, sine)


def forward_kernel(
    meta_ref, q_ref, kv_ref, start_ref, o_ref, low_ref, lse_ref, max_s, sum_s, acc_s,
    *, row, group, order
):
    span = q_ref.shape[1]
    here = meta_ref[0]
    first = meta_ref[1 + 2 * row]
    middle = meta_ref[2 + 2 * row]
    start = start_ref[0]
    key_iota = lax.broadcasted_iota(jnp.int32, (span, span), 0)

    def step(block, masked, diagonal):
        slot = 0 if diagonal else slot_of(block ^ here, order)
        k_t = kv_ref[slot, 0:DH, :]
        v_t = kv_ref[slot, DH : 2 * DH, :]
        keys = k_t.T
        if masked:
            keep = key_iota + block * span >= start
        if diagonal:
            keep = keep & (key_iota <= lax.broadcasted_iota(jnp.int32, (span, span), 1))
        for g in range(group):
            scores = mm(keys, q_ref[DH * g : DH * g + DH, :])
            if masked:
                scores = jnp.where(keep, scores, neg_big)
            top = jnp.max(scores, axis=0, keepdims=True)
            if diagonal:
                new_max = top
            else:
                old_max = max_s[g : g + 1, :]
                new_max = jnp.maximum(old_max, top)
            weights = jnp.exp(scores - new_max)
            total = jnp.sum(weights, axis=0, keepdims=True)
            mixed = mm(v_t, weights.astype(bf16))
            at = slice(DH * g, DH * g + DH)
            if diagonal:
                sum_s[g : g + 1, :] = total
                acc_s[at, :] = mixed
            else:
                factor = jnp.exp(old_max - new_max)
                sum_s[g : g + 1, :] = sum_s[g : g + 1, :] * factor + total
                acc_s[at, :] = acc_s[at, :] * factor + mixed
            max_s[g : g + 1, :] = new_max

    step(here, True, True)

    @pl.loop(first, middle)
    def _(block):
        step(block, True, False)

    @pl.loop(middle, here)
    def _(block):
        step(block, False, False)

    for g in range(group):
        at = slice(DH * g, DH * g + DH)
        total = sum_s[g : g + 1, :]
        out = acc_s[at, :] / total
        o_ref[at, :] = out
        low_ref[at, :] = out.astype(bf16)
        lse_ref[0, g : g + 1, :] = max_s[g : g + 1, :] + jnp.log(total)


def attend(row, meta, q_t, kv_all, starts, group, order):
    span = q_t.shape[1]
    blocks = kv_all.shape[0]
    key_heads = kv_all.shape[1] // (2 * DH)
    cols = group * DH
    head_spec = pl.BlockSpec((cols, span), lambda h, m: (h, 0))
    return pl.pallas_call(
        functools.partial(forward_kernel, row=row, group=group, order=order),
        grid_spec=pltpu.PrefetchScalarGridSpec(
            num_scalar_prefetch=1,
            grid=(key_heads,),
            in_specs=[
                head_spec,
                pl.BlockSpec((blocks, 2 * DH, span), lambda h, m: (0, h, 0)),
                pl.BlockSpec((1, 1, span), lambda h, m: (row, 0, 0)),
            ],
            out_specs=[
                head_spec,
                head_spec,
                pl.BlockSpec((1, group, span), lambda h, m: (h, 0, 0)),
            ],
            scratch_shapes=[
                pltpu.VMEM((group, span), f32),
                pltpu.VMEM((group, span), f32),
                pltpu.VMEM((cols, span), f32),
            ],
        ),
        out_shape=[
            jax.ShapeDtypeStruct((key_heads * cols, span), f32),
            jax.ShapeDtypeStruct((key_heads * cols, span), bf16),
            jax.ShapeDtypeStruct((key_heads, group, span), f32),
        ],
        compiler_params=pltpu.CompilerParams(vmem_limit_bytes=40 * 2**20),
        cost_estimate=pl.CostEstimate(
            flops=16 * blocks * span * span * cols,
            bytes_accessed=4 * kv_all.size,
            transcendentals=0,
        ),
    )(meta, q_t, kv_all, starts)


def backward_kernel(
    meta_ref, q_ref, do_ref, o_ref, lse_ref, kv_ref, start_ref, cos_ref, sin_ref,
    dq_ref, dkv_ref, dq_s, q_s, do_t_s, do_s, delta_s,
    *, row, group, order, scale
):
    span = q_ref.shape[1]
    here = meta_ref[0]
    first = meta_ref[1 + 2 * row]
    middle = meta_ref[2 + 2 * row]
    start = start_ref[0]
    key_iota = lax.broadcasted_iota(jnp.int32, (span, span), 0)
    dkv_ref[...] = jnp.zeros(dkv_ref.shape, bf16)
    part = do_ref.shape[3]
    for device in range(do_ref.shape[0]):
        do_t_s[:, part * device : part * (device + 1)] = do_ref[device, 0]
    for g in range(group):
        at = slice(DH * g, DH * g + DH)
        q_s[g] = q_ref[at, :].T
        do_s[g] = do_t_s[at, :].T
        delta_s[g : g + 1, :] = jnp.sum(
            do_t_s[at, :].astype(f32) * o_ref[at, :], axis=0, keepdims=True
        )

    def step(block, masked, diagonal):
        slot = 0 if diagonal else slot_of(block ^ here, order)
        k_t = kv_ref[slot, 0:DH, :]
        v_t = kv_ref[slot, DH : 2 * DH, :]
        keys = k_t.T
        values = v_t.T
        if masked:
            keep = key_iota + block * span >= start
        if diagonal:
            keep = keep & (key_iota <= lax.broadcasted_iota(jnp.int32, (span, span), 1))
        d_keys = None
        d_values = None
        for g in range(group):
            at = slice(DH * g, DH * g + DH)
            scores = mm(keys, q_ref[at, :])
            probs = jnp.exp(scores - lse_ref[0, g : g + 1, :])
            if masked:
                probs = jnp.where(keep, probs, 0.0)
            d_probs = mm(values, do_t_s[at, :])
            d_scores = (probs * (d_probs - delta_s[g : g + 1, :])).astype(bf16)
            dq = mm(k_t, d_scores)
            if diagonal:
                dq_s[at, :] = dq
            else:
                dq_s[at, :] += dq
            dv = mm(probs.astype(bf16), do_s[g])
            dk = mm(d_scores, q_s[g])
            d_keys = dk if d_keys is None else d_keys + dk
            d_values = dv if d_values is None else d_values + dv
        dkv_ref[slot, 0:DH, :] = d_keys.T.astype(bf16)
        dkv_ref[slot, DH : 2 * DH, :] = d_values.T.astype(bf16)

    step(here, True, True)

    @pl.loop(first, middle)
    def _(block):
        step(block, True, False)

    @pl.loop(middle, here)
    def _(block):
        step(block, False, False)

    cosine = cos_ref[0]
    sine = sin_ref[0]
    for g in range(group):
        low = dq_s[DH * g : DH * g + HALF, :] * scale
        high = dq_s[DH * g + HALF : DH * g + DH, :] * scale
        dq_ref[DH * g : DH * g + HALF, :] = (low * cosine + high * sine).astype(bf16)
        dq_ref[DH * g + HALF : DH * g + DH, :] = (high * cosine - low * sine).astype(bf16)


def attend_back(row, meta, q_t, do_parts, o_t, lse, kv_all, starts, cosine, sine, group, order):
    span = q_t.shape[1]
    blocks = kv_all.shape[0]
    key_heads = kv_all.shape[1] // (2 * DH)
    cols = group * DH
    kv_devices, _, _, part = do_parts.shape
    head_spec = pl.BlockSpec((cols, span), lambda h, m: (h, 0))
    kv_spec = pl.BlockSpec((blocks, 2 * DH, span), lambda h, m: (0, h, 0))
    angle_spec = pl.BlockSpec((1, HALF, span), lambda h, m: (row, 0, 0))
    return pl.pallas_call(
        functools.partial(
            backward_kernel, row=row, group=group, order=order, scale=DH ** (-0.5)
        ),
        grid_spec=pltpu.PrefetchScalarGridSpec(
            num_scalar_prefetch=1,
            grid=(key_heads,),
            in_specs=[
                head_spec,
                pl.BlockSpec((kv_devices, 1, cols, part), lambda h, m: (0, row, h, 0)),
                head_spec,
                pl.BlockSpec((1, group, span), lambda h, m: (h, 0, 0)),
                kv_spec,
                pl.BlockSpec((1, 1, span), lambda h, m: (row, 0, 0)),
                angle_spec,
                angle_spec,
            ],
            out_specs=[head_spec, kv_spec],
            scratch_shapes=[
                pltpu.VMEM((cols, span), f32),
                pltpu.VMEM((group, span, DH), bf16),
                pltpu.VMEM((cols, span), bf16),
                pltpu.VMEM((group, span, DH), bf16),
                pltpu.VMEM((group, span), f32),
            ],
        ),
        out_shape=[
            jax.ShapeDtypeStruct((key_heads * cols, span), bf16),
            jax.ShapeDtypeStruct(kv_all.shape, bf16),
        ],
        compiler_params=pltpu.CompilerParams(vmem_limit_bytes=40 * 2**20),
        cost_estimate=pl.CostEstimate(
            flops=40 * blocks * span * span * cols,
            bytes_accessed=4 * kv_all.size,
            transcendentals=0,
        ),
    )(meta, q_t, do_parts, o_t, lse, kv_all, starts, cosine, sine)


def experts_kernel(core_ref, *refs, experts):
    (
        heads_ref, x_ref, dy_ref, mix_ref, gain_ref, own_ref, other_ref, gate_ref, up_ref, down_ref
    ) = refs[:10]
    outs = refs[10:]
    row_count, part = heads_ref.shape[1], heads_ref.shape[3]
    out_ref, dh_ref, ggate_ref, gup_ref, send_out, keep_out, gain_grad_ref = outs[:7]
    d_heads_ref = outs[7]
    hid_s, hat_s, recip_s, norm_s, norm_t_s, acc_s, dn_s, w_out_s = outs[8:]
    expert = pl.program_id(0)
    width = x_ref.shape[1]

    @pl.when(expert == 0)
    def _():
        for device in range(own_ref.shape[0]):
            w_out_s[device, core_ref[0]] = own_ref[device]
            w_out_s[device, 1 - core_ref[0]] = other_ref[device]
        w_out = w_out_s[...].reshape(-1, width)
        for row in range(row_count):
            at = slice(part * row, part * (row + 1))
            branch = mm(heads_ref[:, row].reshape(-1, part).T, w_out)
            hidden = x_ref[at, :].astype(f32) + branch
            recip = lax.rsqrt(jnp.mean(hidden * hidden, axis=-1, keepdims=True) + epsilon)
            hat = hidden * recip
            hid_s[at, :] = hidden
            hat_s[at, :] = hat
            recip_s[at, :] = recip
            norm_s[at, :] = (hat * gain_ref[...]).astype(bf16)
        norm_t_s[...] = norm_s[...].T
        acc_s[...] = hid_s[...]
        dn_s[...] = jnp.zeros(dn_s.shape, f32)

    normed = norm_s[...]
    mix = mix_ref[0]
    gate_pre = mm(normed, gate_ref[0])
    up_pre = mm(normed, up_ref[0])
    gate_sig = 1.0 / (1.0 + jnp.exp(-gate_pre))
    gate_act = gate_pre * gate_sig
    hid = (gate_act * up_pre).astype(bf16)
    acc_s[...] += mix * mm(hid, down_ref[0])
    d_expert = (mix * dy_ref[...].astype(f32)).astype(bf16)
    d_hid = mm(d_expert, down_ref[0], NT)
    d_gate = (d_hid * up_pre * (gate_sig * (1.0 + gate_pre * (1.0 - gate_sig)))).astype(bf16)
    d_up = (d_hid * gate_act).astype(bf16)
    dn_s[...] += mm(d_gate, gate_ref[0], NT) + mm(d_up, up_ref[0], NT)
    grad_down = mm(hid.T, d_expert).astype(bf16)
    half = experts // 2

    @pl.when(expert < half)
    def _():
        send_out[expert] = grad_down

    @pl.when(expert >= half)
    def _():
        keep_out[expert - half] = grad_down

    ggate_ref[0] = mm(norm_t_s[...], d_gate).astype(bf16)
    gup_ref[0] = mm(norm_t_s[...], d_up).astype(bf16)

    @pl.when(expert == experts - 1)
    def _():
        out_ref[...] = acc_s[...].astype(bf16)
        hat = hat_s[...]
        d_norm = dn_s[...]
        w_out = w_out_s[...].reshape(-1, width)
        gain_grad_ref[...] = jnp.sum(d_norm * hat, axis=0, keepdims=True)
        d_hat = d_norm * gain_ref[...]
        mean = jnp.mean(d_hat * hat, axis=-1, keepdims=True)
        d_hidden = dy_ref[...].astype(f32) + recip_s[...] * (d_hat - hat * mean)
        dh_ref[...] = d_hidden
        d_branch = d_hidden.astype(bf16)
        grad_out = None
        for row in range(row_count):
            at = slice(part * row, part * (row + 1))
            piece = d_branch[at, :]
            d_heads_ref[:, row] = (
                mm(w_out, piece, NT).astype(bf16).reshape(d_heads_ref.shape[0], -1, part)
            )
            term = mm(heads_ref[:, row].reshape(-1, part), piece)
            grad_out = term if grad_out is None else grad_out + term
        grad_out = grad_out.astype(bf16)
        part_rows = grad_out.shape[0] // (2 * (send_out.shape[0] - half))

        @pl.when(core_ref[0] == 0)
        def _():
            for at in range(send_out.shape[0] - half):
                keep_out[half + at] = grad_out[part_rows * at : part_rows * (at + 1)]
                start = grad_out.shape[0] // 2 + part_rows * at
                send_out[half + at] = grad_out[start : start + part_rows]

        @pl.when(core_ref[0] != 0)
        def _():
            for at in range(send_out.shape[0] - half):
                send_out[half + at] = grad_out[part_rows * at : part_rows * (at + 1)]
                start = grad_out.shape[0] // 2 + part_rows * at
                keep_out[half + at] = grad_out[start : start + part_rows]


def run_experts(
    core, heads, x_rows, dy_rows, mix, gain, w_out_half, w_out_other, w_gate, w_up, w_down
):
    own, width = x_rows.shape
    experts, _, hidden = w_gate.shape
    kv_devices, row_count, _, part = heads.shape
    half_rows = w_out_half.shape[1]
    head_cols = 2 * kv_devices * half_rows

    def whole(shape):
        return pl.BlockSpec(shape, lambda e, m: (0,) * len(shape))

    half = experts // 2

    def which(e, m):
        return lax.rem(e + (1 - m[0]) * half, experts)

    gate_spec = pl.BlockSpec((1, width, hidden), lambda e, m: (which(e, m), 0, 0))
    down_spec = pl.BlockSpec((1, hidden, width), lambda e, m: (which(e, m), 0, 0))
    outer = (half + head_cols // (2 * hidden), hidden, width)
    return pl.pallas_call(
        functools.partial(experts_kernel, experts=experts),
        grid_spec=pltpu.PrefetchScalarGridSpec(
            num_scalar_prefetch=1,
            grid=(experts,),
            in_specs=[
                whole(heads.shape),
                whole((own, width)),
                whole((own, width)),
                pl.BlockSpec((1, own, 1), lambda e, m: (which(e, m), 0, 0)),
                whole((1, width)),
                whole(w_out_half.shape),
                whole(w_out_half.shape),
                gate_spec,
                gate_spec,
                down_spec,
            ],
            out_specs=[
                whole((own, width)),
                whole((own, width)),
                gate_spec,
                gate_spec,
                whole(outer),
                whole(outer),
                whole((1, width)),
                whole(heads.shape),
            ],
            scratch_shapes=[
                pltpu.VMEM((own, width), f32),
                pltpu.VMEM((own, width), f32),
                pltpu.VMEM((own, 1), f32),
                pltpu.VMEM((own, width), bf16),
                pltpu.VMEM((width, own), bf16),
                pltpu.VMEM((own, width), f32),
                pltpu.VMEM((own, width), f32),
                pltpu.VMEM((kv_devices, 2, half_rows, width), bf16),
            ],
        ),
        out_shape=[
            jax.ShapeDtypeStruct((own, width), bf16),
            jax.ShapeDtypeStruct((own, width), f32),
            jax.ShapeDtypeStruct(w_gate.shape, bf16),
            jax.ShapeDtypeStruct(w_up.shape, bf16),
            jax.ShapeDtypeStruct(outer, bf16),
            jax.ShapeDtypeStruct(outer, bf16),
            jax.ShapeDtypeStruct((1, width), f32),
            jax.ShapeDtypeStruct(heads.shape, bf16),
        ],
        compiler_params=pltpu.CompilerParams(vmem_limit_bytes=56 * 2**20),
        cost_estimate=pl.CostEstimate(
            flops=18 * own * width * hidden * experts,
            bytes_accessed=6 * w_gate.size * 2,
            transcendentals=0,
        ),
    )(
        core, heads, x_rows, dy_rows, mix, gain, w_out_half, w_out_other,
        w_gate, w_up, w_down,
    )


def inner_kernel(*refs, row_count, query_cols, key_heads):
    dq = refs[:row_count]
    dkv = refs[row_count : 2 * row_count]
    n_ref, cos_ref, sin_ref, parts_ref, grad_ref, inner_s = refs[2 * row_count :]
    kv_devices = parts_ref.shape[0]
    part = parts_ref.shape[2] // row_count
    grad = None
    for row in range(row_count):
        cosine = cos_ref[row]
        sine = sin_ref[row]
        inner_s[0:query_cols, :] = dq[row][...]
        for head in range(key_heads):
            at = 2 * DH * head
            low = dkv[row][at : at + HALF, :].astype(f32)
            high = dkv[row][at + HALF : at + DH, :].astype(f32)
            to = query_cols + DH * head
            inner_s[to : to + HALF, :] = (low * cosine + high * sine).astype(bf16)
            inner_s[to + HALF : to + DH, :] = (high * cosine - low * sine).astype(bf16)
            to = query_cols + DH * (key_heads + head)
            inner_s[to : to + DH, :] = dkv[row][at + DH : at + 2 * DH, :]
        for device in range(kv_devices):
            parts_ref[device, :, part * row : part * (row + 1)] = inner_s[
                :, part * device : part * (device + 1)
            ]
        term = mm(inner_s[...], n_ref[row])
        grad = term if grad is None else grad + term
    grad_ref[...] = grad.astype(bf16)


def inner_grads(dq, dkv, gathered, cosine, sine, kv_devices, key_heads):
    row_count = len(dq)
    query_cols, span = dq[0].shape
    cols, width = query_cols + dkv[0].shape[0], gathered.shape[2]
    own = row_count * span // kv_devices
    return pl.pallas_call(
        functools.partial(
            inner_kernel, row_count=row_count, query_cols=query_cols, key_heads=key_heads
        ),
        out_shape=[
            jax.ShapeDtypeStruct((kv_devices, cols, own), bf16),
            jax.ShapeDtypeStruct((cols, width), bf16),
        ],
        scratch_shapes=[pltpu.VMEM((cols, span), bf16)],
        compiler_params=pltpu.CompilerParams(vmem_limit_bytes=40 * 2**20),
        cost_estimate=pl.CostEstimate(
            flops=2 * row_count * span * cols * width,
            bytes_accessed=4 * gathered.size,
            transcendentals=0,
        ),
    )(*dq, *dkv, gathered, cosine, sine)


def tokens_kernel(place_ref, *refs):
    own_ref, other_ref, x_ref, dh_ref, gain_ref, out_ref = refs[-6:]
    x_float = x_ref[...].astype(f32)
    recip = lax.rsqrt(jnp.mean(x_float * x_float, axis=-1, keepdims=True) + epsilon)
    x_hat = x_float * recip
    core = place_ref[0]
    d_normed = None
    for mask, piece in enumerate(refs[:-6]):
        device = place_ref[1] ^ mask
        term = mm(piece[core].T, own_ref[device])
        term += mm(piece[1 - core].T, other_ref[device])
        d_normed = term if d_normed is None else d_normed + term
    d_hat = d_normed * gain_ref[...]
    mean = jnp.mean(d_hat * x_hat, axis=-1, keepdims=True)
    out_ref[...] = (dh_ref[...] + recip * (d_hat - x_hat * mean)).astype(bf16)


def token_grads(place, d_inner, w_half, w_other, x_rows, d_hidden, gain):
    own, width = x_rows.shape
    return pl.pallas_call(
        tokens_kernel,
        in_specs=[pl.BlockSpec(memory_space=pltpu.SMEM)]
        + [pl.BlockSpec(memory_space=pltpu.VMEM)] * (5 + len(d_inner)),
        out_shape=jax.ShapeDtypeStruct((own, width), bf16),
        compiler_params=pltpu.CompilerParams(vmem_limit_bytes=40 * 2**20),
        cost_estimate=pl.CostEstimate(
            flops=4 * w_half.size * own, bytes_accessed=4 * w_half.size, transcendentals=0
        ),
    )(place, *d_inner, w_half, w_other, x_rows, d_hidden, gain)


def widen_kernel(core_ref, gate_ref, up_ref, own_ref, other_ref, ggate_ref, gup_ref, gdown_ref, *, half):
    ggate_ref[...] = gate_ref[...].astype(f32)
    gup_ref[...] = up_ref[...].astype(f32)

    @pl.when(pl.program_id(0) < half)
    def _():
        gdown_ref[0] = own_ref[...].astype(f32)

    @pl.when(pl.program_id(0) >= half)
    def _():
        gdown_ref[0] = other_ref[...].astype(f32)


def widen(core, grad_gate, grad_up, own_down, other_down):
    experts, width, hidden = grad_gate.shape
    half = experts // 2

    def which(e, m):
        return lax.rem(e + m[0] * half, experts)

    gate_spec = pl.BlockSpec((1, width, hidden), lambda e, m: (which(e, m), 0, 0))
    down_spec = pl.BlockSpec((1, hidden, width), lambda e, m: (which(e, m), 0, 0))
    return pl.pallas_call(
        functools.partial(widen_kernel, half=half),
        grid_spec=pltpu.PrefetchScalarGridSpec(
            num_scalar_prefetch=1,
            grid=(experts,),
            in_specs=[
                gate_spec,
                gate_spec,
                pl.BlockSpec((hidden, width), lambda e, m: (jnp.minimum(e, half - 1), 0)),
                pl.BlockSpec((hidden, width), lambda e, m: (jnp.maximum(e - half, 0), 0)),
            ],
            out_specs=[gate_spec, gate_spec, down_spec],
        ),
        out_shape=[
            jax.ShapeDtypeStruct(grad_gate.shape, f32),
            jax.ShapeDtypeStruct(grad_gate.shape, f32),
            jax.ShapeDtypeStruct((experts, hidden, width), f32),
        ],
        compiler_params=pltpu.CompilerParams(vmem_limit_bytes=60 * 2**20),
        cost_estimate=pl.CostEstimate(
            flops=0, bytes_accessed=18 * grad_gate.size, transcendentals=0
        ),
    )(core, grad_gate, grad_up, own_down, other_down)


def per_device(
    tokens,
    cotangent,
    norm_first,
    w_query,
    w_key,
    w_value,
    w_out,
    norm_second,
    w_gate,
    w_up,
    w_down,
    routes,
    gate_weights,
    segment_ids,
    positions,
):
    row_count, block_len, width = tokens.shape
    kv_devices = lax.axis_size("kv")
    seq_devices = lax.axis_size("seq")
    seq_len = block_len * kv_devices
    seq_index = lax.axis_index("seq")
    query_cols = w_query.shape[1]
    key_cols = w_key.shape[1]
    query_heads = query_cols // DH
    key_heads = key_cols // DH
    group = query_heads // key_heads
    expert_count = w_gate.shape[0]
    own = row_count * block_len
    rows = range(row_count)
    orders = [seq_order(row, seq_devices) for row in rows]

    place = seq_index * seq_len + jnp.arange(seq_len, dtype=jnp.int32)
    starts = place[None, :] - positions
    first_block = starts[:, 0] // seq_len
    middle_block = jnp.clip((starts[:, -1] + seq_len - 1) // seq_len, first_block, seq_index)
    bounds = jnp.stack([first_block, middle_block], axis=1).reshape(-1)
    meta = jnp.concatenate([seq_index[None], bounds]).astype(jnp.int32)
    starts3 = starts.reshape(row_count, 1, seq_len)
    freqs = theta_base ** (-(jnp.arange(HALF, dtype=f32) * 2.0) / DH)
    angles = freqs[None, :, None] * positions.astype(f32)[:, None, :]
    cosine = jnp.cos(angles)
    sine = jnp.sin(angles)

    x_float = tokens.astype(f32)
    recip_first = lax.rsqrt(jnp.mean(x_float * x_float, axis=-1, keepdims=True) + epsilon)
    normed = (x_float * recip_first * norm_first).astype(bf16)
    gathered = lax.all_gather(normed, "kv", axis=1, tiled=True)

    w_t = jnp.concatenate([w_query.T, w_key.T, w_value.T], axis=0)
    inner_cols = w_t.shape[0]
    expert_ids = jnp.arange(expert_count, dtype=jnp.int32)
    picks = routes[..., None] == expert_ids
    local_load = jnp.sum(picks.astype(f32), axis=(0, 1, 2))
    core_index = seq_index % 2
    half_rows = query_cols // 2
    w_out_half = lax.all_gather(cut(w_out, core_index, half_rows), "kv")
    w_out_other = swap(w_out_half, "seq", 1)
    w_inner_half = lax.all_gather(cut(w_t, core_index, inner_cols // 2), "kv")
    w_inner_other = swap(w_inner_half, "seq", 1)

    def exchange(value):
        return lax.all_to_all(value, "kv", 0, 0)

    q_t, kv_all, o_t, lse, heads = [], [], [], [], []
    kv_t = []
    for row in rows:
        q_row, kv_row = project(row, w_t, gathered, cosine, sine, query_heads, key_heads)
        q_t.append(q_row)
        kv_t.append(kv_row)
    kv_t = lax.optimization_barrier(kv_t)
    kv_all = [spread_seq(kv_t[row], orders[row], None) for row in rows]
    kv_all = lax.optimization_barrier(kv_all)
    for row in rows:
        o_row, low_row, lse_row = attend(
            row, meta, q_t[row], kv_all[row], starts3, group, orders[row]
        )
        o_t.append(o_row)
        lse.append(lse_row)
        heads.append(low_row.reshape(query_cols, kv_devices, block_len).transpose(1, 0, 2))
    heads = exchange(jnp.stack(heads, axis=1))

    mix = jnp.sum(picks.astype(f32) * gate_weights[..., None], axis=2)
    mix = mix.reshape(own, expert_count).T[:, :, None]
    x_rows = tokens.reshape(own, width)
    core = core_index.astype(jnp.int32)[None]
    outs = run_experts(
        core,
        heads,
        x_rows,
        cotangent.reshape(own, width),
        mix,
        norm_second.reshape(1, width),
        w_out_half,
        w_out_other,
        w_gate,
        w_up,
        w_down,
    )
    block_out, d_hidden, grad_gate, grad_up, send_out, keep_out, second_part = outs[:7]
    d_heads = outs[7]
    grad_gate, grad_up = lax.psum((grad_gate, grad_up), ("seq", "kv"))

    chips = seq_devices // 2
    groups = [[2 * chip + one for chip in range(chips)] for one in range(2)]

    def over_chips(value):
        return lax.all_to_all(value, "seq", 0, 0, axis_index_groups=groups)

    def total(value):
        return jnp.sum(value.astype(f32), axis=0).astype(bf16)

    def copies(value, number):
        return jnp.broadcast_to(value[None], (number,) + value.shape)

    def rest(d_heads, d_hidden, send_out, keep_out, second_part):
        do_parts = exchange(d_heads)
        outer = added(keep_out, swap(send_out, "seq", 1)).reshape(chips, -1, width)
        sums = jnp.concatenate([second_part[0], local_load])
        for axis in ("seq", "kv"):
            sums = sum_over(sums, axis)
        do_parts = behind(do_parts, (outer, sums))
        outer = over_chips(outer)
        dq, dkv = [], []
        for row in rows:
            dq_row, dkv_row = attend_back(
                row, meta, q_t[row], do_parts, o_t[row], lse[row], kv_all[row], starts3,
                cosine, sine, group, orders[row],
            )
            dq.append(dq_row)
            dkv.append(collect_seq(dkv_row, orders[row]))
        outer = total(behind(outer, dq[-1]))
        rows_left = outer.shape[0]
        outer = exchange(outer.reshape(kv_devices, rows_left // kv_devices, width))
        outer = total(behind(outer, dkv[-1]))
        dkv[-1] = behind(dkv[-1], outer)
        outer = exchange(copies(outer, kv_devices)).reshape(rows_left, width)
        d_parts, grad_inner_part = inner_grads(
            dq, dkv, gathered, cosine, sine, kv_devices, key_heads
        )
        half = inner_cols // 2
        paths = [seq_order(at, seq_devices) for at in range(2)]
        shares = [halve_seq(grad_inner_part[half * at :][:half], paths[at]) for at in range(2)]
        outer = copies(behind(outer, shares), chips)
        d_parts = behind(d_parts, outer).reshape(kv_devices, 2, inner_cols // 2, own)
        outer = over_chips(outer).reshape(-1, width)
        kv_index = lax.axis_index("kv")
        d_inner = [
            swap(lax.dynamic_index_in_dim(d_parts, kv_index ^ mask, 0, keepdims=False), "kv", mask)
            for mask in range(kv_devices)
        ]
        place = jnp.stack([core_index, kv_index]).astype(jnp.int32)
        d_tokens = token_grads(
            place, d_inner, w_inner_half, w_inner_other, x_rows, d_hidden, norm_first.reshape(1, width)
        )
        outer = behind(outer, d_tokens)
        other_outer = swap(outer, "seq", 1)
        shares = behind(shares, outer)
        grad_inner = jnp.concatenate(
            [double_seq(shares[at], paths[at]) for at in range(2)], axis=0
        ).astype(f32)
        first_part = jnp.sum(w_t.astype(f32) * grad_inner, axis=0)
        first_sum = sum_over(first_part, "kv") / norm_first
        half_devices = kv_devices // 2
        start = (expert_count // 2) * w_down.shape[1] + lax.rem(kv_index, half_devices) * query_cols
        pieces = [
            lax.dynamic_slice_in_dim(pair, start, query_cols, 0) for pair in (outer, other_outer)
        ]
        own_out = jnp.where(kv_index // half_devices == core_index, *pieces).astype(f32)
        return d_tokens, grad_inner, first_sum, outer, other_outer, own_out, sums

    operands = (d_heads, d_hidden, send_out, keep_out, second_part)
    shapes = jax.eval_shape(rest, *operands)
    d_tokens, grad_inner, first_sum, own_outer, other_outer, own_out, sums = lax.cond(
        positions[0, 0] >= 0,
        rest,
        lambda *ignored: jax.tree.map(lambda leaf: jnp.zeros(leaf.shape, leaf.dtype), shapes),
        *operands,
    )
    grad_gate, grad_up, grad_down = widen(core, grad_gate, grad_up, own_outer, other_outer)
    return (
        block_out.reshape(tokens.shape),
        d_tokens.reshape(tokens.shape),
        first_sum,
        grad_inner[:query_cols].T,
        grad_inner[query_cols : query_cols + key_cols].T,
        grad_inner[query_cols + key_cols :].T,
        own_out,
        sums[:width],
        grad_gate,
        grad_up,
        grad_down,
        sums[width:].astype(jnp.int32),
    )


def solution(mesh):
    in_specs = (
        P(None, ("seq", "kv"), None),
        P(None, ("seq", "kv"), None),
        P(),
        P(None, "kv"),
        P(None, "kv"),
        P(None, "kv"),
        P("kv", None),
        P(),
        P(),
        P(),
        P(),
        P(None, ("seq", "kv"), None),
        P(None, ("seq", "kv"), None),
        P(),
        P(None, "seq"),
    )
    out_specs = (
        P(None, ("seq", "kv"), None),
        P(None, ("seq", "kv"), None),
        P(),
        P(None, "kv"),
        P(None, "kv"),
        P(None, "kv"),
        P("kv", None),
        P(),
        P(),
        P(),
        P(),
        P(),
    )
    return jax.shard_map(
        per_device, mesh=mesh, in_specs=in_specs, out_specs=out_specs, check_vma=False
    )
```

```python
import functools

import jax
import jax.numpy as jnp
from jax import lax
from jax.experimental import pallas as pl
from jax.experimental.pallas import tpu as pltpu
from jax.sharding import PartitionSpec as P

DH = 64
HALF = DH // 2

epsilon = 1e-05
neg_big = -1e30
theta_base = 10000.0
highest = lax.Precision.HIGHEST
f32 = jnp.float32
bf16 = jnp.bfloat16

NN = (((1,), (0,)), ((), ()))
NT = (((1,), (1,)), ((), ()))


def mm(a, b, dims=NN):
    return lax.dot_general(a, b, dims, preferred_element_type=f32)


def seq_bits(axis_size):
    bits = []
    bit = 2
    while bit < axis_size:
        bits.append(bit)
        bit *= 2
    return bits


def seq_order(row, axis_size):
    bits = seq_bits(axis_size)
    return (bits if row % 2 == 0 else bits[::-1]) + [1]


def slot_of(mask, order):
    slot = 0
    for at, bit in enumerate(order):
        slot = slot + (((mask >> (bit.bit_length() - 1)) & 1) << at)
    return slot


def swap(value, axis, mask):
    if mask == 0:
        return value
    count = lax.axis_size(axis)
    return lax.ppermute(value, axis, [(source, source ^ mask) for source in range(count)])


def spread_seq(value, order, other):
    held = value[None]
    for bit in order:
        if bit == order[-1]:
            held = behind(held, other)
        held = jnp.concatenate([held, swap(held, "seq", bit)], axis=0)
    return held


def collect_seq(value, order):
    held = value
    for bit in order[::-1]:
        half = held.shape[0] // 2
        came = swap(held[half:], "seq", bit)
        held = (held[:half].astype(f32) + came.astype(f32)).astype(bf16)
    return held[0]


def halve_seq(value, order):
    index = lax.axis_index("seq")
    held = value
    for bit in order[::-1]:
        half = held.shape[0] // 2
        upper = (index & bit) != 0
        keep = jnp.where(upper, held[half:], held[:half])
        send = jnp.where(upper, held[:half], held[half:])
        held = (keep.astype(f32) + swap(send, "seq", bit).astype(f32)).astype(bf16)
    return held


def double_seq(value, order):
    index = lax.axis_index("seq")
    held = value
    for bit in order:
        upper = (index & bit) != 0
        came = swap(held, "seq", bit)
        held = jnp.where(
            upper,
            jnp.concatenate([came, held], axis=0),
            jnp.concatenate([held, came], axis=0),
        )
    return held


def behind(value, other):
    return value if other is None else lax.optimization_barrier((value, other))[0]


def cut(value, index, size):
    return lax.dynamic_slice_in_dim(value, index * size, size, 0)


def sum_over(value, axis):
    mask = 1
    while mask < lax.axis_size(axis):
        value = value + swap(value, axis, mask)
        mask *= 2
    return value


def added(first, second):
    return (first.astype(f32) + second.astype(f32)).astype(bf16)


def qkv_kernel(w_ref, n_ref, cos_ref, sin_ref, q_ref, kv_ref, *, query_heads, key_heads, scale):
    acc = mm(w_ref[...], n_ref[0], NT)
    cosine = cos_ref[0]
    sine = sin_ref[0]
    for head in range(query_heads):
        low = acc[DH * head : DH * head + HALF]
        high = acc[DH * head + HALF : DH * head + DH]
        q_ref[DH * head : DH * head + HALF, :] = ((low * cosine - high * sine) * scale).astype(bf16)
        q_ref[DH * head + HALF : DH * head + DH, :] = (
            (high * cosine + low * sine) * scale
        ).astype(bf16)
    base = DH * query_heads
    for head in range(key_heads):
        low = acc[base + DH * head : base + DH * head + HALF]
        high = acc[base + DH * head + HALF : base + DH * head + DH]
        at = 2 * DH * head
        kv_ref[at : at + HALF, :] = (low * cosine - high * sine).astype(bf16)
        kv_ref[at + HALF : at + DH, :] = (high * cosine + low * sine).astype(bf16)
        start = base + DH * (key_heads + head)
        kv_ref[at + DH : at + 2 * DH, :] = acc[start : start + DH].astype(bf16)


def project(row, w_t, gathered, cosine, sine, query_heads, key_heads):
    cols, width = w_t.shape
    count = gathered.shape[1]
    tile = 256
    q_cols = query_heads * DH
    kv_cols = 2 * key_heads * DH
    return pl.pallas_call(
        functools.partial(
            qkv_kernel, query_heads=query_heads, key_heads=key_heads, scale=DH ** (-0.5)
        ),
        grid=(count // tile,),
        in_specs=[
            pl.BlockSpec((cols, width), lambda i: (0, 0)),
            pl.BlockSpec((1, tile, width), lambda i: (row, i, 0)),
            pl.BlockSpec((1, HALF, tile), lambda i: (row, 0, i)),
            pl.BlockSpec((1, HALF, tile), lambda i: (row, 0, i)),
        ],
        out_specs=[
            pl.BlockSpec((q_cols, tile), lambda i: (0, i)),
            pl.BlockSpec((kv_cols, tile), lambda i: (0, i)),
        ],
        out_shape=[
            jax.ShapeDtypeStruct((q_cols, count), bf16),
            jax.ShapeDtypeStruct((kv_cols, count), bf16),
        ],
        compiler_params=pltpu.CompilerParams(vmem_limit_bytes=60 * 2**20),
        cost_estimate=pl.CostEstimate(
            flops=2 * cols * width * count, bytes_accessed=4 * count * width, transcendentals=0
        ),
    )(w_t, gathered, cosine, sine)


def forward_kernel(
    meta_ref, q_ref, kv_ref, start_ref, o_ref, low_ref, lse_ref, max_s, sum_s, acc_s,
    *, row, group, order
):
    span = q_ref.shape[1]
    here = meta_ref[0]
    first = meta_ref[1 + 2 * row]
    middle = meta_ref[2 + 2 * row]
    start = start_ref[0]
    key_iota = lax.broadcasted_iota(jnp.int32, (span, span), 0)

    def step(block, masked, diagonal):
        slot = 0 if diagonal else slot_of(block ^ here, order)
        k_t = kv_ref[slot, 0:DH, :]
        v_t = kv_ref[slot, DH : 2 * DH, :]
        keys = k_t.T
        if masked:
            keep = key_iota + block * span >= start
        if diagonal:
            keep = keep & (key_iota <= lax.broadcasted_iota(jnp.int32, (span, span), 1))
        for g in range(group):
            scores = mm(keys, q_ref[DH * g : DH * g + DH, :])
            if masked:
                scores = jnp.where(keep, scores, neg_big)
            top = jnp.max(scores, axis=0, keepdims=True)
            if diagonal:
                new_max = top
            else:
                old_max = max_s[g : g + 1, :]
                new_max = jnp.maximum(old_max, top)
            weights = jnp.exp(scores - new_max)
            total = jnp.sum(weights, axis=0, keepdims=True)
            mixed = mm(v_t, weights.astype(bf16))
            at = slice(DH * g, DH * g + DH)
            if diagonal:
                sum_s[g : g + 1, :] = total
                acc_s[at, :] = mixed
            else:
                factor = jnp.exp(old_max - new_max)
                sum_s[g : g + 1, :] = sum_s[g : g + 1, :] * factor + total
                acc_s[at, :] = acc_s[at, :] * factor + mixed
            max_s[g : g + 1, :] = new_max

    step(here, True, True)

    @pl.loop(first, middle)
    def _(block):
        step(block, True, False)

    @pl.loop(middle, here)
    def _(block):
        step(block, False, False)

    for g in range(group):
        at = slice(DH * g, DH * g + DH)
        total = sum_s[g : g + 1, :]
        out = acc_s[at, :] / total
        o_ref[at, :] = out
        low_ref[at, :] = out.astype(bf16)
        lse_ref[0, g : g + 1, :] = max_s[g : g + 1, :] + jnp.log(total)


def attend(row, meta, q_t, kv_all, starts, group, order):
    span = q_t.shape[1]
    blocks = kv_all.shape[0]
    key_heads = kv_all.shape[1] // (2 * DH)
    cols = group * DH
    head_spec = pl.BlockSpec((cols, span), lambda h, m: (h, 0))
    return pl.pallas_call(
        functools.partial(forward_kernel, row=row, group=group, order=order),
        grid_spec=pltpu.PrefetchScalarGridSpec(
            num_scalar_prefetch=1,
            grid=(key_heads,),
            in_specs=[
                head_spec,
                pl.BlockSpec((blocks, 2 * DH, span), lambda h, m: (0, h, 0)),
                pl.BlockSpec((1, 1, span), lambda h, m: (row, 0, 0)),
            ],
            out_specs=[
                head_spec,
                head_spec,
                pl.BlockSpec((1, group, span), lambda h, m: (h, 0, 0)),
            ],
            scratch_shapes=[
                pltpu.VMEM((group, span), f32),
                pltpu.VMEM((group, span), f32),
                pltpu.VMEM((cols, span), f32),
            ],
        ),
        out_shape=[
            jax.ShapeDtypeStruct((key_heads * cols, span), f32),
            jax.ShapeDtypeStruct((key_heads * cols, span), bf16),
            jax.ShapeDtypeStruct((key_heads, group, span), f32),
        ],
        compiler_params=pltpu.CompilerParams(vmem_limit_bytes=40 * 2**20),
        cost_estimate=pl.CostEstimate(
            flops=16 * blocks * span * span * cols,
            bytes_accessed=4 * kv_all.size,
            transcendentals=0,
        ),
    )(meta, q_t, kv_all, starts)


def backward_kernel(
    meta_ref, q_ref, do_ref, o_ref, lse_ref, kv_ref, start_ref, cos_ref, sin_ref,
    dq_ref, dkv_ref, dq_s, q_s, do_t_s, do_s, delta_s,
    *, row, group, order, scale
):
    span = q_ref.shape[1]
    here = meta_ref[0]
    first = meta_ref[1 + 2 * row]
    middle = meta_ref[2 + 2 * row]
    start = start_ref[0]
    key_iota = lax.broadcasted_iota(jnp.int32, (span, span), 0)
    dkv_ref[...] = jnp.zeros(dkv_ref.shape, bf16)
    part = do_ref.shape[3]
    for device in range(do_ref.shape[0]):
        do_t_s[:, part * device : part * (device + 1)] = do_ref[device, 0]
    for g in range(group):
        at = slice(DH * g, DH * g + DH)
        q_s[g] = q_ref[at, :].T
        do_s[g] = do_t_s[at, :].T
        delta_s[g : g + 1, :] = jnp.sum(
            do_t_s[at, :].astype(f32) * o_ref[at, :], axis=0, keepdims=True
        )

    def step(block, masked, diagonal):
        slot = 0 if diagonal else slot_of(block ^ here, order)
        k_t = kv_ref[slot, 0:DH, :]
        v_t = kv_ref[slot, DH : 2 * DH, :]
        keys = k_t.T
        values = v_t.T
        if masked:
            keep = key_iota + block * span >= start
        if diagonal:
            keep = keep & (key_iota <= lax.broadcasted_iota(jnp.int32, (span, span), 1))
        d_keys = None
        d_values = None
        for g in range(group):
            at = slice(DH * g, DH * g + DH)
            scores = mm(keys, q_ref[at, :])
            probs = jnp.exp(scores - lse_ref[0, g : g + 1, :])
            if masked:
                probs = jnp.where(keep, probs, 0.0)
            d_probs = mm(values, do_t_s[at, :])
            d_scores = (probs * (d_probs - delta_s[g : g + 1, :])).astype(bf16)
            dq = mm(k_t, d_scores)
            if diagonal:
                dq_s[at, :] = dq
            else:
                dq_s[at, :] += dq
            dv = mm(probs.astype(bf16), do_s[g])
            dk = mm(d_scores, q_s[g])
            d_keys = dk if d_keys is None else d_keys + dk
            d_values = dv if d_values is None else d_values + dv
        dkv_ref[slot, 0:DH, :] = d_keys.T.astype(bf16)
        dkv_ref[slot, DH : 2 * DH, :] = d_values.T.astype(bf16)

    step(here, True, True)

    @pl.loop(first, middle)
    def _(block):
        step(block, True, False)

    @pl.loop(middle, here)
    def _(block):
        step(block, False, False)

    cosine = cos_ref[0]
    sine = sin_ref[0]
    for g in range(group):
        low = dq_s[DH * g : DH * g + HALF, :] * scale
        high = dq_s[DH * g + HALF : DH * g + DH, :] * scale
        dq_ref[DH * g : DH * g + HALF, :] = (low * cosine + high * sine).astype(bf16)
        dq_ref[DH * g + HALF : DH * g + DH, :] = (high * cosine - low * sine).astype(bf16)


def attend_back(row, meta, q_t, do_parts, o_t, lse, kv_all, starts, cosine, sine, group, order):
    span = q_t.shape[1]
    blocks = kv_all.shape[0]
    key_heads = kv_all.shape[1] // (2 * DH)
    cols = group * DH
    kv_devices, _, _, part = do_parts.shape
    head_spec = pl.BlockSpec((cols, span), lambda h, m: (h, 0))
    kv_spec = pl.BlockSpec((blocks, 2 * DH, span), lambda h, m: (0, h, 0))
    angle_spec = pl.BlockSpec((1, HALF, span), lambda h, m: (row, 0, 0))
    return pl.pallas_call(
        functools.partial(
            backward_kernel, row=row, group=group, order=order, scale=DH ** (-0.5)
        ),
        grid_spec=pltpu.PrefetchScalarGridSpec(
            num_scalar_prefetch=1,
            grid=(key_heads,),
            in_specs=[
                head_spec,
                pl.BlockSpec((kv_devices, 1, cols, part), lambda h, m: (0, row, h, 0)),
                head_spec,
                pl.BlockSpec((1, group, span), lambda h, m: (h, 0, 0)),
                kv_spec,
                pl.BlockSpec((1, 1, span), lambda h, m: (row, 0, 0)),
                angle_spec,
                angle_spec,
            ],
            out_specs=[head_spec, kv_spec],
            scratch_shapes=[
                pltpu.VMEM((cols, span), f32),
                pltpu.VMEM((group, span, DH), bf16),
                pltpu.VMEM((cols, span), bf16),
                pltpu.VMEM((group, span, DH), bf16),
                pltpu.VMEM((group, span), f32),
            ],
        ),
        out_shape=[
            jax.ShapeDtypeStruct((key_heads * cols, span), bf16),
            jax.ShapeDtypeStruct(kv_all.shape, bf16),
        ],
        compiler_params=pltpu.CompilerParams(vmem_limit_bytes=40 * 2**20),
        cost_estimate=pl.CostEstimate(
            flops=40 * blocks * span * span * cols,
            bytes_accessed=4 * kv_all.size,
            transcendentals=0,
        ),
    )(meta, q_t, do_parts, o_t, lse, kv_all, starts, cosine, sine)


def experts_kernel(core_ref, *refs, experts):
    (
        heads_ref, x_ref, dy_ref, mix_ref, gain_ref, own_ref, other_ref, gate_ref, up_ref, down_ref
    ) = refs[:10]
    outs = refs[10:]
    row_count, part = heads_ref.shape[1], heads_ref.shape[3]
    out_ref, dh_ref, ggate_ref, gup_ref, send_out, keep_out, gain_grad_ref = outs[:7]
    d_heads_ref = outs[7]
    hid_s, hat_s, recip_s, norm_s, norm_t_s, acc_s, dn_s, w_out_s = outs[8:]
    expert = pl.program_id(0)
    width = x_ref.shape[1]

    @pl.when(expert == 0)
    def _():
        for device in range(own_ref.shape[0]):
            w_out_s[device, core_ref[0]] = own_ref[device]
            w_out_s[device, 1 - core_ref[0]] = other_ref[device]
        w_out = w_out_s[...].reshape(-1, width)
        for row in range(row_count):
            at = slice(part * row, part * (row + 1))
            branch = mm(heads_ref[:, row].reshape(-1, part).T, w_out)
            hidden = x_ref[at, :].astype(f32) + branch
            recip = lax.rsqrt(jnp.mean(hidden * hidden, axis=-1, keepdims=True) + epsilon)
            hat = hidden * recip
            hid_s[at, :] = hidden
            hat_s[at, :] = hat
            recip_s[at, :] = recip
            norm_s[at, :] = (hat * gain_ref[...]).astype(bf16)
        norm_t_s[...] = norm_s[...].T
        acc_s[...] = hid_s[...]
        dn_s[...] = jnp.zeros(dn_s.shape, f32)

    normed = norm_s[...]
    mix = mix_ref[0]
    gate_pre = mm(normed, gate_ref[0])
    up_pre = mm(normed, up_ref[0])
    gate_sig = 1.0 / (1.0 + jnp.exp(-gate_pre))
    gate_act = gate_pre * gate_sig
    hid = (gate_act * up_pre).astype(bf16)
    acc_s[...] += mix * mm(hid, down_ref[0])
    d_expert = (mix * dy_ref[...].astype(f32)).astype(bf16)
    d_hid = mm(d_expert, down_ref[0], NT)
    d_gate = (d_hid * up_pre * (gate_sig * (1.0 + gate_pre * (1.0 - gate_sig)))).astype(bf16)
    d_up = (d_hid * gate_act).astype(bf16)
    dn_s[...] += mm(d_gate, gate_ref[0], NT) + mm(d_up, up_ref[0], NT)
    grad_down = mm(hid.T, d_expert).astype(bf16)
    half = experts // 2

    @pl.when(expert < half)
    def _():
        send_out[expert] = grad_down

    @pl.when(expert >= half)
    def _():
        keep_out[expert - half] = grad_down

    ggate_ref[0] = mm(norm_t_s[...], d_gate).astype(bf16)
    gup_ref[0] = mm(norm_t_s[...], d_up).astype(bf16)

    @pl.when(expert == experts - 1)
    def _():
        out_ref[...] = acc_s[...].astype(bf16)
        hat = hat_s[...]
        d_norm = dn_s[...]
        w_out = w_out_s[...].reshape(-1, width)
        gain_grad_ref[...] = jnp.sum(d_norm * hat, axis=0, keepdims=True)
        d_hat = d_norm * gain_ref[...]
        mean = jnp.mean(d_hat * hat, axis=-1, keepdims=True)
        d_hidden = dy_ref[...].astype(f32) + recip_s[...] * (d_hat - hat * mean)
        dh_ref[...] = d_hidden
        d_branch = d_hidden.astype(bf16)
        grad_out = None
        for row in range(row_count):
            at = slice(part * row, part * (row + 1))
            piece = d_branch[at, :]
            d_heads_ref[:, row] = (
                mm(w_out, piece, NT).astype(bf16).reshape(d_heads_ref.shape[0], -1, part)
            )
            term = mm(heads_ref[:, row].reshape(-1, part), piece)
            grad_out = term if grad_out is None else grad_out + term
        grad_out = grad_out.astype(bf16)
        part_rows = grad_out.shape[0] // (2 * (send_out.shape[0] - half))

        @pl.when(core_ref[0] == 0)
        def _():
            for at in range(send_out.shape[0] - half):
                keep_out[half + at] = grad_out[part_rows * at : part_rows * (at + 1)]
                start = grad_out.shape[0] // 2 + part_rows * at
                send_out[half + at] = grad_out[start : start + part_rows]

        @pl.when(core_ref[0] != 0)
        def _():
            for at in range(send_out.shape[0] - half):
                send_out[half + at] = grad_out[part_rows * at : part_rows * (at + 1)]
                start = grad_out.shape[0] // 2 + part_rows * at
                keep_out[half + at] = grad_out[start : start + part_rows]


def run_experts(
    core, heads, x_rows, dy_rows, mix, gain, w_out_half, w_out_other, w_gate, w_up, w_down
):
    own, width = x_rows.shape
    experts, _, hidden = w_gate.shape
    kv_devices, row_count, _, part = heads.shape
    half_rows = w_out_half.shape[1]
    head_cols = 2 * kv_devices * half_rows

    def whole(shape):
        return pl.BlockSpec(shape, lambda e, m: (0,) * len(shape))

    half = experts // 2

    def which(e, m):
        return lax.rem(e + (1 - m[0]) * half, experts)

    gate_spec = pl.BlockSpec((1, width, hidden), lambda e, m: (which(e, m), 0, 0))
    down_spec = pl.BlockSpec((1, hidden, width), lambda e, m: (which(e, m), 0, 0))
    outer = (half + head_cols // (2 * hidden), hidden, width)
    return pl.pallas_call(
        functools.partial(experts_kernel, experts=experts),
        grid_spec=pltpu.PrefetchScalarGridSpec(
            num_scalar_prefetch=1,
            grid=(experts,),
            in_specs=[
                whole(heads.shape),
                whole((own, width)),
                whole((own, width)),
                pl.BlockSpec((1, own, 1), lambda e, m: (which(e, m), 0, 0)),
                whole((1, width)),
                whole(w_out_half.shape),
                whole(w_out_half.shape),
                gate_spec,
                gate_spec,
                down_spec,
            ],
            out_specs=[
                whole((own, width)),
                whole((own, width)),
                gate_spec,
                gate_spec,
                whole(outer),
                whole(outer),
                whole((1, width)),
                whole(heads.shape),
            ],
            scratch_shapes=[
                pltpu.VMEM((own, width), f32),
                pltpu.VMEM((own, width), f32),
                pltpu.VMEM((own, 1), f32),
                pltpu.VMEM((own, width), bf16),
                pltpu.VMEM((width, own), bf16),
                pltpu.VMEM((own, width), f32),
                pltpu.VMEM((own, width), f32),
                pltpu.VMEM((kv_devices, 2, half_rows, width), bf16),
            ],
        ),
        out_shape=[
            jax.ShapeDtypeStruct((own, width), bf16),
            jax.ShapeDtypeStruct((own, width), f32),
            jax.ShapeDtypeStruct(w_gate.shape, bf16),
            jax.ShapeDtypeStruct(w_up.shape, bf16),
            jax.ShapeDtypeStruct(outer, bf16),
            jax.ShapeDtypeStruct(outer, bf16),
            jax.ShapeDtypeStruct((1, width), f32),
            jax.ShapeDtypeStruct(heads.shape, bf16),
        ],
        compiler_params=pltpu.CompilerParams(vmem_limit_bytes=56 * 2**20),
        cost_estimate=pl.CostEstimate(
            flops=18 * own * width * hidden * experts,
            bytes_accessed=6 * w_gate.size * 2,
            transcendentals=0,
        ),
    )(
        core, heads, x_rows, dy_rows, mix, gain, w_out_half, w_out_other,
        w_gate, w_up, w_down,
    )


def inner_kernel(*refs, row_count, query_cols, key_heads):
    dq = refs[:row_count]
    dkv = refs[row_count : 2 * row_count]
    n_ref, cos_ref, sin_ref, parts_ref, grad_ref, inner_s = refs[2 * row_count :]
    kv_devices = parts_ref.shape[0]
    part = parts_ref.shape[2] // row_count
    grad = None
    for row in range(row_count):
        cosine = cos_ref[row]
        sine = sin_ref[row]
        inner_s[0:query_cols, :] = dq[row][...]
        for head in range(key_heads):
            at = 2 * DH * head
            low = dkv[row][at : at + HALF, :].astype(f32)
            high = dkv[row][at + HALF : at + DH, :].astype(f32)
            to = query_cols + DH * head
            inner_s[to : to + HALF, :] = (low * cosine + high * sine).astype(bf16)
            inner_s[to + HALF : to + DH, :] = (high * cosine - low * sine).astype(bf16)
            to = query_cols + DH * (key_heads + head)
            inner_s[to : to + DH, :] = dkv[row][at + DH : at + 2 * DH, :]
        for device in range(kv_devices):
            parts_ref[device, :, part * row : part * (row + 1)] = inner_s[
                :, part * device : part * (device + 1)
            ]
        term = mm(inner_s[...], n_ref[row])
        grad = term if grad is None else grad + term
    grad_ref[...] = grad.astype(bf16)


def inner_grads(dq, dkv, gathered, cosine, sine, kv_devices, key_heads):
    row_count = len(dq)
    query_cols, span = dq[0].shape
    cols, width = query_cols + dkv[0].shape[0], gathered.shape[2]
    own = row_count * span // kv_devices
    return pl.pallas_call(
        functools.partial(
            inner_kernel, row_count=row_count, query_cols=query_cols, key_heads=key_heads
        ),
        out_shape=[
            jax.ShapeDtypeStruct((kv_devices, cols, own), bf16),
            jax.ShapeDtypeStruct((cols, width), bf16),
        ],
        scratch_shapes=[pltpu.VMEM((cols, span), bf16)],
        compiler_params=pltpu.CompilerParams(vmem_limit_bytes=40 * 2**20),
        cost_estimate=pl.CostEstimate(
            flops=2 * row_count * span * cols * width,
            bytes_accessed=4 * gathered.size,
            transcendentals=0,
        ),
    )(*dq, *dkv, gathered, cosine, sine)


def tokens_kernel(place_ref, *refs):
    own_ref, other_ref, x_ref, dh_ref, gain_ref, out_ref = refs[-6:]
    x_float = x_ref[...].astype(f32)
    recip = lax.rsqrt(jnp.mean(x_float * x_float, axis=-1, keepdims=True) + epsilon)
    x_hat = x_float * recip
    core = place_ref[0]
    d_normed = None
    for mask, piece in enumerate(refs[:-6]):
        device = place_ref[1] ^ mask
        term = mm(piece[core].T, own_ref[device])
        term += mm(piece[1 - core].T, other_ref[device])
        d_normed = term if d_normed is None else d_normed + term
    d_hat = d_normed * gain_ref[...]
    mean = jnp.mean(d_hat * x_hat, axis=-1, keepdims=True)
    out_ref[...] = (dh_ref[...] + recip * (d_hat - x_hat * mean)).astype(bf16)


def token_grads(place, d_inner, w_half, w_other, x_rows, d_hidden, gain):
    own, width = x_rows.shape
    return pl.pallas_call(
        tokens_kernel,
        in_specs=[pl.BlockSpec(memory_space=pltpu.SMEM)]
        + [pl.BlockSpec(memory_space=pltpu.VMEM)] * (5 + len(d_inner)),
        out_shape=jax.ShapeDtypeStruct((own, width), bf16),
        compiler_params=pltpu.CompilerParams(vmem_limit_bytes=40 * 2**20),
        cost_estimate=pl.CostEstimate(
            flops=4 * w_half.size * own, bytes_accessed=4 * w_half.size, transcendentals=0
        ),
    )(place, *d_inner, w_half, w_other, x_rows, d_hidden, gain)


def widen_whole_kernel(gate_ref, up_ref, ggate_ref, gup_ref):
    ggate_ref[...] = gate_ref[...].astype(f32)
    gup_ref[...] = up_ref[...].astype(f32)


def widen_whole(grad_gate, grad_up):
    experts, width, hidden = grad_gate.shape
    spec = pl.BlockSpec((1, width, hidden), lambda e: (e, 0, 0))
    return pl.pallas_call(
        widen_whole_kernel,
        grid=(experts,),
        in_specs=[spec, spec],
        out_specs=[spec, spec],
        out_shape=[jax.ShapeDtypeStruct(grad_gate.shape, f32)] * 2,
        compiler_params=pltpu.CompilerParams(vmem_limit_bytes=60 * 2**20),
        cost_estimate=pl.CostEstimate(
            flops=0, bytes_accessed=12 * grad_gate.size, transcendentals=0
        ),
    )(grad_gate, grad_up)


def widen_halves_kernel(core_ref, own_ref, other_ref, gdown_ref, *, half):
    @pl.when(pl.program_id(0) < half)
    def _():
        gdown_ref[0] = own_ref[...].astype(f32)

    @pl.when(pl.program_id(0) >= half)
    def _():
        gdown_ref[0] = other_ref[...].astype(f32)


def widen_halves(core, own_rows, other_rows, experts, hidden):
    width = own_rows.shape[1]
    half = experts // 2
    return pl.pallas_call(
        functools.partial(widen_halves_kernel, half=half),
        grid_spec=pltpu.PrefetchScalarGridSpec(
            num_scalar_prefetch=1,
            grid=(experts,),
            in_specs=[
                pl.BlockSpec((hidden, width), lambda e, m: (jnp.minimum(e, half - 1), 0)),
                pl.BlockSpec((hidden, width), lambda e, m: (jnp.maximum(e - half, 0), 0)),
            ],
            out_specs=pl.BlockSpec(
                (1, hidden, width), lambda e, m: (lax.rem(e + m[0] * half, experts), 0, 0)
            ),
        ),
        out_shape=jax.ShapeDtypeStruct((experts, hidden, width), f32),
        compiler_params=pltpu.CompilerParams(vmem_limit_bytes=60 * 2**20),
        cost_estimate=pl.CostEstimate(
            flops=0, bytes_accessed=6 * experts * hidden * width, transcendentals=0
        ),
    )(core, own_rows, other_rows)


def per_device(
    tokens,
    cotangent,
    norm_first,
    w_query,
    w_key,
    w_value,
    w_out,
    norm_second,
    w_gate,
    w_up,
    w_down,
    routes,
    gate_weights,
    segment_ids,
    positions,
):
    row_count, block_len, width = tokens.shape
    kv_devices = lax.axis_size("kv")
    seq_devices = lax.axis_size("seq")
    seq_len = block_len * kv_devices
    seq_index = lax.axis_index("seq")
    query_cols = w_query.shape[1]
    key_cols = w_key.shape[1]
    query_heads = query_cols // DH
    key_heads = key_cols // DH
    group = query_heads // key_heads
    expert_count = w_gate.shape[0]
    own = row_count * block_len
    rows = range(row_count)
    orders = [seq_order(row, seq_devices) for row in rows]

    place = seq_index * seq_len + jnp.arange(seq_len, dtype=jnp.int32)
    starts = place[None, :] - positions
    first_block = starts[:, 0] // seq_len
    middle_block = jnp.clip((starts[:, -1] + seq_len - 1) // seq_len, first_block, seq_index)
    bounds = jnp.stack([first_block, middle_block], axis=1).reshape(-1)
    meta = jnp.concatenate([seq_index[None], bounds]).astype(jnp.int32)
    starts3 = starts.reshape(row_count, 1, seq_len)
    freqs = theta_base ** (-(jnp.arange(HALF, dtype=f32) * 2.0) / DH)
    angles = freqs[None, :, None] * positions.astype(f32)[:, None, :]
    cosine = jnp.cos(angles)
    sine = jnp.sin(angles)

    x_float = tokens.astype(f32)
    recip_first = lax.rsqrt(jnp.mean(x_float * x_float, axis=-1, keepdims=True) + epsilon)
    normed = (x_float * recip_first * norm_first).astype(bf16)
    gathered = lax.all_gather(normed, "kv", axis=1, tiled=True)

    w_t = jnp.concatenate([w_query.T, w_key.T, w_value.T], axis=0)
    inner_cols = w_t.shape[0]
    expert_ids = jnp.arange(expert_count, dtype=jnp.int32)
    picks = routes[..., None] == expert_ids
    local_load = jnp.sum(picks.astype(f32), axis=(0, 1, 2))
    core_index = seq_index % 2
    half_rows = query_cols // 2
    w_out_half = lax.all_gather(cut(w_out, core_index, half_rows), "kv")
    w_out_other = swap(w_out_half, "seq", 1)
    w_inner_half = lax.all_gather(cut(w_t, core_index, inner_cols // 2), "kv")
    w_inner_other = swap(w_inner_half, "seq", 1)

    def exchange(value):
        return lax.all_to_all(value, "kv", 0, 0)

    q_t, kv_all, o_t, lse, heads = [], [], [], [], []
    kv_t = []
    for row in rows:
        q_row, kv_row = project(row, w_t, gathered, cosine, sine, query_heads, key_heads)
        q_t.append(q_row)
        kv_t.append(kv_row)
    kv_t = lax.optimization_barrier(kv_t)
    kv_all = [spread_seq(kv_t[row], orders[row], None) for row in rows]
    kv_all = lax.optimization_barrier(kv_all)
    for row in rows:
        o_row, low_row, lse_row = attend(
            row, meta, q_t[row], kv_all[row], starts3, group, orders[row]
        )
        o_t.append(o_row)
        lse.append(lse_row)
        heads.append(low_row.reshape(query_cols, kv_devices, block_len).transpose(1, 0, 2))
    heads = exchange(jnp.stack(heads, axis=1))

    mix = jnp.sum(picks.astype(f32) * gate_weights[..., None], axis=2)
    mix = mix.reshape(own, expert_count).T[:, :, None]
    x_rows = tokens.reshape(own, width)
    core = core_index.astype(jnp.int32)[None]
    outs = run_experts(
        core,
        heads,
        x_rows,
        cotangent.reshape(own, width),
        mix,
        norm_second.reshape(1, width),
        w_out_half,
        w_out_other,
        w_gate,
        w_up,
        w_down,
    )
    block_out, d_hidden, grad_gate, grad_up, send_out, keep_out, second_part = outs[:7]
    d_heads = outs[7]
    grad_gate, grad_up = lax.psum((grad_gate, grad_up), ("seq", "kv"))

    chips = seq_devices // 2
    groups = [[2 * chip + one for chip in range(chips)] for one in range(2)]

    def over_chips(value):
        return lax.all_to_all(value, "seq", 0, 0, axis_index_groups=groups)

    def total(value):
        return jnp.sum(value.astype(f32), axis=0).astype(bf16)

    def copies(value, number):
        return jnp.broadcast_to(value[None], (number,) + value.shape)

    def rest(d_heads, d_hidden, send_out, keep_out, second_part):
        do_parts = exchange(d_heads)
        outer = added(keep_out, swap(send_out, "seq", 1)).reshape(chips, -1, width)
        sums = jnp.concatenate([second_part[0], local_load])
        for axis in ("seq", "kv"):
            sums = sum_over(sums, axis)
        do_parts = behind(do_parts, (outer, sums))
        outer = over_chips(outer)
        dq, dkv = [], []
        for row in rows:
            dq_row, dkv_row = attend_back(
                row, meta, q_t[row], do_parts, o_t[row], lse[row], kv_all[row], starts3,
                cosine, sine, group, orders[row],
            )
            dq.append(dq_row)
            dkv.append(collect_seq(dkv_row, orders[row]))
        outer = total(behind(outer, dq[-1]))
        rows_left = outer.shape[0]
        outer = exchange(outer.reshape(kv_devices, rows_left // kv_devices, width))
        outer = total(behind(outer, dkv[-1]))
        dkv[-1] = behind(dkv[-1], outer)
        outer = exchange(copies(outer, kv_devices)).reshape(rows_left, width)
        d_parts, grad_inner_part = inner_grads(
            dq, dkv, gathered, cosine, sine, kv_devices, key_heads
        )
        half = inner_cols // 2
        paths = [seq_order(at, seq_devices) for at in range(2)]
        shares = [halve_seq(grad_inner_part[half * at :][:half], paths[at]) for at in range(2)]
        outer = copies(behind(outer, shares), chips)
        d_parts = behind(d_parts, outer).reshape(kv_devices, 2, inner_cols // 2, own)
        outer = over_chips(outer).reshape(-1, width)
        kv_index = lax.axis_index("kv")
        d_inner = [
            swap(lax.dynamic_index_in_dim(d_parts, kv_index ^ mask, 0, keepdims=False), "kv", mask)
            for mask in range(kv_devices)
        ]
        place = jnp.stack([core_index, kv_index]).astype(jnp.int32)
        d_tokens = token_grads(
            place, d_inner, w_inner_half, w_inner_other, x_rows, d_hidden, norm_first.reshape(1, width)
        )
        outer = behind(outer, d_tokens)
        return d_tokens, outer, behind(shares, outer), sums

    operands = (d_heads, d_hidden, send_out, keep_out, second_part)
    shapes = jax.eval_shape(rest, *operands)
    d_tokens, outer, shares, sums = lax.cond(
        positions[0, 0] >= 0,
        rest,
        lambda *ignored: jax.tree.map(lambda leaf: jnp.zeros(leaf.shape, leaf.dtype), shapes),
        *operands,
    )
    kv_index = lax.axis_index("kv")
    paths = [seq_order(at, seq_devices) for at in range(2)]
    other_outer = swap(outer, "seq", 1)
    grad_inner = jnp.concatenate(
        [double_seq(shares[at], paths[at]) for at in range(2)], axis=0
    ).astype(f32)
    first_part = jnp.sum(w_t.astype(f32) * grad_inner, axis=0)
    first_sum = sum_over(first_part, "kv") / norm_first
    half_devices = kv_devices // 2
    start = (expert_count // 2) * w_down.shape[1] + lax.rem(kv_index, half_devices) * query_cols
    pieces = [
        lax.dynamic_slice_in_dim(pair, start, query_cols, 0) for pair in (outer, other_outer)
    ]
    own_out = jnp.where(kv_index // half_devices == core_index, *pieces).astype(f32)
    grad_gate, grad_up = widen_whole(grad_gate, grad_up)
    grad_down = widen_halves(core, outer, other_outer, expert_count, w_down.shape[1])
    return (
        block_out.reshape(tokens.shape),
        d_tokens.reshape(tokens.shape),
        first_sum,
        grad_inner[:query_cols].T,
        grad_inner[query_cols : query_cols + key_cols].T,
        grad_inner[query_cols + key_cols :].T,
        own_out,
        sums[:width],
        grad_gate,
        grad_up,
        grad_down,
        sums[width:].astype(jnp.int32),
    )


def solution(mesh):
    in_specs = (
        P(None, ("seq", "kv"), None),
        P(None, ("seq", "kv"), None),
        P(),
        P(None, "kv"),
        P(None, "kv"),
        P(None, "kv"),
        P("kv", None),
        P(),
        P(),
        P(),
        P(),
        P(None, ("seq", "kv"), None),
        P(None, ("seq", "kv"), None),
        P(),
        P(None, "seq"),
    )
    out_specs = (
        P(None, ("seq", "kv"), None),
        P(None, ("seq", "kv"), None),
        P(),
        P(None, "kv"),
        P(None, "kv"),
        P(None, "kv"),
        P("kv", None),
        P(),
        P(),
        P(),
        P(),
        P(),
    )
    return jax.shard_map(
        per_device, mesh=mesh, in_specs=in_specs, out_specs=out_specs, check_vma=False
    )
```

```python
import functools

import jax
import jax.numpy as jnp
from jax import lax
from jax.experimental import pallas as pl
from jax.experimental.pallas import tpu as pltpu
from jax.sharding import PartitionSpec as P

DH = 64
HALF = DH // 2

epsilon = 1e-05
neg_big = -1e30
theta_base = 10000.0
highest = lax.Precision.HIGHEST
f32 = jnp.float32
bf16 = jnp.bfloat16

NN = (((1,), (0,)), ((), ()))
NT = (((1,), (1,)), ((), ()))


def mm(a, b, dims=NN):
    return lax.dot_general(a, b, dims, preferred_element_type=f32)


def seq_bits(axis_size):
    bits = []
    bit = 2
    while bit < axis_size:
        bits.append(bit)
        bit *= 2
    return bits


def seq_order(row, axis_size):
    bits = seq_bits(axis_size)
    return (bits if row % 2 == 0 else bits[::-1]) + [1]


def slot_of(mask, order):
    slot = 0
    for at, bit in enumerate(order):
        slot = slot + (((mask >> (bit.bit_length() - 1)) & 1) << at)
    return slot


def swap(value, axis, mask):
    if mask == 0:
        return value
    count = lax.axis_size(axis)
    return lax.ppermute(value, axis, [(source, source ^ mask) for source in range(count)])


def spread_seq(value, order, other):
    held = value[None]
    for bit in order:
        if bit == order[-1]:
            held = behind(held, other)
        held = jnp.concatenate([held, swap(held, "seq", bit)], axis=0)
    return held


def collect_seq(value, order):
    held = value
    for bit in order[::-1]:
        half = held.shape[0] // 2
        came = swap(held[half:], "seq", bit)
        held = (held[:half].astype(f32) + came.astype(f32)).astype(bf16)
    return held[0]


def halve_seq(value, order):
    index = lax.axis_index("seq")
    held = value
    for bit in order[::-1]:
        half = held.shape[0] // 2
        upper = (index & bit) != 0
        keep = jnp.where(upper, held[half:], held[:half])
        send = jnp.where(upper, held[:half], held[half:])
        held = (keep.astype(f32) + swap(send, "seq", bit).astype(f32)).astype(bf16)
    return held


def double_seq(value, order):
    index = lax.axis_index("seq")
    held = value
    for bit in order:
        upper = (index & bit) != 0
        came = swap(held, "seq", bit)
        held = jnp.where(
            upper,
            jnp.concatenate([came, held], axis=0),
            jnp.concatenate([held, came], axis=0),
        )
    return held


def behind(value, other):
    return value if other is None else lax.optimization_barrier((value, other))[0]


def cut(value, index, size):
    return lax.dynamic_slice_in_dim(value, index * size, size, 0)


def sum_over(value, axis):
    mask = 1
    while mask < lax.axis_size(axis):
        value = value + swap(value, axis, mask)
        mask *= 2
    return value


def added(first, second):
    return (first.astype(f32) + second.astype(f32)).astype(bf16)


def qkv_kernel(w_ref, n_ref, cos_ref, sin_ref, q_ref, kv_ref, *, query_heads, key_heads, scale):
    acc = mm(w_ref[...], n_ref[0], NT)
    cosine = cos_ref[0]
    sine = sin_ref[0]
    for head in range(query_heads):
        low = acc[DH * head : DH * head + HALF]
        high = acc[DH * head + HALF : DH * head + DH]
        q_ref[DH * head : DH * head + HALF, :] = ((low * cosine - high * sine) * scale).astype(bf16)
        q_ref[DH * head + HALF : DH * head + DH, :] = (
            (high * cosine + low * sine) * scale
        ).astype(bf16)
    base = DH * query_heads
    for head in range(key_heads):
        low = acc[base + DH * head : base + DH * head + HALF]
        high = acc[base + DH * head + HALF : base + DH * head + DH]
        at = 2 * DH * head
        kv_ref[at : at + HALF, :] = (low * cosine - high * sine).astype(bf16)
        kv_ref[at + HALF : at + DH, :] = (high * cosine + low * sine).astype(bf16)
        start = base + DH * (key_heads + head)
        kv_ref[at + DH : at + 2 * DH, :] = acc[start : start + DH].astype(bf16)


def project(row, w_t, gathered, cosine, sine, query_heads, key_heads):
    cols, width = w_t.shape
    count = gathered.shape[1]
    tile = 256
    q_cols = query_heads * DH
    kv_cols = 2 * key_heads * DH
    return pl.pallas_call(
        functools.partial(
            qkv_kernel, query_heads=query_heads, key_heads=key_heads, scale=DH ** (-0.5)
        ),
        grid=(count // tile,),
        in_specs=[
            pl.BlockSpec((cols, width), lambda i: (0, 0)),
            pl.BlockSpec((1, tile, width), lambda i: (row, i, 0)),
            pl.BlockSpec((1, HALF, tile), lambda i: (row, 0, i)),
            pl.BlockSpec((1, HALF, tile), lambda i: (row, 0, i)),
        ],
        out_specs=[
            pl.BlockSpec((q_cols, tile), lambda i: (0, i)),
            pl.BlockSpec((kv_cols, tile), lambda i: (0, i)),
        ],
        out_shape=[
            jax.ShapeDtypeStruct((q_cols, count), bf16),
            jax.ShapeDtypeStruct((kv_cols, count), bf16),
        ],
        compiler_params=pltpu.CompilerParams(vmem_limit_bytes=60 * 2**20),
        cost_estimate=pl.CostEstimate(
            flops=2 * cols * width * count, bytes_accessed=4 * count * width, transcendentals=0
        ),
    )(w_t, gathered, cosine, sine)


def forward_kernel(
    meta_ref, q_ref, kv_ref, start_ref, o_ref, low_ref, lse_ref, max_s, sum_s, acc_s,
    *, row, group, order
):
    span = q_ref.shape[1]
    here = meta_ref[0]
    first = meta_ref[1 + 2 * row]
    middle = meta_ref[2 + 2 * row]
    start = start_ref[0]
    key_iota = lax.broadcasted_iota(jnp.int32, (span, span), 0)

    def step(block, masked, diagonal):
        slot = 0 if diagonal else slot_of(block ^ here, order)
        k_t = kv_ref[slot, 0:DH, :]
        v_t = kv_ref[slot, DH : 2 * DH, :]
        keys = k_t.T
        if masked:
            keep = key_iota + block * span >= start
        if diagonal:
            keep = keep & (key_iota <= lax.broadcasted_iota(jnp.int32, (span, span), 1))
        for g in range(group):
            scores = mm(keys, q_ref[DH * g : DH * g + DH, :])
            if masked:
                scores = jnp.where(keep, scores, neg_big)
            top = jnp.max(scores, axis=0, keepdims=True)
            if diagonal:
                new_max = top
            else:
                old_max = max_s[g : g + 1, :]
                new_max = jnp.maximum(old_max, top)
            weights = jnp.exp(scores - new_max)
            total = jnp.sum(weights, axis=0, keepdims=True)
            mixed = mm(v_t, weights.astype(bf16))
            at = slice(DH * g, DH * g + DH)
            if diagonal:
                sum_s[g : g + 1, :] = total
                acc_s[at, :] = mixed
            else:
                factor = jnp.exp(old_max - new_max)
                sum_s[g : g + 1, :] = sum_s[g : g + 1, :] * factor + total
                acc_s[at, :] = acc_s[at, :] * factor + mixed
            max_s[g : g + 1, :] = new_max

    step(here, True, True)

    @pl.loop(first, middle)
    def _(block):
        step(block, True, False)

    @pl.loop(middle, here)
    def _(block):
        step(block, False, False)

    for g in range(group):
        at = slice(DH * g, DH * g + DH)
        total = sum_s[g : g + 1, :]
        out = acc_s[at, :] / total
        o_ref[at, :] = out
        low_ref[at, :] = out.astype(bf16)
        lse_ref[0, g : g + 1, :] = max_s[g : g + 1, :] + jnp.log(total)


def attend(row, meta, q_t, kv_all, starts, group, order):
    span = q_t.shape[1]
    blocks = kv_all.shape[0]
    key_heads = kv_all.shape[1] // (2 * DH)
    cols = group * DH
    head_spec = pl.BlockSpec((cols, span), lambda h, m: (h, 0))
    return pl.pallas_call(
        functools.partial(forward_kernel, row=row, group=group, order=order),
        grid_spec=pltpu.PrefetchScalarGridSpec(
            num_scalar_prefetch=1,
            grid=(key_heads,),
            in_specs=[
                head_spec,
                pl.BlockSpec((blocks, 2 * DH, span), lambda h, m: (0, h, 0)),
                pl.BlockSpec((1, 1, span), lambda h, m: (row, 0, 0)),
            ],
            out_specs=[
                head_spec,
                head_spec,
                pl.BlockSpec((1, group, span), lambda h, m: (h, 0, 0)),
            ],
            scratch_shapes=[
                pltpu.VMEM((group, span), f32),
                pltpu.VMEM((group, span), f32),
                pltpu.VMEM((cols, span), f32),
            ],
        ),
        out_shape=[
            jax.ShapeDtypeStruct((key_heads * cols, span), f32),
            jax.ShapeDtypeStruct((key_heads * cols, span), bf16),
            jax.ShapeDtypeStruct((key_heads, group, span), f32),
        ],
        compiler_params=pltpu.CompilerParams(vmem_limit_bytes=40 * 2**20),
        cost_estimate=pl.CostEstimate(
            flops=16 * blocks * span * span * cols,
            bytes_accessed=4 * kv_all.size,
            transcendentals=0,
        ),
    )(meta, q_t, kv_all, starts)


def backward_kernel(
    meta_ref, q_ref, do_ref, o_ref, lse_ref, kv_ref, start_ref, cos_ref, sin_ref,
    dq_ref, dkv_ref, dq_s, q_s, do_t_s, do_s, delta_s,
    *, row, group, order, scale
):
    span = q_ref.shape[1]
    here = meta_ref[0]
    first = meta_ref[1 + 2 * row]
    middle = meta_ref[2 + 2 * row]
    start = start_ref[0]
    key_iota = lax.broadcasted_iota(jnp.int32, (span, span), 0)
    dkv_ref[...] = jnp.zeros(dkv_ref.shape, bf16)
    part = do_ref.shape[3]
    for device in range(do_ref.shape[0]):
        do_t_s[:, part * device : part * (device + 1)] = do_ref[device, 0]
    for g in range(group):
        at = slice(DH * g, DH * g + DH)
        q_s[g] = q_ref[at, :].T
        do_s[g] = do_t_s[at, :].T
        delta_s[g : g + 1, :] = jnp.sum(
            do_t_s[at, :].astype(f32) * o_ref[at, :], axis=0, keepdims=True
        )

    def step(block, masked, diagonal):
        slot = 0 if diagonal else slot_of(block ^ here, order)
        k_t = kv_ref[slot, 0:DH, :]
        v_t = kv_ref[slot, DH : 2 * DH, :]
        keys = k_t.T
        values = v_t.T
        if masked:
            keep = key_iota + block * span >= start
        if diagonal:
            keep = keep & (key_iota <= lax.broadcasted_iota(jnp.int32, (span, span), 1))
        d_keys = None
        d_values = None
        for g in range(group):
            at = slice(DH * g, DH * g + DH)
            scores = mm(keys, q_ref[at, :])
            probs = jnp.exp(scores - lse_ref[0, g : g + 1, :])
            if masked:
                probs = jnp.where(keep, probs, 0.0)
            d_probs = mm(values, do_t_s[at, :])
            d_scores = (probs * (d_probs - delta_s[g : g + 1, :])).astype(bf16)
            dq = mm(k_t, d_scores)
            if diagonal:
                dq_s[at, :] = dq
            else:
                dq_s[at, :] += dq
            dv = mm(probs.astype(bf16), do_s[g])
            dk = mm(d_scores, q_s[g])
            d_keys = dk if d_keys is None else d_keys + dk
            d_values = dv if d_values is None else d_values + dv
        dkv_ref[slot, 0:DH, :] = d_keys.T.astype(bf16)
        dkv_ref[slot, DH : 2 * DH, :] = d_values.T.astype(bf16)

    step(here, True, True)

    @pl.loop(first, middle)
    def _(block):
        step(block, True, False)

    @pl.loop(middle, here)
    def _(block):
        step(block, False, False)

    cosine = cos_ref[0]
    sine = sin_ref[0]
    for g in range(group):
        low = dq_s[DH * g : DH * g + HALF, :] * scale
        high = dq_s[DH * g + HALF : DH * g + DH, :] * scale
        dq_ref[DH * g : DH * g + HALF, :] = (low * cosine + high * sine).astype(bf16)
        dq_ref[DH * g + HALF : DH * g + DH, :] = (high * cosine - low * sine).astype(bf16)


def attend_back(row, meta, q_t, do_parts, o_t, lse, kv_all, starts, cosine, sine, group, order):
    span = q_t.shape[1]
    blocks = kv_all.shape[0]
    key_heads = kv_all.shape[1] // (2 * DH)
    cols = group * DH
    kv_devices, _, _, part = do_parts.shape
    head_spec = pl.BlockSpec((cols, span), lambda h, m: (h, 0))
    kv_spec = pl.BlockSpec((blocks, 2 * DH, span), lambda h, m: (0, h, 0))
    angle_spec = pl.BlockSpec((1, HALF, span), lambda h, m: (row, 0, 0))
    return pl.pallas_call(
        functools.partial(
            backward_kernel, row=row, group=group, order=order, scale=DH ** (-0.5)
        ),
        grid_spec=pltpu.PrefetchScalarGridSpec(
            num_scalar_prefetch=1,
            grid=(key_heads,),
            in_specs=[
                head_spec,
                pl.BlockSpec((kv_devices, 1, cols, part), lambda h, m: (0, row, h, 0)),
                head_spec,
                pl.BlockSpec((1, group, span), lambda h, m: (h, 0, 0)),
                kv_spec,
                pl.BlockSpec((1, 1, span), lambda h, m: (row, 0, 0)),
                angle_spec,
                angle_spec,
            ],
            out_specs=[head_spec, kv_spec],
            scratch_shapes=[
                pltpu.VMEM((cols, span), f32),
                pltpu.VMEM((group, span, DH), bf16),
                pltpu.VMEM((cols, span), bf16),
                pltpu.VMEM((group, span, DH), bf16),
                pltpu.VMEM((group, span), f32),
            ],
        ),
        out_shape=[
            jax.ShapeDtypeStruct((key_heads * cols, span), bf16),
            jax.ShapeDtypeStruct(kv_all.shape, bf16),
        ],
        compiler_params=pltpu.CompilerParams(vmem_limit_bytes=40 * 2**20),
        cost_estimate=pl.CostEstimate(
            flops=40 * blocks * span * span * cols,
            bytes_accessed=4 * kv_all.size,
            transcendentals=0,
        ),
    )(meta, q_t, do_parts, o_t, lse, kv_all, starts, cosine, sine)


def experts_kernel(core_ref, *refs, experts):
    (
        heads_ref, x_ref, dy_ref, mix_ref, gain_ref, own_ref, other_ref, gate_ref, up_ref, down_ref
    ) = refs[:10]
    outs = refs[10:]
    row_count, part = heads_ref.shape[1], heads_ref.shape[3]
    out_ref, dh_ref, ggate_ref, gup_ref, send_out, keep_out, gain_grad_ref = outs[:7]
    d_heads_ref = outs[7]
    hid_s, hat_s, recip_s, norm_s, norm_t_s, acc_s, dn_s, w_out_s = outs[8:]
    expert = pl.program_id(0)
    width = x_ref.shape[1]

    @pl.when(expert == 0)
    def _():
        for device in range(own_ref.shape[0]):
            w_out_s[device, core_ref[0]] = own_ref[device]
            w_out_s[device, 1 - core_ref[0]] = other_ref[device]
        w_out = w_out_s[...].reshape(-1, width)
        for row in range(row_count):
            at = slice(part * row, part * (row + 1))
            branch = mm(heads_ref[:, row].reshape(-1, part).T, w_out)
            hidden = x_ref[at, :].astype(f32) + branch
            recip = lax.rsqrt(jnp.mean(hidden * hidden, axis=-1, keepdims=True) + epsilon)
            hat = hidden * recip
            hid_s[at, :] = hidden
            hat_s[at, :] = hat
            recip_s[at, :] = recip
            norm_s[at, :] = (hat * gain_ref[...]).astype(bf16)
        norm_t_s[...] = norm_s[...].T
        acc_s[...] = hid_s[...]
        dn_s[...] = jnp.zeros(dn_s.shape, f32)

    normed = norm_s[...]
    mix = mix_ref[0]
    gate_pre = mm(normed, gate_ref[0])
    up_pre = mm(normed, up_ref[0])
    gate_sig = 1.0 / (1.0 + jnp.exp(-gate_pre))
    gate_act = gate_pre * gate_sig
    hid = (gate_act * up_pre).astype(bf16)
    acc_s[...] += mix * mm(hid, down_ref[0])
    d_expert = (mix * dy_ref[...].astype(f32)).astype(bf16)
    d_hid = mm(d_expert, down_ref[0], NT)
    d_gate = (d_hid * up_pre * (gate_sig * (1.0 + gate_pre * (1.0 - gate_sig)))).astype(bf16)
    d_up = (d_hid * gate_act).astype(bf16)
    dn_s[...] += mm(d_gate, gate_ref[0], NT) + mm(d_up, up_ref[0], NT)
    grad_down = mm(hid.T, d_expert).astype(bf16)
    half = experts // 2

    @pl.when(expert < half)
    def _():
        send_out[expert] = grad_down

    @pl.when(expert >= half)
    def _():
        keep_out[expert - half] = grad_down

    ggate_ref[0] = mm(norm_t_s[...], d_gate).astype(bf16)
    gup_ref[0] = mm(norm_t_s[...], d_up).astype(bf16)

    @pl.when(expert == experts - 1)
    def _():
        out_ref[...] = acc_s[...].astype(bf16)
        hat = hat_s[...]
        d_norm = dn_s[...]
        w_out = w_out_s[...].reshape(-1, width)
        gain_grad_ref[...] = jnp.sum(d_norm * hat, axis=0, keepdims=True)
        d_hat = d_norm * gain_ref[...]
        mean = jnp.mean(d_hat * hat, axis=-1, keepdims=True)
        d_hidden = dy_ref[...].astype(f32) + recip_s[...] * (d_hat - hat * mean)
        dh_ref[...] = d_hidden
        d_branch = d_hidden.astype(bf16)
        grad_out = None
        for row in range(row_count):
            at = slice(part * row, part * (row + 1))
            piece = d_branch[at, :]
            d_heads_ref[:, row] = (
                mm(w_out, piece, NT).astype(bf16).reshape(d_heads_ref.shape[0], -1, part)
            )
            term = mm(heads_ref[:, row].reshape(-1, part), piece)
            grad_out = term if grad_out is None else grad_out + term
        grad_out = grad_out.astype(bf16)
        part_rows = grad_out.shape[0] // (2 * (send_out.shape[0] - half))

        @pl.when(core_ref[0] == 0)
        def _():
            for at in range(send_out.shape[0] - half):
                keep_out[half + at] = grad_out[part_rows * at : part_rows * (at + 1)]
                start = grad_out.shape[0] // 2 + part_rows * at
                send_out[half + at] = grad_out[start : start + part_rows]

        @pl.when(core_ref[0] != 0)
        def _():
            for at in range(send_out.shape[0] - half):
                send_out[half + at] = grad_out[part_rows * at : part_rows * (at + 1)]
                start = grad_out.shape[0] // 2 + part_rows * at
                keep_out[half + at] = grad_out[start : start + part_rows]


def run_experts(
    core, heads, x_rows, dy_rows, mix, gain, w_out_half, w_out_other, w_gate, w_up, w_down
):
    own, width = x_rows.shape
    experts, _, hidden = w_gate.shape
    kv_devices, row_count, _, part = heads.shape
    half_rows = w_out_half.shape[1]
    head_cols = 2 * kv_devices * half_rows

    def whole(shape):
        return pl.BlockSpec(shape, lambda e, m: (0,) * len(shape))

    half = experts // 2

    def which(e, m):
        return lax.rem(e + (1 - m[0]) * half, experts)

    gate_spec = pl.BlockSpec((1, width, hidden), lambda e, m: (which(e, m), 0, 0))
    down_spec = pl.BlockSpec((1, hidden, width), lambda e, m: (which(e, m), 0, 0))
    outer = (half + head_cols // (2 * hidden), hidden, width)
    return pl.pallas_call(
        functools.partial(experts_kernel, experts=experts),
        grid_spec=pltpu.PrefetchScalarGridSpec(
            num_scalar_prefetch=1,
            grid=(experts,),
            in_specs=[
                whole(heads.shape),
                whole((own, width)),
                whole((own, width)),
                pl.BlockSpec((1, own, 1), lambda e, m: (which(e, m), 0, 0)),
                whole((1, width)),
                whole(w_out_half.shape),
                whole(w_out_half.shape),
                gate_spec,
                gate_spec,
                down_spec,
            ],
            out_specs=[
                whole((own, width)),
                whole((own, width)),
                gate_spec,
                gate_spec,
                whole(outer),
                whole(outer),
                whole((1, width)),
                whole(heads.shape),
            ],
            scratch_shapes=[
                pltpu.VMEM((own, width), f32),
                pltpu.VMEM((own, width), f32),
                pltpu.VMEM((own, 1), f32),
                pltpu.VMEM((own, width), bf16),
                pltpu.VMEM((width, own), bf16),
                pltpu.VMEM((own, width), f32),
                pltpu.VMEM((own, width), f32),
                pltpu.VMEM((kv_devices, 2, half_rows, width), bf16),
            ],
        ),
        out_shape=[
            jax.ShapeDtypeStruct((own, width), bf16),
            jax.ShapeDtypeStruct((own, width), f32),
            jax.ShapeDtypeStruct(w_gate.shape, bf16),
            jax.ShapeDtypeStruct(w_up.shape, bf16),
            jax.ShapeDtypeStruct(outer, bf16),
            jax.ShapeDtypeStruct(outer, bf16),
            jax.ShapeDtypeStruct((1, width), f32),
            jax.ShapeDtypeStruct(heads.shape, bf16),
        ],
        compiler_params=pltpu.CompilerParams(vmem_limit_bytes=56 * 2**20),
        cost_estimate=pl.CostEstimate(
            flops=18 * own * width * hidden * experts,
            bytes_accessed=6 * w_gate.size * 2,
            transcendentals=0,
        ),
    )(
        core, heads, x_rows, dy_rows, mix, gain, w_out_half, w_out_other,
        w_gate, w_up, w_down,
    )


def inner_kernel(*refs, row_count, query_cols, key_heads):
    dq = refs[:row_count]
    dkv = refs[row_count : 2 * row_count]
    n_ref, cos_ref, sin_ref, parts_ref, grad_ref, inner_s = refs[2 * row_count :]
    kv_devices = parts_ref.shape[0]
    part = parts_ref.shape[2] // row_count
    grad = None
    for row in range(row_count):
        cosine = cos_ref[row]
        sine = sin_ref[row]
        inner_s[0:query_cols, :] = dq[row][...]
        for head in range(key_heads):
            at = 2 * DH * head
            low = dkv[row][at : at + HALF, :].astype(f32)
            high = dkv[row][at + HALF : at + DH, :].astype(f32)
            to = query_cols + DH * head
            inner_s[to : to + HALF, :] = (low * cosine + high * sine).astype(bf16)
            inner_s[to + HALF : to + DH, :] = (high * cosine - low * sine).astype(bf16)
            to = query_cols + DH * (key_heads + head)
            inner_s[to : to + DH, :] = dkv[row][at + DH : at + 2 * DH, :]
        for device in range(kv_devices):
            parts_ref[device, :, part * row : part * (row + 1)] = inner_s[
                :, part * device : part * (device + 1)
            ]
        term = mm(inner_s[...], n_ref[row])
        grad = term if grad is None else grad + term
    grad_ref[...] = grad.astype(bf16)


def inner_grads(dq, dkv, gathered, cosine, sine, kv_devices, key_heads):
    row_count = len(dq)
    query_cols, span = dq[0].shape
    cols, width = query_cols + dkv[0].shape[0], gathered.shape[2]
    own = row_count * span // kv_devices
    return pl.pallas_call(
        functools.partial(
            inner_kernel, row_count=row_count, query_cols=query_cols, key_heads=key_heads
        ),
        out_shape=[
            jax.ShapeDtypeStruct((kv_devices, cols, own), bf16),
            jax.ShapeDtypeStruct((cols, width), bf16),
        ],
        scratch_shapes=[pltpu.VMEM((cols, span), bf16)],
        compiler_params=pltpu.CompilerParams(vmem_limit_bytes=40 * 2**20),
        cost_estimate=pl.CostEstimate(
            flops=2 * row_count * span * cols * width,
            bytes_accessed=4 * gathered.size,
            transcendentals=0,
        ),
    )(*dq, *dkv, gathered, cosine, sine)


def tokens_kernel(place_ref, *refs):
    own_ref, other_ref, x_ref, dh_ref, gain_ref, out_ref = refs[-6:]
    x_float = x_ref[...].astype(f32)
    recip = lax.rsqrt(jnp.mean(x_float * x_float, axis=-1, keepdims=True) + epsilon)
    x_hat = x_float * recip
    core = place_ref[0]
    d_normed = None
    for mask, piece in enumerate(refs[:-6]):
        device = place_ref[1] ^ mask
        term = mm(piece[core].T, own_ref[device])
        term += mm(piece[1 - core].T, other_ref[device])
        d_normed = term if d_normed is None else d_normed + term
    d_hat = d_normed * gain_ref[...]
    mean = jnp.mean(d_hat * x_hat, axis=-1, keepdims=True)
    out_ref[...] = (dh_ref[...] + recip * (d_hat - x_hat * mean)).astype(bf16)


def token_grads(place, d_inner, w_half, w_other, x_rows, d_hidden, gain):
    own, width = x_rows.shape
    return pl.pallas_call(
        tokens_kernel,
        in_specs=[pl.BlockSpec(memory_space=pltpu.SMEM)]
        + [pl.BlockSpec(memory_space=pltpu.VMEM)] * (5 + len(d_inner)),
        out_shape=jax.ShapeDtypeStruct((own, width), bf16),
        compiler_params=pltpu.CompilerParams(vmem_limit_bytes=40 * 2**20),
        cost_estimate=pl.CostEstimate(
            flops=4 * w_half.size * own, bytes_accessed=4 * w_half.size, transcendentals=0
        ),
    )(place, *d_inner, w_half, w_other, x_rows, d_hidden, gain)


def widen_whole_kernel(gate_ref, up_ref, ggate_ref, gup_ref):
    ggate_ref[...] = gate_ref[...].astype(f32)
    gup_ref[...] = up_ref[...].astype(f32)


def widen_whole(grad_gate, grad_up):
    experts, width, hidden = grad_gate.shape
    spec = pl.BlockSpec((1, width, hidden), lambda e: (e, 0, 0))
    return pl.pallas_call(
        widen_whole_kernel,
        grid=(experts,),
        in_specs=[spec, spec],
        out_specs=[spec, spec],
        out_shape=[jax.ShapeDtypeStruct(grad_gate.shape, f32)] * 2,
        compiler_params=pltpu.CompilerParams(vmem_limit_bytes=60 * 2**20),
        cost_estimate=pl.CostEstimate(
            flops=0, bytes_accessed=12 * grad_gate.size, transcendentals=0
        ),
    )(grad_gate, grad_up)


def widen_halves_kernel(core_ref, own_ref, other_ref, gdown_ref, *, half):
    @pl.when(pl.program_id(0) < half)
    def _():
        gdown_ref[0] = own_ref[...].astype(f32)

    @pl.when(pl.program_id(0) >= half)
    def _():
        gdown_ref[0] = other_ref[...].astype(f32)


def widen_halves(core, own_rows, other_rows, experts, hidden):
    width = own_rows.shape[1]
    half = experts // 2
    return pl.pallas_call(
        functools.partial(widen_halves_kernel, half=half),
        grid_spec=pltpu.PrefetchScalarGridSpec(
            num_scalar_prefetch=1,
            grid=(experts,),
            in_specs=[
                pl.BlockSpec((hidden, width), lambda e, m: (jnp.minimum(e, half - 1), 0)),
                pl.BlockSpec((hidden, width), lambda e, m: (jnp.maximum(e - half, 0), 0)),
            ],
            out_specs=pl.BlockSpec(
                (1, hidden, width), lambda e, m: (lax.rem(e + m[0] * half, experts), 0, 0)
            ),
        ),
        out_shape=jax.ShapeDtypeStruct((experts, hidden, width), f32),
        compiler_params=pltpu.CompilerParams(vmem_limit_bytes=60 * 2**20),
        cost_estimate=pl.CostEstimate(
            flops=0, bytes_accessed=6 * experts * hidden * width, transcendentals=0
        ),
    )(core, own_rows, other_rows)


def per_device(
    tokens,
    cotangent,
    norm_first,
    w_query,
    w_key,
    w_value,
    w_out,
    norm_second,
    w_gate,
    w_up,
    w_down,
    routes,
    gate_weights,
    segment_ids,
    positions,
):
    row_count, block_len, width = tokens.shape
    kv_devices = lax.axis_size("kv")
    seq_devices = lax.axis_size("seq")
    seq_len = block_len * kv_devices
    seq_index = lax.axis_index("seq")
    query_cols = w_query.shape[1]
    key_cols = w_key.shape[1]
    query_heads = query_cols // DH
    key_heads = key_cols // DH
    group = query_heads // key_heads
    expert_count = w_gate.shape[0]
    own = row_count * block_len
    rows = range(row_count)
    orders = [seq_order(row, seq_devices) for row in rows]

    place = seq_index * seq_len + jnp.arange(seq_len, dtype=jnp.int32)
    starts = place[None, :] - positions
    first_block = starts[:, 0] // seq_len
    middle_block = jnp.clip((starts[:, -1] + seq_len - 1) // seq_len, first_block, seq_index)
    bounds = jnp.stack([first_block, middle_block], axis=1).reshape(-1)
    meta = jnp.concatenate([seq_index[None], bounds]).astype(jnp.int32)
    starts3 = starts.reshape(row_count, 1, seq_len)
    freqs = theta_base ** (-(jnp.arange(HALF, dtype=f32) * 2.0) / DH)
    angles = freqs[None, :, None] * positions.astype(f32)[:, None, :]
    cosine = jnp.cos(angles)
    sine = jnp.sin(angles)

    x_float = tokens.astype(f32)
    recip_first = lax.rsqrt(jnp.mean(x_float * x_float, axis=-1, keepdims=True) + epsilon)
    normed = (x_float * recip_first * norm_first).astype(bf16)
    gathered = lax.all_gather(normed, "kv", axis=1, tiled=True)

    w_t = jnp.concatenate([w_query.T, w_key.T, w_value.T], axis=0)
    inner_cols = w_t.shape[0]
    expert_ids = jnp.arange(expert_count, dtype=jnp.int32)
    picks = routes[..., None] == expert_ids
    local_load = jnp.sum(picks.astype(f32), axis=(0, 1, 2))
    core_index = seq_index % 2
    half_rows = query_cols // 2
    w_out_half = lax.all_gather(cut(w_out, core_index, half_rows), "kv")
    w_out_other = swap(w_out_half, "seq", 1)
    w_inner_half = lax.all_gather(cut(w_t, core_index, inner_cols // 2), "kv")
    w_inner_other = swap(w_inner_half, "seq", 1)

    def exchange(value):
        return lax.all_to_all(value, "kv", 0, 0)

    q_t, kv_all, o_t, lse, heads = [], [], [], [], []
    kv_t = []
    for row in rows:
        q_row, kv_row = project(row, w_t, gathered, cosine, sine, query_heads, key_heads)
        q_t.append(q_row)
        kv_t.append(kv_row)
    kv_t = lax.optimization_barrier(kv_t)
    kv_all = [spread_seq(kv_t[row], orders[row], None) for row in rows]
    kv_all = lax.optimization_barrier(kv_all)
    for row in rows:
        o_row, low_row, lse_row = attend(
            row, meta, q_t[row], kv_all[row], starts3, group, orders[row]
        )
        o_t.append(o_row)
        lse.append(lse_row)
        heads.append(low_row.reshape(query_cols, kv_devices, block_len).transpose(1, 0, 2))
    heads = exchange(jnp.stack(heads, axis=1))

    mix = jnp.sum(picks.astype(f32) * gate_weights[..., None], axis=2)
    mix = mix.reshape(own, expert_count).T[:, :, None]
    x_rows = tokens.reshape(own, width)
    core = core_index.astype(jnp.int32)[None]
    outs = run_experts(
        core,
        heads,
        x_rows,
        cotangent.reshape(own, width),
        mix,
        norm_second.reshape(1, width),
        w_out_half,
        w_out_other,
        w_gate,
        w_up,
        w_down,
    )
    block_out, d_hidden, grad_gate, grad_up, send_out, keep_out, second_part = outs[:7]
    d_heads = outs[7]
    grad_gate, grad_up = lax.psum((grad_gate, grad_up), ("seq", "kv"))

    chips = seq_devices // 2
    groups = [[2 * chip + one for chip in range(chips)] for one in range(2)]

    def over_chips(value):
        return lax.all_to_all(value, "seq", 0, 0, axis_index_groups=groups)

    def total(value):
        return jnp.sum(value.astype(f32), axis=0).astype(bf16)

    def copies(value, number):
        return jnp.broadcast_to(value[None], (number,) + value.shape)

    def rest(d_heads, d_hidden, send_out, keep_out, second_part):
        do_parts = exchange(d_heads)
        outer = added(keep_out, swap(send_out, "seq", 1)).reshape(chips, -1, width)
        sums = jnp.concatenate([second_part[0], local_load])
        for axis in ("seq", "kv"):
            sums = sum_over(sums, axis)
        do_parts = behind(do_parts, (outer, sums))
        outer = over_chips(outer)
        dq, dkv = [], []
        for row in rows:
            dq_row, dkv_row = attend_back(
                row, meta, q_t[row], do_parts, o_t[row], lse[row], kv_all[row], starts3,
                cosine, sine, group, orders[row],
            )
            dq.append(dq_row)
            dkv.append(collect_seq(dkv_row, orders[row]))
        outer = total(behind(outer, dq[-1]))
        rows_left = outer.shape[0]
        outer = exchange(outer.reshape(kv_devices, rows_left // kv_devices, width))
        outer = total(behind(outer, dkv[-1]))
        dkv[-1] = behind(dkv[-1], outer)
        outer = exchange(copies(outer, kv_devices)).reshape(rows_left, width)
        d_parts, grad_inner_part = inner_grads(
            dq, dkv, gathered, cosine, sine, kv_devices, key_heads
        )
        half = inner_cols // 2
        paths = [seq_order(at, seq_devices) for at in range(2)]
        shares = [halve_seq(grad_inner_part[half * at :][:half], paths[at]) for at in range(2)]
        outer = copies(behind(outer, shares), chips)
        d_parts = behind(d_parts, outer).reshape(kv_devices, 2, inner_cols // 2, own)
        outer = over_chips(outer).reshape(-1, width)
        kv_index = lax.axis_index("kv")
        d_inner = [
            swap(lax.dynamic_index_in_dim(d_parts, kv_index ^ mask, 0, keepdims=False), "kv", mask)
            for mask in range(kv_devices)
        ]
        place = jnp.stack([core_index, kv_index]).astype(jnp.int32)
        d_tokens = token_grads(
            place, d_inner, w_inner_half, w_inner_other, x_rows, d_hidden, norm_first.reshape(1, width)
        )
        outer = behind(outer, d_tokens)
        return d_tokens, outer, behind(shares, outer), sums

    operands = (d_heads, d_hidden, send_out, keep_out, second_part)
    shapes = jax.eval_shape(rest, *operands)
    d_tokens, outer, shares, sums = lax.cond(
        positions[0, 0] >= 0,
        rest,
        lambda *ignored: jax.tree.map(lambda leaf: jnp.zeros(leaf.shape, leaf.dtype), shapes),
        *operands,
    )
    kv_index = lax.axis_index("kv")
    paths = [seq_order(at, seq_devices) for at in range(2)]
    other_outer = swap(outer, "seq", 1)
    grad_inner = jnp.concatenate(
        [double_seq(shares[at], paths[at]) for at in range(2)], axis=0
    ).astype(f32)
    grad_gate, grad_up = widen_whole(grad_gate, grad_up)
    first_part = jnp.sum(w_t.astype(f32) * behind(grad_inner, grad_gate), axis=0)
    first_sum = sum_over(first_part, "kv") / norm_first
    half_devices = kv_devices // 2
    start = (expert_count // 2) * w_down.shape[1] + lax.rem(kv_index, half_devices) * query_cols
    pieces = [
        lax.dynamic_slice_in_dim(pair, start, query_cols, 0) for pair in (outer, other_outer)
    ]
    own_out = jnp.where(kv_index // half_devices == core_index, *pieces).astype(f32)
    grad_down = widen_halves(core, outer, other_outer, expert_count, w_down.shape[1])
    return (
        block_out.reshape(tokens.shape),
        d_tokens.reshape(tokens.shape),
        first_sum,
        grad_inner[:query_cols].T,
        grad_inner[query_cols : query_cols + key_cols].T,
        grad_inner[query_cols + key_cols :].T,
        own_out,
        sums[:width],
        grad_gate,
        grad_up,
        grad_down,
        sums[width:].astype(jnp.int32),
    )


def solution(mesh):
    in_specs = (
        P(None, ("seq", "kv"), None),
        P(None, ("seq", "kv"), None),
        P(),
        P(None, "kv"),
        P(None, "kv"),
        P(None, "kv"),
        P("kv", None),
        P(),
        P(),
        P(),
        P(),
        P(None, ("seq", "kv"), None),
        P(None, ("seq", "kv"), None),
        P(),
        P(None, "seq"),
    )
    out_specs = (
        P(None, ("seq", "kv"), None),
        P(None, ("seq", "kv"), None),
        P(),
        P(None, "kv"),
        P(None, "kv"),
        P(None, "kv"),
        P("kv", None),
        P(),
        P(),
        P(),
        P(),
        P(),
    )
    return jax.shard_map(
        per_device, mesh=mesh, in_specs=in_specs, out_specs=out_specs, check_vma=False
    )
```
